32 devices in a mesh: samp: 16 (over z, y, core), blk: 2 (over x).
Axes of the slice: x: 2, y: 2, z: 4, core: 2. Of those that a mesh axis runs over, the one named last changes fastest.
Arguments:
- activations: bfloat16 [16, 1024, 768], P('samp', 'blk'), may hold values from -6 to 6
- single_cond: bfloat16 [2, 1024, 384], P(None, 'blk'), may hold values from -6 to 6
- pair_repr: bfloat16 [2, 1024, 1024, 128], P(None, 'blk', 'samp'), may hold values from -6 to 6
- struct_id: int32 [16], P('samp'), may hold values from 0 to 1, as said below
- seq_lengths: int32 [2], replicated, may hold values from 513 to 1024, as said below
- qkvg_weight: bfloat16 [768, 3072], replicated, may hold values from -0.21875 to 0.21875
- query_bias: float32 [768], replicated, may hold values from -4 to 4
- out_weight: bfloat16 [768, 768], replicated, may hold values from -3.5 to 3.5
- in_weight: bfloat16 [768, 3072], replicated, may hold values from -0.21875 to 0.21875
- down_weight: bfloat16 [1536, 768], replicated, may hold values from -0.3125 to 0.3125
- cond_weight: bfloat16 [2, 384, 2304], replicated, may hold values from -0.3125 to 0.3125
- cond_bias: float32 [2, 1536], replicated, may hold values from -4 to 4
- single_gain: float32 [2, 384], replicated, may hold values from 0.1 to 1.9
- pair_gain: float32 [128], replicated, may hold values from 0.1 to 1.9
- pair_weight: bfloat16 [128, 16], replicated, may hold values from -0.5 to 0.5
- cotangent: bfloat16 [16, 1024, 768], P('samp', 'blk'), may hold values from -6 to 6
Outputs:
- block_out: bfloat16 [16, 1024, 768], P('samp', 'blk')
- act_grad: float32 [16, 1024, 768], P('samp', 'blk')
- single_grad: float32 [2, 1024, 384], P(None, 'blk')
- pair_grad: float32 [2, 1024, 1024, 128], P(None, 'blk', 'samp')
- qkvg_grad: float32 [768, 3072], P('samp', 'blk')
- query_bias_grad: float32 [768], replicated
- out_grad: float32 [768, 768], P('samp', 'blk')
- in_grad: float32 [768, 3072], P('samp', 'blk')
- down_grad: float32 [1536, 768], P('samp', 'blk')
- cond_grad: float32 [2, 384, 2304], P(None, 'samp', 'blk')
- cond_bias_grad: float32 [2, 1536], replicated
- single_gain_grad: float32 [2, 384], replicated
- pair_gain_grad: float32 [128], replicated
- pair_weight_grad: float32 [128, 16], replicated
The draws below stay inside these ranges and needn't reach their ends.
Inputs may be any that keep to these rules, and one draw needn't show every extreme that they name: `struct_id`: exactly 8 samples belong to each of the two structures. `seq_lengths`: one structure, drawn from the seed, has all 1024 tokens.
All inputs are finite; a program needn't handle non-finite values.
Results may differ from the reference program's by a relative error of at most 0.023.
Values may be sent and summed in bfloat16 or wider, within the bound.
No kernel may reach another device: no remote copies, remote signals or barrier semaphores. Data moves between devices by JAX's collectives and lax.ppermute only.
A program may use at most 384 MiB of HBM per device.

```python
import math
import jax
import jax.numpy as jnp
from jax import lax

D = 768
H = 16
CZ = 128
CS = 384
FF = 1536
STRUCTS = 2
SEQ = 1024
SAMPLES = 16


def draw_struct_id(key, part):
    key = jax.random.fold_in(key, 11)
    order = jax.random.permutation(key, SAMPLES)
    return (order >= SAMPLES // 2).astype(jnp.int32)


def draw_seq_lengths(key, part):
    key = jax.random.fold_in(key, 23)
    first_key, second_key = jax.random.split(key)
    full_one = jax.random.randint(first_key, (), 0, STRUCTS)
    others = jax.random.randint(second_key, (STRUCTS,), SEQ // 2 + 1, SEQ + 1)
    return jnp.where(jnp.arange(STRUCTS) == full_one, SEQ, others).astype(jnp.int32)


def block_levels(stream_key, dims, cuts, low, largest):
    def one(axis_at, blocks):
        steps = jax.random.uniform(jax.random.fold_in(jax.random.fold_in(stream_key, 6), axis_at), (blocks,), jnp.float32, low / len(cuts), largest / len(cuts))
        return jnp.repeat(jnp.exp(steps), dims[axis_at] // blocks).reshape((-1,) + (1,) * (len(dims) - axis_at - 1))

    factor_of = one(*cuts[0])
    for cut in cuts[1:]:
        factor_of = factor_of * one(*cut)
    return factor_of


def normal_values(key, dims, deviation, reach, cuts=(), held_as=jnp.bfloat16):
    values = deviation * jax.random.normal(key, dims, jnp.float32)
    if cuts:
        values = values * block_levels(key, dims, cuts, -0.22, 0.18)
    return jnp.clip(values, -reach, reach).astype(held_as)


def setup_inputs(seed: int = 0) -> dict:
    key_of = jax.random.split(jax.random.key(seed), 17)
    return {
        "activations": normal_values(key_of[0], (SAMPLES, SEQ, D), 1.0, 6.0, ((0, 16), (1, 2))),
        "single_cond": normal_values(key_of[1], (STRUCTS, SEQ, CS), 1.0, 6.0, ((1, 2),)),
        "pair_repr": normal_values(key_of[2], (STRUCTS, SEQ, SEQ, CZ), 1.0, 6.0, ((1, 2), (2, 16))),
        "struct_id": draw_struct_id(jax.random.fold_in(key_of[16], 71), 0),
        "seq_lengths": draw_seq_lengths(jax.random.fold_in(key_of[16], 71), 0),
        "qkvg_weight": normal_values(key_of[5], (D, 4 * D), D ** -0.5, 0.21875),
        "query_bias": normal_values(key_of[6], (D,), 1.0, 4.0, (), jnp.float32),
        "out_weight": normal_values(key_of[7], (D, D), (max(2, D // 256)) ** -0.5, 3.5),
        "in_weight": normal_values(key_of[8], (D, 2 * FF), D ** -0.5, 0.21875),
        "down_weight": normal_values(key_of[9], (FF, D), (FF // 4) ** -0.5, 0.3125),
        "cond_weight": normal_values(key_of[10], (2, CS, 3 * D), CS ** -0.5, 0.3125),
        "cond_bias": normal_values(key_of[11], (2, 2 * D), 1.0, 4.0, (), jnp.float32),
        "single_gain": jnp.clip(1.0 + 0.18 * jax.random.normal(key_of[12], (2, CS), jnp.float32), 0.1, 1.9),
        "pair_gain": jnp.clip(1.0 + 0.18 * jax.random.normal(key_of[13], (CZ,), jnp.float32), 0.1, 1.9),
        "pair_weight": normal_values(key_of[14], (CZ, H), CZ ** -0.5, 0.5),
        "cotangent": normal_values(key_of[15], (SAMPLES, SEQ, D), 1.0, 6.0, ((0, 16), (1, 2))),
    }


@jax.custom_vjp
def low(v):
    return lax.optimization_barrier(v.astype(jnp.bfloat16)).astype(jnp.float32)

@jax.custom_vjp
def low_back(v):
    return v

def low_keep(v):
    return (low(v), None)

def low_pass(kept, grad):
    return (grad,)

def back_keep(v):
    return (v, None)

def back_low(kept, grad):
    return (low(grad),)
low.defvjp(low_keep, low_pass)
low_back.defvjp(back_keep, back_low)
EPS = 1e-05
MASKED = -1000000000.0
HIGH = lax.Precision.HIGHEST

def norm_rows(value):
    center = value - lax.optimization_barrier(jnp.mean(value, axis=-1, keepdims=True))
    return center * lax.rsqrt(lax.optimization_barrier(jnp.mean(center * center, axis=-1, keepdims=True)) + EPS)

def pair_block(rows, pair_gain, pair_weight):
    normed = low(norm_rows(rows) * pair_gain)
    return low_back(low(jnp.einsum('rkz,zh->rhk', normed, pair_weight, precision=HIGH)))

def sample_block(act_row, cond_attn, cond_trans, bias_rows, limit, qkvg_weight, query_bias, out_weight, in_weight, down_weight):
    tokens, width = act_row.shape
    heads = bias_rows.shape[1]
    head_dim = width // heads
    hidden_units = down_weight.shape[0]
    scale_attn = jax.nn.sigmoid(cond_attn[:, :width])
    x_attn = low(scale_attn * norm_rows(act_row) + cond_attn[:, width:2 * width])
    proj_bias = jnp.concatenate([query_bias, jnp.zeros((3 * width,), jnp.float32)])
    projected = low_back(jnp.dot(x_attn, qkvg_weight, precision=HIGH) + proj_bias)
    query = low(projected[:, :width]).reshape(tokens, heads, head_dim)
    keys = low(projected[:, width:2 * width]).reshape(tokens, heads, head_dim)
    values = low(projected[:, 2 * width:3 * width]).reshape(tokens, heads, head_dim)
    gate_pre = projected[:, 3 * width:]
    scores = jnp.einsum('qhd,khd->qhk', query, keys, precision=HIGH) * (1.0 / math.sqrt(head_dim)) + bias_rows
    valid = jnp.arange(tokens) < limit
    scores = low_back(jnp.where(valid[None, None, :], scores, MASKED))
    probs = jax.nn.softmax(scores, axis=-1)
    attn = low_back(jnp.einsum('qhk,khd->qhd', low(probs), values, precision=HIGH)).reshape(tokens, width)
    mixed = low(jax.nn.sigmoid(gate_pre) * attn)
    att_out = low_back(jnp.dot(mixed, out_weight, precision=HIGH))
    hidden_state = act_row + jax.nn.sigmoid(cond_attn[:, 2 * width:]) * att_out
    x_trans = low(jax.nn.sigmoid(cond_trans[:, :width]) * norm_rows(hidden_state) + cond_trans[:, width:2 * width])
    up_proj = low_back(jnp.dot(x_trans, in_weight, precision=HIGH))
    hidden_act = low(jax.nn.silu(up_proj[:, :hidden_units]) * up_proj[:, hidden_units:])
    trans = low_back(jnp.dot(hidden_act, down_weight, precision=HIGH))
    return hidden_state + jax.nn.sigmoid(cond_trans[:, 2 * width:]) * trans

def forward(activations, single_cond, pair_repr, qkvg_weight, query_bias, out_weight, in_weight, down_weight, cond_weight, cond_bias, single_gain, pair_gain, pair_weight, struct_id, seq_lengths):
    structs, seq_len, pair_dim = (pair_repr.shape[0], pair_repr.shape[1], pair_repr.shape[3])
    heads = pair_weight.shape[1]
    width = activations.shape[-1]
    single_hat = norm_rows(single_cond)
    conds = []
    for sublayer in range(2):
        cond_in = low(single_hat * single_gain[sublayer])
        bias_row = jnp.concatenate([cond_bias[sublayer, :width], jnp.zeros((width,), jnp.float32), cond_bias[sublayer, width:]])
        conds.append(low_back(jnp.einsum('cti,ij->ctj', cond_in, cond_weight[sublayer], precision=HIGH) + bias_row))
    row_block = min(128, seq_len)
    blocks = pair_repr.reshape(structs * seq_len // row_block, row_block, seq_len, pair_dim)
    pair_fn = jax.checkpoint(pair_block)
    bias_blocks = lax.map(lambda rows: pair_fn(rows, pair_gain, pair_weight), blocks)
    pair_bias = bias_blocks.reshape(structs, seq_len, heads, seq_len)
    sample_fn = jax.checkpoint(sample_block)

    def sample_step(scan_state, inputs):
        act_row, member = inputs
        result = sample_fn(act_row, conds[0][member], conds[1][member], pair_bias[member], seq_lengths[member], qkvg_weight, query_bias, out_weight, in_weight, down_weight)
        return (scan_state, result)
    ignored, outputs = lax.scan(sample_step, jnp.zeros((), jnp.float32), (activations, struct_id))
    return outputs

def reference(activations, single_cond, pair_repr, struct_id, seq_lengths, qkvg_weight, query_bias, out_weight, in_weight, down_weight, cond_weight, cond_bias, single_gain, pair_gain, pair_weight, cotangent):
    floats = [x.astype(jnp.float32) for x in (activations, single_cond, pair_repr, qkvg_weight, query_bias, out_weight, in_weight, down_weight, cond_weight, cond_bias, single_gain, pair_gain, pair_weight)]

    def forward_fn(*float_args):
        return forward(*float_args, struct_id, seq_lengths)
    block_out, backward = jax.vjp(forward_fn, *floats)
    grads = backward(cotangent.astype(jnp.float32))
    return (block_out.astype(jnp.bfloat16), grads[0], grads[1], grads[2], grads[3], grads[4], grads[5], grads[6], grads[7], grads[8], grads[9], grads[10], grads[11], grads[12])
```

```python
import functools
import math

import jax
import jax.numpy as jnp
from jax import lax
from jax.experimental import pallas as pl
from jax.experimental.pallas import tpu as pltpu
from jax.sharding import PartitionSpec as P

EPS = 1e-05
MASKED = -1000000000.0
LOG2E = 1.4426950408889634
LN2 = 0.6931471805599453
VMEM_BYTES = 56 * 1024 * 1024
TILE_COLS = 384


def norm_rows(value):
    center = value - jnp.mean(value, axis=-1, keepdims=True)
    return center * lax.rsqrt(jnp.mean(center * center, axis=-1, keepdims=True) + EPS)


def pick_struct(table, ids):
    expand = (ids.shape[0],) + (1,) * (table.ndim - 1)
    chosen = jnp.broadcast_to(table[0][None], (ids.shape[0],) + table.shape[1:])
    chosen = jnp.where(ids.reshape(expand) == 1, table[1][None], chosen)
    return chosen


def struct_sum(values, ids, structs):
    expand = (ids.shape[0],) + (1,) * (values.ndim - 1)
    return jnp.stack(
        [
            jnp.sum(jnp.where(ids.reshape(expand) == member, values, 0.0), axis=0)
            for member in range(structs)
        ]
    )


def block_length(piece_len):
    return math.gcd(piece_len, 512)


def local(
    activations,
    single_cond,
    pair_repr,
    struct_id,
    seq_lengths,
    qkvg_weight,
    query_bias,
    out_weight,
    in_weight,
    down_weight,
    cond_weight,
    cond_bias,
    single_gain,
    pair_gain,
    pair_weight,
    cotangent,
):
    samples_dev, tok_rows, width = activations.shape
    heads = pair_weight.shape[1]
    head_dim = width // heads
    hidden_units = down_weight.shape[0]
    structs = single_cond.shape[0]
    seq_total = tok_rows * lax.axis_size("blk")
    score_scale = 1.0 / math.sqrt(head_dim)
    zero_index = jnp.zeros((), jnp.int32)
    key_limit = pick_struct(seq_lengths, struct_id)
    single_hat = norm_rows(single_cond.astype(jnp.float32))
    cond_inputs = []
    cond_rows = []
    for sublayer in range(2):
        cond_in = (single_hat * single_gain[sublayer]).astype(jnp.bfloat16)
        bias_row = jnp.concatenate(
            [
                cond_bias[sublayer, :width],
                jnp.zeros((width,), jnp.float32),
                cond_bias[sublayer, width:],
            ]
        )
        cond_pre = (
            jnp.einsum(
                "cti,ij->ctj", cond_in, cond_weight[sublayer], preferred_element_type=jnp.float32
            )
            + bias_row
        )
        cond_inputs.append(cond_in)
        cond_rows.append(pick_struct(cond_pre, struct_id))
    pair_hat, pair_norm_back = jax.vjp(norm_rows, pair_repr.astype(jnp.float32))
    pair_in = (pair_hat * pair_gain).astype(jnp.bfloat16)
    bias_local = jnp.einsum(
        "crkz,zh->crhk", pair_in, pair_weight, preferred_element_type=jnp.float32
    ).astype(jnp.bfloat16)
    bias_all = lax.all_gather(bias_local, "samp", axis=3, tiled=True)
    act_float = activations.astype(jnp.float32)
    act_hat, act_norm_back = jax.vjp(norm_rows, act_float)
    cond_attn = cond_rows[0]
    scale_attn = jax.nn.sigmoid(cond_attn[..., :width])
    gate_attn = jax.nn.sigmoid(cond_attn[..., 2 * width :])
    x_attn = (scale_attn * act_hat + cond_attn[..., width : 2 * width]).astype(jnp.bfloat16)
    proj_bias = jnp.concatenate([query_bias, jnp.zeros((3 * width,), jnp.float32)])
    projected = (
        jnp.einsum("sti,ij->stj", x_attn, qkvg_weight, preferred_element_type=jnp.float32)
        + proj_bias
    )
    query = (
        projected[..., :width].astype(jnp.bfloat16).reshape(samples_dev, tok_rows, heads, head_dim)
    )
    keys_values = projected[..., width : 3 * width].astype(jnp.bfloat16)
    gate_pre = projected[..., 3 * width :]

    def block_scores(sub_kv, offset):
        block_len = sub_kv.shape[1]
        keys_block = sub_kv[..., :width].reshape(samples_dev, block_len, heads, head_dim)
        scores = (
            jnp.einsum("sqhd,skhd->sqhk", query, keys_block, preferred_element_type=jnp.float32)
            * score_scale
        )
        bias_block = lax.dynamic_slice_in_dim(bias_all, offset, block_len, 3)
        scores = scores + pick_struct(bias_block, struct_id).astype(jnp.float32)
        positions = offset + jnp.arange(block_len, dtype=jnp.int32)
        valid = positions[None, :] < key_limit[:, None]
        return jnp.where(valid[:, None, None, :], scores, MASKED)

    def forward_fold(state, block_kv):
        block_len = block_length(block_kv.shape[1])
        count = block_kv.shape[1] // block_len

        def forward_step(carry, index):
            row_peak, row_total, row_acc = carry
            sub_offset = index * block_len
            sub_kv = lax.dynamic_slice_in_dim(block_kv, index * block_len, block_len, 1)
            scores = block_scores(sub_kv, sub_offset)
            values_block = sub_kv[..., width:].reshape(samples_dev, block_len, heads, head_dim)
            new_peak = jnp.maximum(row_peak, jnp.max(scores, axis=-1))
            rescale = jnp.exp(row_peak - new_peak)
            weights = jnp.exp(scores - new_peak[..., None])
            row_total = row_total * rescale + jnp.sum(weights, axis=-1)
            row_acc = row_acc * rescale[..., None] + jnp.einsum(
                "sqhk,skhd->sqhd",
                weights.astype(jnp.bfloat16),
                values_block,
                preferred_element_type=jnp.float32,
            )
            return ((new_peak, row_total, row_acc), None)

        result, ignored = lax.scan(
            jax.checkpoint(forward_step), state, jnp.arange(count, dtype=jnp.int32)
        )
        return result

    stats_shape = (samples_dev, tok_rows, heads)
    forward_init = (
        jnp.full(stats_shape, -1e30, jnp.float32),
        jnp.zeros(stats_shape, jnp.float32),
        jnp.zeros((samples_dev, tok_rows, heads, head_dim), jnp.float32),
    )
    row_peak, row_total, row_acc = forward_fold(
        forward_init, lax.all_gather(keys_values, "blk", axis=1, tiled=True)
    )
    attn4 = row_acc / row_total[..., None]
    log_sum = row_peak + jnp.log(row_total)
    attn = attn4.reshape(samples_dev, tok_rows, width)
    gate_val = jax.nn.sigmoid(gate_pre)
    mixed = (gate_val * attn).astype(jnp.bfloat16)
    att_out = jnp.einsum("sti,ij->stj", mixed, out_weight, preferred_element_type=jnp.float32)
    hidden_state = act_float + gate_attn * att_out
    cond_trans = cond_rows[1]
    scale_trans = jax.nn.sigmoid(cond_trans[..., :width])
    gate_trans = jax.nn.sigmoid(cond_trans[..., 2 * width :])
    hidden_hat, hidden_norm_back = jax.vjp(norm_rows, hidden_state)
    x_trans = (scale_trans * hidden_hat + cond_trans[..., width : 2 * width]).astype(jnp.bfloat16)
    up_proj = jnp.einsum("sti,ij->stj", x_trans, in_weight, preferred_element_type=jnp.float32)
    up_gate = up_proj[..., :hidden_units]
    up_lin = up_proj[..., hidden_units:]
    sig_gate = jax.nn.sigmoid(up_gate)
    silu_gate = up_gate * sig_gate
    hidden_act = (silu_gate * up_lin).astype(jnp.bfloat16)
    trans = jnp.einsum("stf,fd->std", hidden_act, down_weight, preferred_element_type=jnp.float32)
    block_out = (hidden_state + gate_trans * trans).astype(jnp.bfloat16)
    d_out = cotangent.astype(jnp.float32)
    d_trans = (gate_trans * d_out).astype(jnp.bfloat16)
    grad_down = jnp.einsum("stf,std->fd", hidden_act, d_trans, preferred_element_type=jnp.float32)
    d_hid = jnp.einsum("std,fd->stf", d_trans, down_weight, preferred_element_type=jnp.float32)
    silu_slope = sig_gate * (1.0 + up_gate * (1.0 - sig_gate))
    d_up = jnp.concatenate([d_hid * up_lin * silu_slope, d_hid * silu_gate], axis=-1).astype(
        jnp.bfloat16
    )
    grad_in = jnp.einsum("sti,stj->ij", x_trans, d_up, preferred_element_type=jnp.float32)
    d_xt = jnp.einsum("stj,ij->sti", d_up, in_weight, preferred_element_type=jnp.float32)
    d_hidden = d_out + hidden_norm_back(d_xt * scale_trans)[0]
    d_cond_trans = jnp.concatenate(
        [
            d_xt * hidden_hat * scale_trans * (1.0 - scale_trans),
            d_xt,
            d_out * trans * gate_trans * (1.0 - gate_trans),
        ],
        axis=-1,
    )
    d_att = (gate_attn * d_hidden).astype(jnp.bfloat16)
    grad_out = jnp.einsum("sti,stj->ij", mixed, d_att, preferred_element_type=jnp.float32)
    d_mixed = jnp.einsum("stj,ij->sti", d_att, out_weight, preferred_element_type=jnp.float32)
    d_attn = (gate_val * d_mixed).astype(jnp.bfloat16)
    d_gate_pre = d_mixed * attn * gate_val * (1.0 - gate_val)
    d_attn4 = d_attn.reshape(samples_dev, tok_rows, heads, head_dim)
    row_delta = jnp.sum(d_attn4.astype(jnp.float32) * attn4, axis=-1)

    def backward_fold(state, block_kv):
        block_len = block_length(block_kv.shape[1])
        count = block_kv.shape[1] // block_len

        def backward_step(carry, index):
            d_query, d_kv, d_bias = carry
            sub_offset = index * block_len
            sub_kv = lax.dynamic_slice_in_dim(block_kv, index * block_len, block_len, 1)
            keys_block = sub_kv[..., :width].reshape(samples_dev, block_len, heads, head_dim)
            values_block = sub_kv[..., width:].reshape(samples_dev, block_len, heads, head_dim)
            scores = block_scores(sub_kv, sub_offset)
            attn_probs = jnp.exp(scores - log_sum[..., None])
            d_probs = jnp.einsum(
                "sqhd,skhd->sqhk", d_attn4, values_block, preferred_element_type=jnp.float32
            )
            d_scores = (attn_probs * (d_probs - row_delta[..., None])).astype(jnp.bfloat16)
            d_query = (
                d_query
                + jnp.einsum(
                    "sqhk,skhd->sqhd", d_scores, keys_block, preferred_element_type=jnp.float32
                )
                * score_scale
            )
            d_keys = (
                jnp.einsum("sqhk,sqhd->skhd", d_scores, query, preferred_element_type=jnp.float32)
                * score_scale
            )
            d_values = jnp.einsum(
                "sqhk,sqhd->skhd",
                attn_probs.astype(jnp.bfloat16),
                d_attn4,
                preferred_element_type=jnp.float32,
            )
            d_new = jnp.concatenate(
                [
                    d_keys.reshape(samples_dev, block_len, width),
                    d_values.reshape(samples_dev, block_len, width),
                ],
                axis=-1,
            )
            d_kv = lax.dynamic_update_slice(d_kv, d_new, (zero_index, sub_offset, zero_index))
            bias_part = struct_sum(d_scores.astype(jnp.float32), struct_id, structs)
            d_bias = lax.dynamic_update_slice(
                d_bias, bias_part, (zero_index, zero_index, zero_index, sub_offset)
            )
            return ((d_query, d_kv, d_bias), None)

        result, ignored = lax.scan(
            jax.checkpoint(backward_step), state, jnp.arange(count, dtype=jnp.int32)
        )
        return result

    backward_init = (
        jnp.zeros((samples_dev, tok_rows, heads, head_dim), jnp.float32),
        jnp.zeros((samples_dev, seq_total, 2 * width), jnp.float32),
        jnp.zeros((structs, tok_rows, heads, seq_total), jnp.float32),
    )
    d_query, d_kv, d_bias = backward_fold(
        backward_init, lax.all_gather(keys_values, "blk", axis=1, tiled=True)
    )
    d_kv_own = lax.psum_scatter(
        d_kv.astype(jnp.bfloat16), "blk", scatter_dimension=1, tiled=True
    ).astype(jnp.float32)
    d_proj = jnp.concatenate(
        [d_query.reshape(samples_dev, tok_rows, width), d_kv_own, d_gate_pre], axis=-1
    ).astype(jnp.bfloat16)
    grad_qkvg = jnp.einsum("sti,stj->ij", x_attn, d_proj, preferred_element_type=jnp.float32)
    grad_query_bias = jnp.sum(d_proj[..., :width].astype(jnp.float32), axis=(0, 1))
    d_xa = jnp.einsum("stj,ij->sti", d_proj, qkvg_weight, preferred_element_type=jnp.float32)
    act_grad = d_hidden + act_norm_back(d_xa * scale_attn)[0]
    d_cond_attn = jnp.concatenate(
        [
            d_xa * act_hat * scale_attn * (1.0 - scale_attn),
            d_xa,
            d_hidden * att_out * gate_attn * (1.0 - gate_attn),
        ],
        axis=-1,
    )
    d_cond_all = jnp.concatenate(
        [struct_sum(d_cond_attn, struct_id, structs), struct_sum(d_cond_trans, struct_id, structs)],
        axis=-1,
    )
    bias_sum, cond_sum = (
        lax.psum_scatter(
            d_bias.astype(jnp.bfloat16), "samp", scatter_dimension=3, tiled=True
        ).astype(jnp.float32),
        lax.psum_scatter(
            d_cond_all.astype(jnp.bfloat16), "samp", scatter_dimension=1, tiled=True
        ).astype(jnp.float32),
    )
    bias_round = bias_sum.astype(jnp.bfloat16)
    grad_pair_weight = jnp.einsum(
        "crkz,crhk->zh", pair_in, bias_round, preferred_element_type=jnp.float32
    )
    d_pair_in = jnp.einsum(
        "crhk,zh->crkz", bias_round, pair_weight, preferred_element_type=jnp.float32
    )
    grad_pair_gain = jnp.sum(d_pair_in * pair_hat, axis=(0, 1, 2))
    pair_grad = pair_norm_back(d_pair_in * pair_gain)[0]
    slice_len = cond_sum.shape[1]
    slice_start = lax.axis_index("samp") * slice_len
    single_part = lax.dynamic_slice_in_dim(single_cond, slice_start, slice_len, 1).astype(
        jnp.float32
    )
    part_hat, part_norm_back = jax.vjp(norm_rows, single_part)
    cond_round = cond_sum.astype(jnp.bfloat16)
    d_part_hat = jnp.zeros_like(part_hat)
    cond_grads = []
    cond_bias_grads = []
    gain_grads = []
    for sublayer in range(2):
        d_layer = cond_round[..., sublayer * 3 * width : (sublayer + 1) * 3 * width]
        part_in = lax.dynamic_slice_in_dim(cond_inputs[sublayer], slice_start, slice_len, 1)
        cond_grads.append(
            jnp.einsum("cti,ctj->ij", part_in, d_layer, preferred_element_type=jnp.float32)
        )
        layer_sums = jnp.sum(d_layer.astype(jnp.float32), axis=(0, 1))
        cond_bias_grads.append(jnp.concatenate([layer_sums[:width], layer_sums[2 * width :]]))
        d_in = jnp.einsum(
            "ctj,ij->cti", d_layer, cond_weight[sublayer], preferred_element_type=jnp.float32
        )
        gain_grads.append(jnp.sum(d_in * part_hat, axis=(0, 1)))
        d_part_hat = d_part_hat + d_in * single_gain[sublayer]
    single_part_grad = part_norm_back(d_part_hat)[0]
    single_grad = lax.all_gather(single_part_grad, "samp", axis=1, tiled=True)
    grad_cond = jnp.stack(cond_grads)
    part_qkvg, part_out, part_in_w, part_down, part_cond = (
        lax.psum_scatter(
            grad_qkvg.astype(jnp.bfloat16), "blk", scatter_dimension=1, tiled=True
        ).astype(jnp.float32),
        lax.psum_scatter(
            grad_out.astype(jnp.bfloat16), "blk", scatter_dimension=1, tiled=True
        ).astype(jnp.float32),
        lax.psum_scatter(
            grad_in.astype(jnp.bfloat16), "blk", scatter_dimension=1, tiled=True
        ).astype(jnp.float32),
        lax.psum_scatter(
            grad_down.astype(jnp.bfloat16), "blk", scatter_dimension=1, tiled=True
        ).astype(jnp.float32),
        lax.psum_scatter(
            grad_cond.astype(jnp.bfloat16), "blk", scatter_dimension=2, tiled=True
        ).astype(jnp.float32),
    )
    qkvg_grad, out_grad, in_grad, down_grad, cond_grad = (
        lax.psum_scatter(
            part_qkvg.astype(jnp.bfloat16), "samp", scatter_dimension=0, tiled=True
        ).astype(jnp.float32),
        lax.psum_scatter(
            part_out.astype(jnp.bfloat16), "samp", scatter_dimension=0, tiled=True
        ).astype(jnp.float32),
        lax.psum_scatter(
            part_in_w.astype(jnp.bfloat16), "samp", scatter_dimension=0, tiled=True
        ).astype(jnp.float32),
        lax.psum_scatter(
            part_down.astype(jnp.bfloat16), "samp", scatter_dimension=0, tiled=True
        ).astype(jnp.float32),
        lax.psum_scatter(
            part_cond.astype(jnp.bfloat16), "samp", scatter_dimension=1, tiled=True
        ).astype(jnp.float32),
    )
    query_bias_grad, cond_bias_grad, single_gain_grad, pair_gain_grad, pair_weight_grad = lax.psum(
        (
            grad_query_bias,
            jnp.stack(cond_bias_grads),
            jnp.stack(gain_grads),
            grad_pair_gain,
            grad_pair_weight,
        ),
        ("samp", "blk"),
    )
    return (
        block_out,
        act_grad,
        single_grad,
        pair_grad,
        qkvg_grad,
        query_bias_grad,
        out_grad,
        in_grad,
        down_grad,
        cond_grad,
        cond_bias_grad,
        single_gain_grad,
        pair_gain_grad,
        pair_weight_grad,
    )


FORWARD_GROUP = 4
BACKWARD_GROUP = 4
KEY_CHUNK = 128


def nt_dot(left, right):
    return lax.dot_general(
        left, right, (((1,), (1,)), ((), ())), preferred_element_type=jnp.float32
    )


def nn_dot(left, right):
    return lax.dot_general(
        left, right, (((1,), (0,)), ((), ())), preferred_element_type=jnp.float32
    )


def tn_dot(left, right):
    return lax.dot_general(
        left, right, (((0,), (0,)), ((), ())), preferred_element_type=jnp.float32
    )


def split_two(value):
    high = value.astype(jnp.bfloat16)
    return high, (value - high.astype(jnp.float32)).astype(jnp.bfloat16)


def spends(micros):
    return pl.CostEstimate(
        flops=int(micros * 1e9), bytes_accessed=int(micros * 3e6), transcendentals=0
    )


def pair_rows(pair_ref):
    quarters, rows, cols, chans = pair_ref.shape[2:]
    both = jnp.concatenate([pair_ref[0, 0, quarter] for quarter in range(quarters)], axis=1)
    return both.reshape(rows * quarters * cols, chans)


def pair_forward_kernel(pair_ref, coef_ref, coef_sum_ref, bias_ref, mean_ref, rstd_ref):
    heads = bias_ref.shape[0]
    rows, lanes = mean_ref.shape[2:]
    chans = pair_ref.shape[5]
    cells = pair_rows(pair_ref)
    wide = cells.astype(jnp.float32)
    square_high, square_low = split_two(wide * wide)
    sums = nt_dot(coef_ref[...], jnp.concatenate([cells, square_high], axis=1))
    low_sums = nt_dot(jnp.ones((16, chans), jnp.bfloat16), square_low)
    raw = sums[:heads] + sums[heads : 2 * heads]
    total = sums[2 * heads : 2 * heads + 1]
    squares = sums[2 * heads + 8 : 2 * heads + 9] + low_sums[0:1]
    total_high = total.astype(jnp.bfloat16).astype(jnp.float32)
    total_low = total - total_high
    spread = squares * chans - total_high * total_high
    spread = spread - 2.0 * total_high * total_low - total_low * total_low
    rstd = lax.rsqrt(jnp.maximum(spread, 0.0) * (1.0 / (chans * chans)) + EPS)
    mean = total * (1.0 / chans)
    bias = (raw - coef_sum_ref[...] * mean) * (rstd * LOG2E)
    bias_ref[:, 0, 0] = bias.reshape(heads, rows, lanes).astype(jnp.bfloat16)
    mean_ref[0, 0] = mean.reshape(rows, lanes)
    rstd_ref[0, 0] = rstd.reshape(rows, lanes)


def pair_forward(pair, pair_gain, pair_weight):
    structs, halves, quarters, rows, cols, chans = pair.shape
    heads = pair_weight.shape[1]
    lanes = quarters * cols
    step = 32
    gained = pair_weight.astype(jnp.float32) * pair_gain[:, None]
    high, low = split_two(gained.T)
    ones_row = jnp.zeros((8, chans), jnp.bfloat16).at[0].set(1.0)
    blank = jnp.zeros((8, chans), jnp.bfloat16)
    coef = jnp.concatenate(
        [
            jnp.concatenate([high, low, ones_row, blank], axis=0),
            jnp.concatenate([jnp.zeros((2 * heads, chans), jnp.bfloat16), blank, ones_row], axis=0),
        ],
        axis=1,
    )
    coef_sum = jnp.sum(gained, axis=0)[:, None]
    return pl.pallas_call(
        pair_forward_kernel,
        grid=(halves, structs, rows // step),
        in_specs=[
            pl.BlockSpec((1, 1, quarters, step, cols, chans), lambda h, c, r: (c, h, 0, r, 0, 0)),
            pl.BlockSpec(coef.shape, lambda h, c, r: (0, 0)),
            pl.BlockSpec(coef_sum.shape, lambda h, c, r: (0, 0)),
        ],
        out_specs=[
            pl.BlockSpec((heads, 1, 1, step, lanes), lambda h, c, r: (0, h, c, r, 0)),
            pl.BlockSpec((1, 1, step, lanes), lambda h, c, r: (h, c, r, 0)),
            pl.BlockSpec((1, 1, step, lanes), lambda h, c, r: (h, c, r, 0)),
        ],
        out_shape=[
            jax.ShapeDtypeStruct((heads, halves, structs, rows, lanes), jnp.bfloat16),
            jax.ShapeDtypeStruct((halves, structs, rows, lanes), jnp.float32),
            jax.ShapeDtypeStruct((halves, structs, rows, lanes), jnp.float32),
        ],
        compiler_params=pltpu.CompilerParams(vmem_limit_bytes=VMEM_BYTES),
        cost_estimate=spends(20),
        name="pair_forward",
    )(pair, coef, coef_sum)


def pair_backward_kernel(
    pair_ref, d_bias_ref, bias_ref, mean_ref, rstd_ref, coef_ref, coef_sum_ref, *refs
):
    grad_ref, inner_ref, offset_ref = refs[-3:]
    heads = d_bias_ref.shape[0]
    rows, lanes = mean_ref.shape[2:]
    quarters, _, cols, chans = pair_ref.shape[2:]
    count = rows * lanes
    cells = pair_rows(pair_ref)
    d_bias = d_bias_ref[:, 0, 0].astype(jnp.float32)
    bias = bias_ref[:, 0, 0].astype(jnp.float32)
    mean = mean_ref[0]
    rstd = rstd_ref[0]
    g_mean = jnp.sum(d_bias * coef_sum_ref[...], axis=0, keepdims=True) * (1.0 / chans)
    gy_mean = jnp.sum(d_bias * bias, axis=0, keepdims=True) * (LN2 / chans)
    slope = rstd * rstd * gy_mean
    shift = mean * slope - rstd * g_mean
    scaled = d_bias * rstd

    @pl.when((pl.program_id(0) == 0) & (pl.program_id(1) == 0))
    def _():
        inner_ref[...] = jnp.zeros_like(inner_ref)
        offset_ref[...] = jnp.zeros_like(offset_ref)

    offset_ref[...] += jnp.sum(scaled * mean, axis=1)
    scaled_high, scaled_low = split_two(scaled.reshape(heads, count))
    ends = jnp.concatenate([shift, slope], axis=0).reshape(2, count)
    ends_high, ends_low = split_two(ends)
    blank = jnp.zeros((12, count), jnp.bfloat16)
    inner_ref[...] += nn_dot(jnp.concatenate([scaled_high, scaled_low], axis=0), cells)
    factors = jnp.concatenate([scaled_high, scaled_low, ends_high, ends_low, blank], axis=0)
    spread = tn_dot(factors, coef_ref[...])
    grad = spread[:, :chans] - cells.astype(jnp.float32) * spread[:, chans:]
    grad = grad.reshape(rows, lanes, chans)
    for quarter in range(quarters):
        grad_ref[0, 0, quarter] = grad[:, quarter * cols : (quarter + 1) * cols]


def pair_backward(half, pair, d_bias, bias, mean, rstd, pair_gain, pair_weight, partial):
    structs, _, quarters, half_rows, cols, chans = pair.shape
    heads = pair_weight.shape[1]
    lanes = quarters * cols
    step = 32
    gained = (pair_weight.astype(jnp.float32) * pair_gain[:, None]).T
    coef_sum = jnp.sum(gained, axis=1)[:, None, None]
    ones = jnp.ones((1, chans), jnp.bfloat16)
    zeros = jnp.zeros((1, chans), jnp.bfloat16)
    rows = gained.astype(jnp.bfloat16)
    left = jnp.concatenate([rows, rows, ones, zeros, ones, zeros], axis=0)
    right = jnp.concatenate(
        [jnp.zeros((2 * heads, chans), jnp.bfloat16), zeros, ones, zeros, ones], axis=0
    )
    coef = jnp.concatenate([left, right], axis=1)
    coef = jnp.concatenate([coef, jnp.zeros((12, 2 * chans), jnp.bfloat16)], axis=0)
    grad, inner, offset = pl.pallas_call(
        pair_backward_kernel,
        grid=(structs, half_rows // step),
        in_specs=[
            pl.BlockSpec((1, 1, quarters, step, cols, chans), lambda c, r: (c, half, 0, r, 0, 0)),
            pl.BlockSpec((heads, 1, 1, step, lanes), lambda c, r: (0, half, c, r, 0)),
            pl.BlockSpec((heads, 1, 1, step, lanes), lambda c, r: (0, half, c, r, 0)),
            pl.BlockSpec((1, 1, step, lanes), lambda c, r: (half, c, r, 0)),
            pl.BlockSpec((1, 1, step, lanes), lambda c, r: (half, c, r, 0)),
            pl.BlockSpec(coef.shape, lambda c, r: (0, 0)),
            pl.BlockSpec(coef_sum.shape, lambda c, r: (0, 0, 0)),
        ]
        + [pl.BlockSpec(memory_space=pl.ANY)] * len(partial),
        out_specs=[
            pl.BlockSpec((1, 1, quarters, step, cols, chans), lambda c, r: (c, half, 0, r, 0, 0)),
            pl.BlockSpec((2 * heads, chans), lambda c, r: (0, 0)),
            pl.BlockSpec((heads, lanes), lambda c, r: (0, 0)),
        ],
        input_output_aliases={7: 0} if partial else {},
        out_shape=[
            jax.ShapeDtypeStruct(pair.shape, jnp.float32),
            jax.ShapeDtypeStruct((2 * heads, chans), jnp.float32),
            jax.ShapeDtypeStruct((heads, lanes), jnp.float32),
        ],
        compiler_params=pltpu.CompilerParams(vmem_limit_bytes=VMEM_BYTES),
        cost_estimate=spends(13),
        name="pair_backward",
    )(pair, d_bias, bias, mean, rstd, coef, coef_sum, *partial)
    moment = inner[:heads] + inner[heads:] - jnp.sum(offset, axis=1, keepdims=True)
    grad_weight = moment.T * pair_gain[:, None]
    grad_gain = jnp.sum(moment.T * pair_weight.astype(jnp.float32), axis=1)
    return grad, grad_weight, grad_gain


def attention_forward_kernel(
    ids_ref, limits_ref, blk_ref,
    query_ref, key_own_ref, key_far_ref, value_own_ref, value_far_ref, bias_ref,
    sent_ref, attn_ref, inverse_ref, weights_ref,
    table_ref,
):
    sources, _, structs, _, lanes = bias_ref.shape
    tile = query_ref.shape[2]
    cols = lanes // 2
    sample = pl.program_id(0)
    near = sources // 2

    @pl.when(sample == 0)
    def _():
        for struct in range(structs):
            limit = limits_ref[struct]
            for source in range(sources):
                part = bias_ref[source, 0, struct].astype(jnp.float32).T
                part = jnp.concatenate([part[:cols], part[cols:]], axis=1)
                position = (
                    lax.rem(source // near + blk_ref[0], 2) * (near * cols) + (source % near) * cols
                )
                position = pl.multiple_of(position, cols)
                keys = source * cols + lax.broadcasted_iota(jnp.int32, part.shape, 0)
                table_ref[struct, pl.ds(position, cols)] = jnp.where(
                    keys < limit, part, -1e30
                ).astype(jnp.bfloat16)

    head_dim = query_ref.shape[1]
    for member in range(query_ref.shape[0]):
        struct = ids_ref[sample * query_ref.shape[0] + member]
        keys_t = jnp.concatenate([key_own_ref[member], key_far_ref[member]], axis=1)
        keys = keys_t.astype(jnp.float32).T.astype(jnp.bfloat16)
        values_t = jnp.concatenate([value_own_ref[member], value_far_ref[member]], axis=1)
        values_t = jnp.concatenate(
            [values_t, jnp.ones((16, values_t.shape[1]), jnp.bfloat16)], axis=0
        )
        query = query_ref[member]
        scores = []
        peak = None
        for start in range(0, keys.shape[0], KEY_CHUNK):
            part = nn_dot(keys[start : start + KEY_CHUNK], query)
            part = part + table_ref[struct, start : start + KEY_CHUNK].astype(jnp.float32)
            part_peak = jnp.max(part.reshape(-1, 8, tile), axis=0)
            peak = part_peak if peak is None else jnp.maximum(peak, part_peak)
            scores.append(part)
        peak = jnp.max(peak, axis=0, keepdims=True)
        summed = 0.0
        for index, part in enumerate(scores):
            span = slice(index * KEY_CHUNK, (index + 1) * KEY_CHUNK)
            weights = jnp.exp2(part - peak).astype(jnp.bfloat16)
            weights_ref[member, span] = weights
            summed = summed + nn_dot(values_t[:, span], weights)
        inverse = 1.0 / summed[head_dim : head_dim + 1]
        attn = summed[:head_dim] * inverse
        attn_ref[member] = attn
        sent_ref[member] = attn.astype(jnp.bfloat16)
        inverse_ref[member] = inverse


def attention_forward(half, ids, limits, blk, qkv, kv_far, bias):
    samples, triple, tokens = qkv.shape
    head_dim = triple // 3
    structs = bias.shape[2]
    tile = tokens // 2
    keys = 2 * tokens
    group = FORWARD_GROUP
    part = (group, head_dim, tokens)
    tile_part = (group, head_dim, tile)
    grid_spec = pltpu.PrefetchScalarGridSpec(
        num_scalar_prefetch=3,
        grid=(samples // group,),
        in_specs=[
            pl.BlockSpec(tile_part, lambda n, *_: (n, 0, half)),
            pl.BlockSpec(part, lambda n, *_: (n, 1, 0)),
            pl.BlockSpec(part, lambda n, *_: (n, 0, 0)),
            pl.BlockSpec(part, lambda n, *_: (n, 2, 0)),
            pl.BlockSpec(part, lambda n, *_: (n, 1, 0)),
            pl.BlockSpec(
                (bias.shape[0], 1) + bias.shape[2:], lambda n, *_: (0, half, 0, 0, 0)
            ),
        ],
        out_specs=[
            pl.BlockSpec(tile_part, lambda n, *_: (n, 0, 0)),
            pl.BlockSpec(tile_part, lambda n, *_: (n, 0, 0)),
            pl.BlockSpec((group, 1, tile), lambda n, *_: (n, 0, 0)),
            pl.BlockSpec((group, keys, tile), lambda n, *_: (n, 0, 0)),
        ],
        scratch_shapes=[pltpu.VMEM((structs, keys, tile), jnp.bfloat16)],
    )
    return pl.pallas_call(
        attention_forward_kernel,
        grid_spec=grid_spec,
        out_shape=[
            jax.ShapeDtypeStruct((samples, head_dim, tile), jnp.bfloat16),
            jax.ShapeDtypeStruct((samples, head_dim, tile), jnp.float32),
            jax.ShapeDtypeStruct((samples, 1, tile), jnp.float32),
            jax.ShapeDtypeStruct((samples, keys, tile), jnp.bfloat16),
        ],
        compiler_params=pltpu.CompilerParams(vmem_limit_bytes=VMEM_BYTES),
        cost_estimate=spends(14),
        name="attention_forward",
    )(ids, limits, blk, qkv, qkv, kv_far, qkv, kv_far, bias)


def attention_backward_kernel(
    ids_ref, blk_ref,
    query_ref, key_own_ref, key_far_ref, value_own_ref, value_far_ref,
    d_attn_ref, attn_ref, inverse_ref, weights_ref, *refs, score_scale,
):
    d_query_ref, d_own_ref, d_far_ref, d_bias_ref, total_ref = refs[-5:]
    sources, structs, _, lanes = d_bias_ref.shape
    cols = lanes // 2
    sample = pl.program_id(0)
    near = sources // 2
    group, head_dim, tile = query_ref.shape
    tokens = key_own_ref.shape[2]

    @pl.when(sample == 0)
    def _():
        total_ref[...] = jnp.zeros_like(total_ref)

    tail = jnp.zeros((14, tile), jnp.bfloat16)
    for index in range(group):
        struct = ids_ref[sample * group + index]
        keys_t = jnp.concatenate([key_own_ref[index], key_far_ref[index]], axis=1)
        values_t = jnp.concatenate([value_own_ref[index], value_far_ref[index]], axis=1)
        values_t = jnp.concatenate(
            [values_t, jnp.ones((16, values_t.shape[1]), jnp.bfloat16)], axis=0
        )
        values = turned(values_t)
        inverse = inverse_ref[index]
        d_attn = d_attn_ref[index].astype(jnp.float32)
        delta = jnp.sum(d_attn * attn_ref[index], axis=0, keepdims=True)
        d_attn = (d_attn * inverse).astype(jnp.bfloat16)
        delta_high, delta_low = split_two(-delta * inverse)
        d_probs = nn_dot(values, jnp.concatenate([d_attn, delta_high, delta_low, tail], axis=0))
        weights = weights_ref[index]
        d_scores = weights.astype(jnp.float32) * d_probs
        total_ref[struct] += d_scores
        d_scores = d_scores.astype(jnp.bfloat16)
        d_values = nn_dot(weights, turned(d_attn)).T
        d_keys = nn_dot(d_scores, turned(query_ref[index])).T * LN2
        d_query_ref[index] = (nn_dot(keys_t, d_scores) * score_scale).astype(jnp.bfloat16)
        for place, value in ((slice(0, head_dim), d_keys), (slice(head_dim, None), d_values)):
            own, far = value[:, :tokens], value[:, tokens:]
            if len(refs) > 5:
                own = own + refs[0][index, place].astype(jnp.float32)
                far = far + refs[1][index, place].astype(jnp.float32)
            d_own_ref[index, place] = own.astype(jnp.bfloat16)
            d_far_ref[index, place] = far.astype(jnp.bfloat16)

    @pl.when(sample == pl.num_programs(0) - 1)
    def _():
        for member in range(structs):
            for source in range(sources):
                position = (
                    lax.rem(source // near + blk_ref[0], 2) * (near * cols) + (source % near) * cols
                )
                position = pl.multiple_of(position, cols)
                part = total_ref[member, pl.ds(position, cols)]
                part = jnp.concatenate([part[:, : tile // 2], part[:, tile // 2 :]], axis=0)
                d_bias_ref[source, member] = part.T.astype(jnp.bfloat16)


def attention_backward(half, ids, blk, qkv, kv_far, d_attn, attn, inverse, weights, bias, partial):
    samples, triple, tokens = qkv.shape
    head_dim = triple // 3
    keys, tile = weights.shape[1:]
    bias_shape = bias.shape[:1] + bias.shape[2:]
    structs = bias.shape[2]
    group = BACKWARD_GROUP
    part = (group, head_dim, tokens)
    tile_part = pl.BlockSpec((group, head_dim, tile), lambda n, *_: (n, 0, 0))
    pair_part = pl.BlockSpec((group, 2 * head_dim, tokens), lambda n, *_: (n, 0, 0))
    grid_spec = pltpu.PrefetchScalarGridSpec(
        num_scalar_prefetch=2,
        grid=(samples // group,),
        in_specs=[
            pl.BlockSpec((group, head_dim, tile), lambda n, *_: (n, 0, half)),
            pl.BlockSpec(part, lambda n, *_: (n, 1, 0)),
            pl.BlockSpec(part, lambda n, *_: (n, 0, 0)),
            pl.BlockSpec(part, lambda n, *_: (n, 2, 0)),
            pl.BlockSpec(part, lambda n, *_: (n, 1, 0)),
            tile_part,
            tile_part,
            pl.BlockSpec((group, 1, tile), lambda n, *_: (n, 0, 0)),
            pl.BlockSpec((group, keys, tile), lambda n, *_: (n, 0, 0)),
        ]
        + [pair_part] * len(partial),
        out_specs=[
            tile_part, pair_part, pair_part, pl.BlockSpec(bias_shape, lambda n, *_: (0, 0, 0, 0))
        ],
        scratch_shapes=[pltpu.VMEM((structs, keys, tile), jnp.float32)],
    )
    pair_shape = jax.ShapeDtypeStruct((samples, 2 * head_dim, tokens), jnp.bfloat16)
    return pl.pallas_call(
        functools.partial(attention_backward_kernel, score_scale=1.0 / math.sqrt(head_dim)),
        grid_spec=grid_spec,
        out_shape=[
            jax.ShapeDtypeStruct((samples, head_dim, tile), jnp.bfloat16),
            pair_shape,
            pair_shape,
            jax.ShapeDtypeStruct(bias_shape, jnp.bfloat16),
        ],
        compiler_params=pltpu.CompilerParams(vmem_limit_bytes=VMEM_BYTES),
        cost_estimate=spends(13),
        name="attention_backward",
    )(ids, blk, qkv, qkv, kv_far, qkv, kv_far, d_attn, attn, inverse, weights, *partial)


def turned(value):
    return value.astype(jnp.float32).T.astype(jnp.bfloat16)


def store_tiles(out_refs, core, grad, start):
    groups = out_refs[0].shape[0]
    if core is None:
        rows = grad.reshape(groups, -1, grad.shape[1]).astype(jnp.bfloat16)
        out_refs[0][:, start : start + rows.shape[1]] = rows
        return
    rows = grad.reshape(groups, 2, -1, grad.shape[1]).astype(jnp.bfloat16)
    span = slice(start, start + rows.shape[2])
    for mine in range(2):

        @pl.when(core == mine)
        def _():
            out_refs[0][:, span] = rows[:, mine]
            out_refs[1][:, span] = rows[:, 1 - mine]


def cond_tiles(out_refs, core, cond_t, d_cond_ref, place, stride):
    tiles = out_refs[0].shape[0] * (1 if core is None else 2)
    rows = cond_t.shape[0] // tiles
    per_blk = d_cond_ref.shape[1] // (2 * TILE_COLS)
    blank = jnp.zeros((tiles, -(per_blk * rows) % 16, TILE_COLS), jnp.float32)
    for blk in range(2):
        parts = []
        for chunk in range(per_blk):
            start = (blk * per_blk + chunk) * TILE_COLS
            grad = nn_dot(cond_t, d_cond_ref[:, start : start + TILE_COLS])
            parts.append(grad.reshape(tiles, rows, TILE_COLS))
        grad = jnp.concatenate(parts + [blank], axis=1).reshape(-1, TILE_COLS)
        store_tiles(out_refs, core, grad, blk * stride + place)


def early_grads_kernel(*refs):
    out_refs = refs[-1:]
    pairs = [refs[2 * index : 2 * index + 2] for index in range(7)]
    x_refs, d_up_refs, hidden_refs, d_trans_refs, mixed_refs, d_att_refs, d_cond_refs = pairs
    cond_ref = refs[14]
    place = 0
    tiles = out_refs[0].shape[0]
    stride = out_refs[0].shape[1] // 2
    for left, right_refs in (
        (turned(rows_of(x_refs)), d_up_refs),
        (turned(rows_of(hidden_refs)), d_trans_refs),
        (jnp.concatenate([mixed_refs[0][...], mixed_refs[1][...]], axis=1), d_att_refs),
    ):
        rows = left.shape[0] // tiles
        per_blk = right_refs[0].shape[1] // (2 * TILE_COLS)
        for chunk in range(2 * per_blk):
            span = slice(chunk * TILE_COLS, (chunk + 1) * TILE_COLS)
            right = jnp.concatenate([right_refs[0][:, span], right_refs[1][:, span]], axis=0)
            start = chunk // per_blk * stride + place + chunk % per_blk * rows
            store_tiles(out_refs, None, nn_dot(left, right), start)
        place += per_blk * rows
    cond_tiles(out_refs, None, turned(cond_ref[...]), rows_of(d_cond_refs), place, stride)


def rows_of(refs):
    return jnp.concatenate([refs[0][...], refs[1][...]], axis=0)


def early_grads(samp, operands, cond_in):
    x_trans, d_up, hidden, d_trans, mixed, d_att, d_cond = (pair[0] for pair in operands)
    sizes = [
        x_trans.shape[1] * d_up.shape[1],
        hidden.shape[1] * d_trans.shape[1],
        mixed.shape[0] * d_att.shape[1],
        cond_in.shape[1] * d_cond.shape[1],
    ]
    rows = 16 * math.ceil(sum(sizes) / (samp * 2 * TILE_COLS * 16))
    vmem = pl.BlockSpec(memory_space=pltpu.VMEM)
    return pl.pallas_call(
        early_grads_kernel,
        in_specs=[vmem] * (2 * len(operands) + 1),
        out_specs=vmem,
        out_shape=jax.ShapeDtypeStruct((samp, 2 * rows, TILE_COLS), jnp.bfloat16),
        compiler_params=pltpu.CompilerParams(vmem_limit_bytes=VMEM_BYTES),
        cost_estimate=spends(15),
        name="early_grads",
    )(*[value for pair in operands for value in pair], cond_in)


def norm_parts(value):
    center = value - jnp.mean(value, axis=1, keepdims=True)
    rstd = lax.rsqrt(jnp.mean(center * center, axis=1, keepdims=True) + EPS)
    return center * rstd, rstd


def norm_grad(grad, hat, rstd):
    inner = jnp.mean(grad * hat, axis=1, keepdims=True)
    return rstd * (grad - jnp.mean(grad, axis=1, keepdims=True) - hat * inner)


def sigmoid(value):
    return 1.0 / (1.0 + jnp.exp(-value))


def first_kernel(
    place_ref, single_ref, act_ref, cond_weight_ref, cond_bias_ref, gain_ref, weight_ref,
    query_bias_ref, qkv_ref, gate_t_ref, x_ref, scale_ref, gate_ref, *, score_scale,
):
    heads = qkv_ref.shape[0]
    head_dim = qkv_ref.shape[1] // 3
    tokens, width = act_ref.shape
    single_hat, _ = norm_parts(single_ref[place_ref[1]].astype(jnp.float32))
    cond_in = (single_hat * gain_ref[...]).astype(jnp.bfloat16)
    bias = cond_bias_ref[...]
    scale = sigmoid(nn_dot(cond_in, cond_weight_ref[0, :, :width]) + bias[:, :width])
    scale_ref[...] = scale
    shift = nn_dot(cond_in, cond_weight_ref[0, :, width : 2 * width])
    gate_ref[...] = sigmoid(nn_dot(cond_in, cond_weight_ref[0, :, 2 * width :]) + bias[:, width:])
    act_hat, _ = norm_parts(act_ref[...].astype(jnp.float32))
    x_attn = (scale * act_hat + shift).astype(jnp.bfloat16)
    x_ref[...] = x_attn
    for part in range(4):
        value = nn_dot(x_attn, weight_ref[:, part * width : (part + 1) * width])
        if part == 0:
            value = (value + query_bias_ref[...]) * (score_scale * LOG2E)
        value = value.T
        if part == 3:
            gate_t_ref[...] = sigmoid(value)
        else:
            value = value.reshape(heads, head_dim, tokens).astype(jnp.bfloat16)
            qkv_ref[:, part * head_dim : (part + 1) * head_dim] = value


def first_call(heads, place, single_cond, act, cond_weight, cond_bias, gain, weight, query_bias):
    tokens, width = act.shape
    head_dim = width // heads
    vmem = pl.BlockSpec(memory_space=pltpu.VMEM)
    wide = jax.ShapeDtypeStruct((tokens, width), jnp.float32)
    return pl.pallas_call(
        functools.partial(first_kernel, score_scale=1.0 / math.sqrt(head_dim)),
        grid=(1,),
        in_specs=[
            pl.BlockSpec(memory_space=pltpu.SMEM),
            vmem,
            vmem,
            pl.BlockSpec((1,) + cond_weight.shape[1:], lambda _: (0, 0, 0)),
            vmem,
            vmem,
            vmem,
            vmem,
        ],
        out_specs=[vmem] * 5,
        out_shape=[
            jax.ShapeDtypeStruct((heads, 3 * head_dim, tokens), jnp.bfloat16),
            jax.ShapeDtypeStruct((width, tokens), jnp.float32),
            jax.ShapeDtypeStruct((tokens, width), jnp.bfloat16),
            wide,
            wide,
        ],
        compiler_params=pltpu.CompilerParams(vmem_limit_bytes=VMEM_BYTES),
        cost_estimate=spends(12),
        name="first",
    )(place, single_cond, act, cond_weight, cond_bias, gain, weight, query_bias)


def middle_kernel(
    attn_ref, gate_t_ref, act_ref, gate_attn_ref, cond_ref, cotangent_ref,
    out_weight_ref, in_weight_ref, down_weight_ref,
    block_ref, x_ref, d_up_ref, hid_ref, d_trans_ref, mixed_ref, d_att_ref, d_cond_ref,
    d_hidden_ref, d_cond_gate_ref, d_gate_ref, d_attn_ref,
):
    tokens, width = act_ref.shape
    units = hid_ref.shape[1]
    attn = attn_ref[...].reshape(width, tokens).astype(jnp.float32)
    gate = gate_t_ref[...]
    mixed = gate * attn
    mixed_ref[...] = mixed.astype(jnp.bfloat16)
    att_out = nn_dot(mixed.T.astype(jnp.bfloat16), out_weight_ref[...])
    gate_attn = gate_attn_ref[...]
    hidden = act_ref[...].astype(jnp.float32) + gate_attn * att_out
    hat, rstd = norm_parts(hidden)
    scale = sigmoid(cond_ref[:, :width])
    x_trans = (scale * hat + cond_ref[:, width : 2 * width]).astype(jnp.bfloat16)
    x_ref[...] = x_trans
    up_gate = nn_dot(x_trans, in_weight_ref[:, :units])
    up_lin = nn_dot(x_trans, in_weight_ref[:, units:])
    sig = sigmoid(up_gate)
    silu = up_gate * sig
    hid = (silu * up_lin).astype(jnp.bfloat16)
    hid_ref[...] = hid
    gate_trans = sigmoid(cond_ref[:, 2 * width :])
    cotangent = cotangent_ref[...].astype(jnp.float32)
    gated = gate_trans * cotangent
    d_trans = gated.astype(jnp.bfloat16)
    d_trans_ref[...] = d_trans
    d_hid = nt_dot(d_trans, down_weight_ref[...])
    slope = sig * (1.0 + up_gate * (1.0 - sig))
    d_up_ref[:, :units] = (d_hid * up_lin * slope).astype(jnp.bfloat16)
    d_up_ref[:, units:] = (d_hid * silu).astype(jnp.bfloat16)
    d_xt = nt_dot(d_up_ref[...], in_weight_ref[...])
    scaled = d_xt * scale
    d_hidden = cotangent + norm_grad(scaled, hat, rstd)
    d_hidden_ref[...] = d_hidden
    d_att = (gate_attn * d_hidden).astype(jnp.bfloat16)
    d_att_ref[...] = d_att
    d_mixed = nt_dot(out_weight_ref[...], d_att)
    d_attn_ref[...] = (gate * d_mixed).astype(jnp.bfloat16).reshape(d_attn_ref.shape)
    d_gate_ref[...] = (d_mixed * mixed * (1.0 - gate)).astype(jnp.bfloat16)
    d_cond_gate_ref[...] = (d_hidden * att_out * gate_attn * (1.0 - gate_attn)).astype(jnp.bfloat16)
    trans = nn_dot(hid, down_weight_ref[...])
    block_ref[...] = (hidden + gate_trans * trans).astype(jnp.bfloat16)
    d_cond_ref[:, :width] = (scaled * hat * (1.0 - scale)).astype(jnp.bfloat16)
    d_cond_ref[:, width : 2 * width] = d_xt.astype(jnp.bfloat16)
    d_cond_ref[:, 2 * width :] = (gated * trans * (1.0 - gate_trans)).astype(jnp.bfloat16)


def middle_call(half, attn, gate_t, act, gate_attn, cond, cotangent, *weights):
    tile = attn.shape[2]
    width = act.shape[1]
    units = weights[2].shape[0]
    once = pl.Buffered(1)

    def whole(value):
        zeros = (0,) * value.ndim
        return pl.BlockSpec(value.shape, lambda _: zeros, pipeline_mode=once)

    def rows(value):
        return pl.BlockSpec((tile, value.shape[1]), lambda _: (half, 0), pipeline_mode=once)

    shapes = [
        jax.ShapeDtypeStruct((tile, width), jnp.bfloat16),
        jax.ShapeDtypeStruct((tile, width), jnp.bfloat16),
        jax.ShapeDtypeStruct((tile, 2 * units), jnp.bfloat16),
        jax.ShapeDtypeStruct((tile, units), jnp.bfloat16),
        jax.ShapeDtypeStruct((tile, width), jnp.bfloat16),
        jax.ShapeDtypeStruct((width, tile), jnp.bfloat16),
        jax.ShapeDtypeStruct((tile, width), jnp.bfloat16),
        jax.ShapeDtypeStruct((tile, 3 * width), jnp.bfloat16),
        jax.ShapeDtypeStruct((tile, width), jnp.float32),
        jax.ShapeDtypeStruct((tile, width), jnp.bfloat16),
        jax.ShapeDtypeStruct((width, tile), jnp.bfloat16),
        jax.ShapeDtypeStruct(attn.shape, jnp.bfloat16),
    ]
    return pl.pallas_call(
        middle_kernel,
        grid=(1,),
        in_specs=[
            whole(attn),
            pl.BlockSpec((width, tile), lambda _: (0, half), pipeline_mode=once),
            rows(act), rows(gate_attn), rows(cond), rows(cotangent),
        ]
        + [whole(weight) for weight in weights],
        out_specs=[whole(shape) for shape in shapes],
        out_shape=shapes,
        compiler_params=pltpu.CompilerParams(vmem_limit_bytes=VMEM_BYTES),
        cost_estimate=spends(10),
        name="middle",
    )(attn, gate_t, act, gate_attn, cond, cotangent, *weights)


def final_kernel(
    place_ref, x_ref, d_query_ref, d_kv_ref, d_gate_one_ref, d_gate_two_ref,
    weight_ref, act_ref, scale_ref,
    d_hidden_one_ref, d_hidden_two_ref, d_cond_gate_one_ref, d_cond_gate_two_ref, single_ref, d_hat_ref, cond_weight_ref, gain_ref,
    act_grad_ref, keep_one_ref, give_one_ref, keep_two_ref, give_two_ref, cond_sums_ref, query_sums_ref, gain_sums_ref,
    d_cond_ref,
):
    core = place_ref[0]
    struct = place_ref[1]
    ones = jnp.ones((8, x_ref.shape[0]), jnp.bfloat16)
    left = turned(x_ref[...])
    width, tokens = left.shape
    groups = keep_one_ref.shape[0]
    rows = width // (2 * groups)
    head_dim = d_query_ref.shape[1] // 2
    one = (keep_one_ref, give_one_ref)
    two = (keep_two_ref, give_two_ref)
    stride_one = keep_one_ref.shape[1] // 2
    share = tokens // (2 * groups)
    stride_two = (keep_two_ref.shape[1] - 2 * share) // 2
    first_slots = stride_one // rows
    d_xa = 0.0
    for part in range(4):
        if part == 0:
            right = jnp.concatenate(
                [d_query_ref[:, :head_dim], d_query_ref[:, head_dim:]], axis=2
            )
            right = right.reshape(width, tokens)
            query_sums_ref[...] = nt_dot(ones, right)
        elif part == 3:
            right = jnp.concatenate([d_gate_one_ref[...], d_gate_two_ref[...]], axis=1)
        else:
            right = d_kv_ref[:, (part - 1) * head_dim : part * head_dim].reshape(width, tokens)
        d_xa = d_xa + nn_dot(weight_ref[:, part * width : (part + 1) * width], right)
        for chunk in range(2):
            grad = nt_dot(left, right[chunk * TILE_COLS : (chunk + 1) * TILE_COLS])
            slot = 2 * (part % 2) + chunk
            if slot < first_slots:
                store_tiles(one, core, grad, part // 2 * stride_one + slot * rows)
            else:
                start = part // 2 * stride_two + (slot - first_slots) * rows
                store_tiles(two, core, grad, start)
    d_xa = d_xa.T
    act_hat, act_rstd = norm_parts(act_ref[...].astype(jnp.float32))
    scale = scale_ref[...].astype(jnp.float32)
    grad = d_xa * scale
    d_hidden = rows_of((d_hidden_one_ref, d_hidden_two_ref))
    act_grad_ref[...] = d_hidden + norm_grad(grad, act_hat, act_rstd)
    d_cond_ref[:, :width] = (grad * act_hat * (1.0 - scale)).astype(jnp.bfloat16)
    d_cond_ref[:, width : 2 * width] = d_xa.astype(jnp.bfloat16)
    d_cond_ref[:, 2 * width :] = rows_of((d_cond_gate_one_ref, d_cond_gate_two_ref))
    single_hat, single_rstd = norm_parts(single_ref[...].astype(jnp.float32))
    gain = gain_ref[...]
    cond_t = turned((single_hat * gain).astype(jnp.bfloat16))
    cond_tiles(two, core, cond_t, d_cond_ref, (4 - first_slots) * rows, stride_two)
    d_cond = d_cond_ref[...]
    cond_sums_ref[...] = nn_dot(ones, d_cond)
    d_in = nt_dot(d_cond, cond_weight_ref[...])
    gain_sums_ref[...] = jnp.sum(d_in * single_hat, axis=0, keepdims=True)
    single_grad = norm_grad(d_in * gain + d_hat_ref[...], single_hat, single_rstd)
    single_grad = single_grad.reshape(2 * groups, share, single_grad.shape[1])
    chosen = [jnp.where(struct == member, single_grad, 0.0) for member in range(2)]
    chosen = jnp.concatenate(chosen, axis=1).reshape(-1, single_grad.shape[2])
    store_tiles(two, core, chosen, 2 * stride_two)


def final_call(samp, place, x_attn, d_query, d_kv, d_gate, weight, act, scale, d_hidden,
               d_cond_gate, single, d_hat, cond_weight, gain):
    groups = samp // 2
    tokens, width = act.shape
    chans = single.shape[1]
    rows = width // samp
    one_rows = 3 * rows
    cond_rows = cond_weight.size // (samp * 2 * TILE_COLS)
    two_rows = rows + 16 * math.ceil(cond_rows / 16)
    vmem = pl.BlockSpec(memory_space=pltpu.VMEM)
    share = tokens // samp
    one = jax.ShapeDtypeStruct((groups, 2 * one_rows, TILE_COLS), jnp.bfloat16)
    two = jax.ShapeDtypeStruct((groups, 2 * (two_rows + share), TILE_COLS), jnp.bfloat16)
    return pl.pallas_call(
        final_kernel,
        in_specs=[pl.BlockSpec(memory_space=pltpu.SMEM)] + [vmem] * 16,
        out_specs=[vmem] * 8,
        out_shape=[
            jax.ShapeDtypeStruct((tokens, width), jnp.float32),
            one, one, two, two,
            jax.ShapeDtypeStruct((8, 3 * width), jnp.float32),
            jax.ShapeDtypeStruct((8, width), jnp.float32),
            jax.ShapeDtypeStruct((1, chans), jnp.float32),
        ],
        scratch_shapes=[pltpu.VMEM((tokens, 3 * width), jnp.bfloat16)],
        compiler_params=pltpu.CompilerParams(vmem_limit_bytes=VMEM_BYTES),
        cost_estimate=spends(20),
        name="final",
    )(place, x_attn, d_query, d_kv, *d_gate, weight, act, scale, *d_hidden,
      *d_cond_gate, single, d_hat, cond_weight, gain)


def tie(*values):
    return lax.optimization_barrier(values)


def flip(value, axis, distance):
    size = lax.axis_size(axis)
    return lax.ppermute(value, axis, [(i, i ^ distance) for i in range(size)])


def halve(value, axis, distance, dim):
    bit = (lax.axis_index(axis) // distance) % 2
    keep = lax.dynamic_index_in_dim(value, bit, dim, keepdims=False)
    give = lax.dynamic_index_in_dim(value, 1 - bit, dim, keepdims=False)
    return add_low(keep, flip(give, axis, distance))


def spread(value, distance, dim):
    other = flip(value, "samp", distance)
    first = (lax.axis_index("samp") // distance) % 2 == 0
    return jnp.stack([jnp.where(first, value, other), jnp.where(first, other, value)], axis=dim)


def add_low(left, right):
    return (left.astype(jnp.float32) + right.astype(jnp.float32)).astype(jnp.bfloat16)


def grad_from_tiles(tiles, rows):
    blocks = tiles.reshape(-1, rows, TILE_COLS)
    return blocks.transpose(1, 0, 2).reshape(rows, -1)


def exchange(value):
    return lax.all_to_all(value, "samp", 0, 0, tiled=True)


def fast_local(
    activations,
    single_cond,
    pair_repr,
    struct_id,
    seq_lengths,
    qkvg_weight,
    query_bias,
    out_weight,
    in_weight,
    down_weight,
    cond_weight,
    cond_bias,
    single_gain,
    pair_gain,
    pair_weight,
    cotangent,
):
    samp = lax.axis_size("samp")
    blks = lax.axis_size("blk")
    tokens, width = activations.shape[1:]
    heads = pair_weight.shape[1]
    head_dim = width // heads
    hidden_units = down_weight.shape[0]
    structs, _, cols, chans = pair_repr.shape
    blk_arg = lax.axis_index("blk").astype(jnp.int32)[None]
    index = lax.axis_index("samp").astype(jnp.int32)
    place = jnp.stack([index % 2, struct_id[0]])
    act = activations[0]

    qkv, gate_val, x_attn, scale_attn, gate_attn = first_call(
        heads, place, single_cond, act, cond_weight, cond_bias[:1], single_gain[:1],
        qkvg_weight, query_bias[None],
    )
    own_id = jnp.where(
        lax.broadcasted_iota(jnp.int32, (8, 128), 1) == index, struct_id[0], 0
    ).astype(jnp.float32)
    qkv, pair_in, own_id = tie(qkv, pair_repr, own_id)
    pair = pair_in.reshape(structs, 2, 2, tokens // 4, cols, chans)
    bias_part, pair_mean, pair_rstd = pair_forward(pair, pair_gain, pair_weight)
    own_id, bias_sent = tie(own_id, bias_part)
    for distance in (1, 2, 4):
        own_id = own_id + flip(own_id, "samp", distance)
    qkv, own_id, bias_sent = tie(exchange(qkv), own_id, bias_sent)
    single = jnp.where(struct_id[0] == 1, single_cond[1], single_cond[0])
    single_hat = norm_rows(single.astype(jnp.float32))
    cond_in = (single_hat * single_gain[1]).astype(jnp.bfloat16)
    bias_row = jnp.concatenate(
        [cond_bias[1, :width], jnp.zeros((width,), jnp.float32), cond_bias[1, width:]]
    )
    cond_trans = nn_dot(cond_in, cond_weight[1]) + bias_row
    own_id = own_id + flip(own_id, "samp", 8)
    bias, kv_far, cond_trans, own_id = tie(
        exchange(bias_sent), flip(qkv[:, head_dim:], "blk", 1), cond_trans, own_id
    )
    ids = own_id[0, :samp].astype(jnp.int32)
    forward_args = (ids, seq_lengths, blk_arg, qkv, kv_far)
    sent_one, *saved_one = attention_forward(0, *forward_args, bias)
    sent_one, bias = tie(sent_one, bias)
    sent_two, *saved_two = attention_forward(1, *forward_args, bias)
    attn_one, sent_two = tie(exchange(sent_one), sent_two)
    middle_args = (
        gate_val, act, gate_attn, cond_trans, cotangent[0], out_weight, in_weight, down_weight
    )
    *middle_one, d_attn_one = middle_call(0, attn_one, *middle_args)
    attn_two, d_attn_one = tie(exchange(sent_two), d_attn_one)
    *middle_two, d_attn_two = middle_call(1, attn_two, *middle_args)
    d_attn_one, d_attn_two, *middle_two = tie(exchange(d_attn_one), d_attn_two, *middle_two)
    both = list(zip(middle_one, middle_two))
    block_out = jnp.concatenate(both[0], axis=0)
    d_hidden, d_cond_gate, d_gate_pre = both[8:]

    backward_args = (ids, blk_arg, qkv, kv_far)
    d_query_one, d_own, d_far, d_bias_one = attention_backward(
        0, *backward_args, d_attn_one, *saved_one, bias, ()
    )
    d_attn_two, d_query_one, d_own, d_far = tie(exchange(d_attn_two), d_query_one, d_own, d_far)
    d_query_two, d_own, d_far, d_bias_two = attention_backward(
        1, *backward_args, d_attn_two, *saved_two, bias, (d_own, d_far)
    )
    d_query = jnp.concatenate([d_query_one, d_query_two], axis=1)
    d_bias = jnp.stack([d_bias_one, d_bias_two], axis=1)
    d_far, d_bias, *operands = tie(d_far, d_bias, *[value for pair in both[1:8] for value in pair])
    operands = list(zip(operands[::2], operands[1::2]))
    early = early_grads(samp, operands, cond_in)
    d_cond_one, d_cond_two = operands[6]
    d_cond_trans = jnp.concatenate([d_cond_one, d_cond_two], axis=0)
    d_in = nt_dot(d_cond_trans, cond_weight[1])
    gain_sums_trans = jnp.sum(d_in * single_hat, axis=0)
    cond_sums_trans = jnp.sum(d_cond_trans.astype(jnp.float32), axis=0)
    d_hat = d_in * single_gain[1]
    d_kv = add_low(d_own, flip(d_far, "blk", 1))
    d_kv, d_query, d_hat, gain_sums_trans, cond_sums_trans, early, d_bias = tie(
        d_kv, exchange(d_query), d_hat, gain_sums_trans, cond_sums_trans, early, d_bias
    )
    early = lax.psum_scatter(
        early.reshape(samp * blks, -1, TILE_COLS), ("samp", "blk"), scatter_dimension=0, tiled=True
    )[0]
    d_kv, d_bias = tie(exchange(d_kv), d_bias)
    d_bias = exchange(d_bias)

    (
        act_grad, keep_one, give_one, keep_two, give_two, cond_sums_attn, query_sums, gain_sums_attn,
    ) = final_call(
        samp, place, x_attn, d_query, d_kv, d_gate_pre, qkvg_weight, act, scale_attn,
        d_hidden, d_cond_gate, single, d_hat, cond_weight[0], single_gain[0][None],
    )
    cube = (samp // 8, 2, 2)
    one = add_low(keep_one, flip(give_one, "samp", 1)).reshape(cube + (2, -1, TILE_COLS))
    two = add_low(keep_two, flip(give_two, "samp", 1)).reshape(cube + (-1, TILE_COLS))
    one, two, d_bias = tie(one, two, d_bias)
    pair_grad, weight_grad_one, gain_grad_one = pair_backward(
        0, pair, d_bias, bias_part, pair_mean, pair_rstd, pair_gain, pair_weight, ()
    )
    one = halve(one, "blk", 1, 3)
    two = halve(two, "samp", 2, 2)
    one, two, d_bias, pair_grad = tie(one, two, d_bias, pair_grad)
    pair_grad, weight_grad_two, gain_grad_two = pair_backward(
        1, pair, d_bias, bias_part, pair_mean, pair_rstd, pair_gain, pair_weight, (pair_grad,)
    )
    shared = 2 * tokens // samp
    alone = two[:, :, -shared:]
    two = two[:, :, :-shared].reshape(two.shape[:2] + (2, -1, TILE_COLS))
    one = halve(one, "samp", 2, 2)
    two = halve(two, "blk", 1, 2)
    alone = add_low(alone, flip(alone, "samp", 4))
    one, two, alone, early, pair_grad, weight_grad_two, gain_grad_two = tie(
        one, two, alone, early, pair_grad, weight_grad_two, gain_grad_two
    )
    small = [
        query_sums[0],
        cond_sums_attn[0, :width], cond_sums_attn[0, 2 * width :],
        cond_sums_trans[:width], cond_sums_trans[2 * width :],
        gain_sums_attn[0], gain_sums_trans,
        gain_grad_one + gain_grad_two, (weight_grad_one + weight_grad_two).reshape(-1),
    ]
    summed = jnp.concatenate(small)
    late = halve(jnp.concatenate([one, two], axis=2), "samp", 4, 1)
    alone = add_low(alone, flip(alone, "samp", 8))
    summed = summed + flip(summed, "samp", 1)
    summed = summed + flip(summed, "blk", 1)
    late, alone, summed = tie(late, alone, summed)
    late = halve(late, "samp", 8, 0).astype(jnp.float32)
    alone = spread(alone, 2, 2)
    summed = summed + flip(summed, "samp", 2)
    late, alone, summed = tie(late, alone, summed)
    alone = spread(alone, 1, 3)
    summed = summed + flip(summed, "samp", 4)
    summed = summed + flip(summed, "samp", 8)
    single_grad = alone.reshape(samp, structs, tokens // samp, -1).transpose(1, 0, 2, 3)
    single_grad = single_grad.reshape(structs, tokens, -1).astype(jnp.float32)
    early = early.astype(jnp.float32)
    small_grads = []
    start = 0
    for like in (query_bias, cond_bias, single_gain, pair_gain, pair_weight):
        small_grads.append(summed[start : start + like.size].reshape(like.shape))
        start += like.size
    query_bias_grad, cond_bias_grad, single_gain_grad, pair_gain_grad, pair_weight_grad = small_grads

    def take(tiles, start, rows, width_out):
        count = rows * width_out // TILE_COLS
        return grad_from_tiles(tiles[start : start + count], rows), start + count

    start = 0
    in_grad, start = take(early, start, width // samp, in_weight.shape[1] // blks)
    down_grad, start = take(early, start, hidden_units // samp, width // blks)
    out_grad, start = take(early, start, width // samp, width // blks)
    cond_rows_dev = cond_weight.shape[1] // samp
    cond_cols_dev = cond_weight.shape[2] // blks
    cond_trans_grad, start = take(early, start, cond_rows_dev, cond_cols_dev)
    qkvg_grad, start = take(late, 0, width // samp, qkvg_weight.shape[1] // blks)
    cond_attn_grad, start = take(late, start, cond_rows_dev, cond_cols_dev)
    return (
        block_out[None],
        act_grad[None],
        single_grad,
        pair_grad.reshape(pair_repr.shape),
        qkvg_grad,
        query_bias_grad,
        out_grad,
        in_grad,
        down_grad,
        jnp.stack([cond_attn_grad, cond_trans_grad]),
        cond_bias_grad,
        single_gain_grad,
        pair_gain_grad,
        pair_weight_grad,
    )


def solution(mesh):
    sizes = dict(mesh.shape)
    program = fast_local if (sizes["samp"], sizes["blk"]) == (16, 2) else local
    return jax.shard_map(
        program,
        mesh=mesh,
        in_specs=(
            P("samp", "blk", None),
            P(None, "blk", None),
            P(None, "blk", "samp", None),
            P("samp"),
            P(),
            P(),
            P(),
            P(),
            P(),
            P(),
            P(),
            P(),
            P(),
            P(),
            P(),
            P("samp", "blk", None),
        ),
        out_specs=(
            P("samp", "blk", None),
            P("samp", "blk", None),
            P(None, "blk", None),
            P(None, "blk", "samp", None),
            P("samp", "blk"),
            P(),
            P("samp", "blk"),
            P("samp", "blk"),
            P("samp", "blk"),
            P(None, "samp", "blk"),
            P(),
            P(),
            P(),
            P(),
        ),
        check_vma=False,
    )
```

```python
import functools
import math

import jax
import jax.numpy as jnp
from jax import lax
from jax.experimental import pallas as pl
from jax.experimental.pallas import tpu as pltpu
from jax.sharding import PartitionSpec as P

EPS = 1e-05
MASKED = -1000000000.0
LOG2E = 1.4426950408889634
LN2 = 0.6931471805599453
VMEM_BYTES = 56 * 1024 * 1024
TILE_COLS = 384


def norm_rows(value):
    center = value - jnp.mean(value, axis=-1, keepdims=True)
    return center * lax.rsqrt(jnp.mean(center * center, axis=-1, keepdims=True) + EPS)


def pick_struct(table, ids):
    expand = (ids.shape[0],) + (1,) * (table.ndim - 1)
    chosen = jnp.broadcast_to(table[0][None], (ids.shape[0],) + table.shape[1:])
    chosen = jnp.where(ids.reshape(expand) == 1, table[1][None], chosen)
    return chosen


def struct_sum(values, ids, structs):
    expand = (ids.shape[0],) + (1,) * (values.ndim - 1)
    return jnp.stack(
        [
            jnp.sum(jnp.where(ids.reshape(expand) == member, values, 0.0), axis=0)
            for member in range(structs)
        ]
    )


def block_length(piece_len):
    return math.gcd(piece_len, 512)


def local(
    activations,
    single_cond,
    pair_repr,
    struct_id,
    seq_lengths,
    qkvg_weight,
    query_bias,
    out_weight,
    in_weight,
    down_weight,
    cond_weight,
    cond_bias,
    single_gain,
    pair_gain,
    pair_weight,
    cotangent,
):
    samples_dev, tok_rows, width = activations.shape
    heads = pair_weight.shape[1]
    head_dim = width // heads
    hidden_units = down_weight.shape[0]
    structs = single_cond.shape[0]
    seq_total = tok_rows * lax.axis_size("blk")
    score_scale = 1.0 / math.sqrt(head_dim)
    zero_index = jnp.zeros((), jnp.int32)
    key_limit = pick_struct(seq_lengths, struct_id)
    single_hat = norm_rows(single_cond.astype(jnp.float32))
    cond_inputs = []
    cond_rows = []
    for sublayer in range(2):
        cond_in = (single_hat * single_gain[sublayer]).astype(jnp.bfloat16)
        bias_row = jnp.concatenate(
            [
                cond_bias[sublayer, :width],
                jnp.zeros((width,), jnp.float32),
                cond_bias[sublayer, width:],
            ]
        )
        cond_pre = (
            jnp.einsum(
                "cti,ij->ctj", cond_in, cond_weight[sublayer], preferred_element_type=jnp.float32
            )
            + bias_row
        )
        cond_inputs.append(cond_in)
        cond_rows.append(pick_struct(cond_pre, struct_id))
    pair_hat, pair_norm_back = jax.vjp(norm_rows, pair_repr.astype(jnp.float32))
    pair_in = (pair_hat * pair_gain).astype(jnp.bfloat16)
    bias_local = jnp.einsum(
        "crkz,zh->crhk", pair_in, pair_weight, preferred_element_type=jnp.float32
    ).astype(jnp.bfloat16)
    bias_all = lax.all_gather(bias_local, "samp", axis=3, tiled=True)
    act_float = activations.astype(jnp.float32)
    act_hat, act_norm_back = jax.vjp(norm_rows, act_float)
    cond_attn = cond_rows[0]
    scale_attn = jax.nn.sigmoid(cond_attn[..., :width])
    gate_attn = jax.nn.sigmoid(cond_attn[..., 2 * width :])
    x_attn = (scale_attn * act_hat + cond_attn[..., width : 2 * width]).astype(jnp.bfloat16)
    proj_bias = jnp.concatenate([query_bias, jnp.zeros((3 * width,), jnp.float32)])
    projected = (
        jnp.einsum("sti,ij->stj", x_attn, qkvg_weight, preferred_element_type=jnp.float32)
        + proj_bias
    )
    query = (
        projected[..., :width].astype(jnp.bfloat16).reshape(samples_dev, tok_rows, heads, head_dim)
    )
    keys_values = projected[..., width : 3 * width].astype(jnp.bfloat16)
    gate_pre = projected[..., 3 * width :]

    def block_scores(sub_kv, offset):
        block_len = sub_kv.shape[1]
        keys_block = sub_kv[..., :width].reshape(samples_dev, block_len, heads, head_dim)
        scores = (
            jnp.einsum("sqhd,skhd->sqhk", query, keys_block, preferred_element_type=jnp.float32)
            * score_scale
        )
        bias_block = lax.dynamic_slice_in_dim(bias_all, offset, block_len, 3)
        scores = scores + pick_struct(bias_block, struct_id).astype(jnp.float32)
        positions = offset + jnp.arange(block_len, dtype=jnp.int32)
        valid = positions[None, :] < key_limit[:, None]
        return jnp.where(valid[:, None, None, :], scores, MASKED)

    def forward_fold(state, block_kv):
        block_len = block_length(block_kv.shape[1])
        count = block_kv.shape[1] // block_len

        def forward_step(carry, index):
            row_peak, row_total, row_acc = carry
            sub_offset = index * block_len
            sub_kv = lax.dynamic_slice_in_dim(block_kv, index * block_len, block_len, 1)
            scores = block_scores(sub_kv, sub_offset)
            values_block = sub_kv[..., width:].reshape(samples_dev, block_len, heads, head_dim)
            new_peak = jnp.maximum(row_peak, jnp.max(scores, axis=-1))
            rescale = jnp.exp(row_peak - new_peak)
            weights = jnp.exp(scores - new_peak[..., None])
            row_total = row_total * rescale + jnp.sum(weights, axis=-1)
            row_acc = row_acc * rescale[..., None] + jnp.einsum(
                "sqhk,skhd->sqhd",
                weights.astype(jnp.bfloat16),
                values_block,
                preferred_element_type=jnp.float32,
            )
            return ((new_peak, row_total, row_acc), None)

        result, ignored = lax.scan(
            jax.checkpoint(forward_step), state, jnp.arange(count, dtype=jnp.int32)
        )
        return result

    stats_shape = (samples_dev, tok_rows, heads)
    forward_init = (
        jnp.full(stats_shape, -1e30, jnp.float32),
        jnp.zeros(stats_shape, jnp.float32),
        jnp.zeros((samples_dev, tok_rows, heads, head_dim), jnp.float32),
    )
    row_peak, row_total, row_acc = forward_fold(
        forward_init, lax.all_gather(keys_values, "blk", axis=1, tiled=True)
    )
    attn4 = row_acc / row_total[..., None]
    log_sum = row_peak + jnp.log(row_total)
    attn = attn4.reshape(samples_dev, tok_rows, width)
    gate_val = jax.nn.sigmoid(gate_pre)
    mixed = (gate_val * attn).astype(jnp.bfloat16)
    att_out = jnp.einsum("sti,ij->stj", mixed, out_weight, preferred_element_type=jnp.float32)
    hidden_state = act_float + gate_attn * att_out
    cond_trans = cond_rows[1]
    scale_trans = jax.nn.sigmoid(cond_trans[..., :width])
    gate_trans = jax.nn.sigmoid(cond_trans[..., 2 * width :])
    hidden_hat, hidden_norm_back = jax.vjp(norm_rows, hidden_state)
    x_trans = (scale_trans * hidden_hat + cond_trans[..., width : 2 * width]).astype(jnp.bfloat16)
    up_proj = jnp.einsum("sti,ij->stj", x_trans, in_weight, preferred_element_type=jnp.float32)
    up_gate = up_proj[..., :hidden_units]
    up_lin = up_proj[..., hidden_units:]
    sig_gate = jax.nn.sigmoid(up_gate)
    silu_gate = up_gate * sig_gate
    hidden_act = (silu_gate * up_lin).astype(jnp.bfloat16)
    trans = jnp.einsum("stf,fd->std", hidden_act, down_weight, preferred_element_type=jnp.float32)
    block_out = (hidden_state + gate_trans * trans).astype(jnp.bfloat16)
    d_out = cotangent.astype(jnp.float32)
    d_trans = (gate_trans * d_out).astype(jnp.bfloat16)
    grad_down = jnp.einsum("stf,std->fd", hidden_act, d_trans, preferred_element_type=jnp.float32)
    d_hid = jnp.einsum("std,fd->stf", d_trans, down_weight, preferred_element_type=jnp.float32)
    silu_slope = sig_gate * (1.0 + up_gate * (1.0 - sig_gate))
    d_up = jnp.concatenate([d_hid * up_lin * silu_slope, d_hid * silu_gate], axis=-1).astype(
        jnp.bfloat16
    )
    grad_in = jnp.einsum("sti,stj->ij", x_trans, d_up, preferred_element_type=jnp.float32)
    d_xt = jnp.einsum("stj,ij->sti", d_up, in_weight, preferred_element_type=jnp.float32)
    d_hidden = d_out + hidden_norm_back(d_xt * scale_trans)[0]
    d_cond_trans = jnp.concatenate(
        [
            d_xt * hidden_hat * scale_trans * (1.0 - scale_trans),
            d_xt,
            d_out * trans * gate_trans * (1.0 - gate_trans),
        ],
        axis=-1,
    )
    d_att = (gate_attn * d_hidden).astype(jnp.bfloat16)
    grad_out = jnp.einsum("sti,stj->ij", mixed, d_att, preferred_element_type=jnp.float32)
    d_mixed = jnp.einsum("stj,ij->sti", d_att, out_weight, preferred_element_type=jnp.float32)
    d_attn = (gate_val * d_mixed).astype(jnp.bfloat16)
    d_gate_pre = d_mixed * attn * gate_val * (1.0 - gate_val)
    d_attn4 = d_attn.reshape(samples_dev, tok_rows, heads, head_dim)
    row_delta = jnp.sum(d_attn4.astype(jnp.float32) * attn4, axis=-1)

    def backward_fold(state, block_kv):
        block_len = block_length(block_kv.shape[1])
        count = block_kv.shape[1] // block_len

        def backward_step(carry, index):
            d_query, d_kv, d_bias = carry
            sub_offset = index * block_len
            sub_kv = lax.dynamic_slice_in_dim(block_kv, index * block_len, block_len, 1)
            keys_block = sub_kv[..., :width].reshape(samples_dev, block_len, heads, head_dim)
            values_block = sub_kv[..., width:].reshape(samples_dev, block_len, heads, head_dim)
            scores = block_scores(sub_kv, sub_offset)
            attn_probs = jnp.exp(scores - log_sum[..., None])
            d_probs = jnp.einsum(
                "sqhd,skhd->sqhk", d_attn4, values_block, preferred_element_type=jnp.float32
            )
            d_scores = (attn_probs * (d_probs - row_delta[..., None])).astype(jnp.bfloat16)
            d_query = (
                d_query
                + jnp.einsum(
                    "sqhk,skhd->sqhd", d_scores, keys_block, preferred_element_type=jnp.float32
                )
                * score_scale
            )
            d_keys = (
                jnp.einsum("sqhk,sqhd->skhd", d_scores, query, preferred_element_type=jnp.float32)
                * score_scale
            )
            d_values = jnp.einsum(
                "sqhk,sqhd->skhd",
                attn_probs.astype(jnp.bfloat16),
                d_attn4,
                preferred_element_type=jnp.float32,
            )
            d_new = jnp.concatenate(
                [
                    d_keys.reshape(samples_dev, block_len, width),
                    d_values.reshape(samples_dev, block_len, width),
                ],
                axis=-1,
            )
            d_kv = lax.dynamic_update_slice(d_kv, d_new, (zero_index, sub_offset, zero_index))
            bias_part = struct_sum(d_scores.astype(jnp.float32), struct_id, structs)
            d_bias = lax.dynamic_update_slice(
                d_bias, bias_part, (zero_index, zero_index, zero_index, sub_offset)
            )
            return ((d_query, d_kv, d_bias), None)

        result, ignored = lax.scan(
            jax.checkpoint(backward_step), state, jnp.arange(count, dtype=jnp.int32)
        )
        return result

    backward_init = (
        jnp.zeros((samples_dev, tok_rows, heads, head_dim), jnp.float32),
        jnp.zeros((samples_dev, seq_total, 2 * width), jnp.float32),
        jnp.zeros((structs, tok_rows, heads, seq_total), jnp.float32),
    )
    d_query, d_kv, d_bias = backward_fold(
        backward_init, lax.all_gather(keys_values, "blk", axis=1, tiled=True)
    )
    d_kv_own = lax.psum_scatter(
        d_kv.astype(jnp.bfloat16), "blk", scatter_dimension=1, tiled=True
    ).astype(jnp.float32)
    d_proj = jnp.concatenate(
        [d_query.reshape(samples_dev, tok_rows, width), d_kv_own, d_gate_pre], axis=-1
    ).astype(jnp.bfloat16)
    grad_qkvg = jnp.einsum("sti,stj->ij", x_attn, d_proj, preferred_element_type=jnp.float32)
    grad_query_bias = jnp.sum(d_proj[..., :width].astype(jnp.float32), axis=(0, 1))
    d_xa = jnp.einsum("stj,ij->sti", d_proj, qkvg_weight, preferred_element_type=jnp.float32)
    act_grad = d_hidden + act_norm_back(d_xa * scale_attn)[0]
    d_cond_attn = jnp.concatenate(
        [
            d_xa * act_hat * scale_attn * (1.0 - scale_attn),
            d_xa,
            d_hidden * att_out * gate_attn * (1.0 - gate_attn),
        ],
        axis=-1,
    )
    d_cond_all = jnp.concatenate(
        [struct_sum(d_cond_attn, struct_id, structs), struct_sum(d_cond_trans, struct_id, structs)],
        axis=-1,
    )
    bias_sum, cond_sum = (
        lax.psum_scatter(
            d_bias.astype(jnp.bfloat16), "samp", scatter_dimension=3, tiled=True
        ).astype(jnp.float32),
        lax.psum_scatter(
            d_cond_all.astype(jnp.bfloat16), "samp", scatter_dimension=1, tiled=True
        ).astype(jnp.float32),
    )
    bias_round = bias_sum.astype(jnp.bfloat16)
    grad_pair_weight = jnp.einsum(
        "crkz,crhk->zh", pair_in, bias_round, preferred_element_type=jnp.float32
    )
    d_pair_in = jnp.einsum(
        "crhk,zh->crkz", bias_round, pair_weight, preferred_element_type=jnp.float32
    )
    grad_pair_gain = jnp.sum(d_pair_in * pair_hat, axis=(0, 1, 2))
    pair_grad = pair_norm_back(d_pair_in * pair_gain)[0]
    slice_len = cond_sum.shape[1]
    slice_start = lax.axis_index("samp") * slice_len
    single_part = lax.dynamic_slice_in_dim(single_cond, slice_start, slice_len, 1).astype(
        jnp.float32
    )
    part_hat, part_norm_back = jax.vjp(norm_rows, single_part)
    cond_round = cond_sum.astype(jnp.bfloat16)
    d_part_hat = jnp.zeros_like(part_hat)
    cond_grads = []
    cond_bias_grads = []
    gain_grads = []
    for sublayer in range(2):
        d_layer = cond_round[..., sublayer * 3 * width : (sublayer + 1) * 3 * width]
        part_in = lax.dynamic_slice_in_dim(cond_inputs[sublayer], slice_start, slice_len, 1)
        cond_grads.append(
            jnp.einsum("cti,ctj->ij", part_in, d_layer, preferred_element_type=jnp.float32)
        )
        layer_sums = jnp.sum(d_layer.astype(jnp.float32), axis=(0, 1))
        cond_bias_grads.append(jnp.concatenate([layer_sums[:width], layer_sums[2 * width :]]))
        d_in = jnp.einsum(
            "ctj,ij->cti", d_layer, cond_weight[sublayer], preferred_element_type=jnp.float32
        )
        gain_grads.append(jnp.sum(d_in * part_hat, axis=(0, 1)))
        d_part_hat = d_part_hat + d_in * single_gain[sublayer]
    single_part_grad = part_norm_back(d_part_hat)[0]
    single_grad = lax.all_gather(single_part_grad, "samp", axis=1, tiled=True)
    grad_cond = jnp.stack(cond_grads)
    part_qkvg, part_out, part_in_w, part_down, part_cond = (
        lax.psum_scatter(
            grad_qkvg.astype(jnp.bfloat16), "blk", scatter_dimension=1, tiled=True
        ).astype(jnp.float32),
        lax.psum_scatter(
            grad_out.astype(jnp.bfloat16), "blk", scatter_dimension=1, tiled=True
        ).astype(jnp.float32),
        lax.psum_scatter(
            grad_in.astype(jnp.bfloat16), "blk", scatter_dimension=1, tiled=True
        ).astype(jnp.float32),
        lax.psum_scatter(
            grad_down.astype(jnp.bfloat16), "blk", scatter_dimension=1, tiled=True
        ).astype(jnp.float32),
        lax.psum_scatter(
            grad_cond.astype(jnp.bfloat16), "blk", scatter_dimension=2, tiled=True
        ).astype(jnp.float32),
    )
    qkvg_grad, out_grad, in_grad, down_grad, cond_grad = (
        lax.psum_scatter(
            part_qkvg.astype(jnp.bfloat16), "samp", scatter_dimension=0, tiled=True
        ).astype(jnp.float32),
        lax.psum_scatter(
            part_out.astype(jnp.bfloat16), "samp", scatter_dimension=0, tiled=True
        ).astype(jnp.float32),
        lax.psum_scatter(
            part_in_w.astype(jnp.bfloat16), "samp", scatter_dimension=0, tiled=True
        ).astype(jnp.float32),
        lax.psum_scatter(
            part_down.astype(jnp.bfloat16), "samp", scatter_dimension=0, tiled=True
        ).astype(jnp.float32),
        lax.psum_scatter(
            part_cond.astype(jnp.bfloat16), "samp", scatter_dimension=1, tiled=True
        ).astype(jnp.float32),
    )
    query_bias_grad, cond_bias_grad, single_gain_grad, pair_gain_grad, pair_weight_grad = lax.psum(
        (
            grad_query_bias,
            jnp.stack(cond_bias_grads),
            jnp.stack(gain_grads),
            grad_pair_gain,
            grad_pair_weight,
        ),
        ("samp", "blk"),
    )
    return (
        block_out,
        act_grad,
        single_grad,
        pair_grad,
        qkvg_grad,
        query_bias_grad,
        out_grad,
        in_grad,
        down_grad,
        cond_grad,
        cond_bias_grad,
        single_gain_grad,
        pair_gain_grad,
        pair_weight_grad,
    )


FORWARD_GROUP = 4
BACKWARD_GROUP = 4
KEY_CHUNK = 128


def nt_dot(left, right):
    return lax.dot_general(
        left, right, (((1,), (1,)), ((), ())), preferred_element_type=jnp.float32
    )


def nn_dot(left, right):
    return lax.dot_general(
        left, right, (((1,), (0,)), ((), ())), preferred_element_type=jnp.float32
    )


def tn_dot(left, right):
    return lax.dot_general(
        left, right, (((0,), (0,)), ((), ())), preferred_element_type=jnp.float32
    )


def split_two(value):
    high = value.astype(jnp.bfloat16)
    return high, (value - high.astype(jnp.float32)).astype(jnp.bfloat16)


def spends(micros):
    return pl.CostEstimate(
        flops=int(micros * 1e9), bytes_accessed=int(micros * 3e6), transcendentals=0
    )


def pair_rows(pair_ref):
    quarters, rows, cols, chans = pair_ref.shape[2:]
    both = jnp.concatenate([pair_ref[0, 0, quarter] for quarter in range(quarters)], axis=1)
    return both.reshape(rows * quarters * cols, chans)


def pair_forward_kernel(pair_ref, coef_ref, coef_sum_ref, bias_ref, mean_ref, rstd_ref):
    heads = bias_ref.shape[0]
    rows, lanes = mean_ref.shape[2:]
    chans = pair_ref.shape[5]
    cells = pair_rows(pair_ref)
    wide = cells.astype(jnp.float32)
    square_high, square_low = split_two(wide * wide)
    sums = nt_dot(coef_ref[...], jnp.concatenate([cells, square_high], axis=1))
    low_sums = nt_dot(jnp.ones((16, chans), jnp.bfloat16), square_low)
    raw = sums[:heads] + sums[heads : 2 * heads]
    total = sums[2 * heads : 2 * heads + 1]
    squares = sums[2 * heads + 8 : 2 * heads + 9] + low_sums[0:1]
    total_high = total.astype(jnp.bfloat16).astype(jnp.float32)
    total_low = total - total_high
    spread = squares * chans - total_high * total_high
    spread = spread - 2.0 * total_high * total_low - total_low * total_low
    rstd = lax.rsqrt(jnp.maximum(spread, 0.0) * (1.0 / (chans * chans)) + EPS)
    mean = total * (1.0 / chans)
    bias = (raw - coef_sum_ref[...] * mean) * (rstd * LOG2E)
    bias_ref[:, 0, 0] = bias.reshape(heads, rows, lanes).astype(jnp.bfloat16)
    mean_ref[0, 0] = mean.reshape(rows, lanes)
    rstd_ref[0, 0] = rstd.reshape(rows, lanes)


def pair_forward(pair, pair_gain, pair_weight):
    structs, halves, quarters, rows, cols, chans = pair.shape
    heads = pair_weight.shape[1]
    lanes = quarters * cols
    step = 32
    gained = pair_weight.astype(jnp.float32) * pair_gain[:, None]
    high, low = split_two(gained.T)
    ones_row = jnp.zeros((8, chans), jnp.bfloat16).at[0].set(1.0)
    blank = jnp.zeros((8, chans), jnp.bfloat16)
    coef = jnp.concatenate(
        [
            jnp.concatenate([high, low, ones_row, blank], axis=0),
            jnp.concatenate([jnp.zeros((2 * heads, chans), jnp.bfloat16), blank, ones_row], axis=0),
        ],
        axis=1,
    )
    coef_sum = jnp.sum(gained, axis=0)[:, None]
    return pl.pallas_call(
        pair_forward_kernel,
        grid=(halves, structs, rows // step),
        in_specs=[
            pl.BlockSpec((1, 1, quarters, step, cols, chans), lambda h, c, r: (c, h, 0, r, 0, 0)),
            pl.BlockSpec(coef.shape, lambda h, c, r: (0, 0)),
            pl.BlockSpec(coef_sum.shape, lambda h, c, r: (0, 0)),
        ],
        out_specs=[
            pl.BlockSpec((heads, 1, 1, step, lanes), lambda h, c, r: (0, h, c, r, 0)),
            pl.BlockSpec((1, 1, step, lanes), lambda h, c, r: (h, c, r, 0)),
            pl.BlockSpec((1, 1, step, lanes), lambda h, c, r: (h, c, r, 0)),
        ],
        out_shape=[
            jax.ShapeDtypeStruct((heads, halves, structs, rows, lanes), jnp.bfloat16),
            jax.ShapeDtypeStruct((halves, structs, rows, lanes), jnp.float32),
            jax.ShapeDtypeStruct((halves, structs, rows, lanes), jnp.float32),
        ],
        compiler_params=pltpu.CompilerParams(vmem_limit_bytes=VMEM_BYTES),
        cost_estimate=spends(20),
        name="pair_forward",
    )(pair, coef, coef_sum)


def pair_backward_kernel(
    pair_ref, d_bias_ref, bias_ref, mean_ref, rstd_ref, coef_ref, coef_sum_ref, *refs
):
    grad_ref, inner_ref, offset_ref = refs[-3:]
    heads = d_bias_ref.shape[0]
    rows, lanes = mean_ref.shape[2:]
    quarters, _, cols, chans = pair_ref.shape[2:]
    count = rows * lanes
    cells = pair_rows(pair_ref)
    d_bias = d_bias_ref[:, 0].astype(jnp.float32)
    bias = bias_ref[:, 0, 0].astype(jnp.float32)
    mean = mean_ref[0]
    rstd = rstd_ref[0]
    g_mean = jnp.sum(d_bias * coef_sum_ref[...], axis=0, keepdims=True) * (1.0 / chans)
    gy_mean = jnp.sum(d_bias * bias, axis=0, keepdims=True) * (LN2 / chans)
    slope = rstd * rstd * gy_mean
    shift = mean * slope - rstd * g_mean
    scaled = d_bias * rstd

    @pl.when((pl.program_id(0) == 0) & (pl.program_id(1) == 0))
    def _():
        inner_ref[...] = jnp.zeros_like(inner_ref)
        offset_ref[...] = jnp.zeros_like(offset_ref)

    offset_ref[...] += jnp.sum(scaled * mean, axis=1)
    scaled_high, scaled_low = split_two(scaled.reshape(heads, count))
    ends = jnp.concatenate([shift, slope], axis=0).reshape(2, count)
    ends_high, ends_low = split_two(ends)
    blank = jnp.zeros((12, count), jnp.bfloat16)
    inner_ref[...] += nn_dot(jnp.concatenate([scaled_high, scaled_low], axis=0), cells)
    factors = jnp.concatenate([scaled_high, scaled_low, ends_high, ends_low, blank], axis=0)
    spread = tn_dot(factors, coef_ref[...])
    grad = spread[:, :chans] - cells.astype(jnp.float32) * spread[:, chans:]
    grad = grad.reshape(rows, lanes, chans)
    for quarter in range(quarters):
        grad_ref[0, 0, quarter] = grad[:, quarter * cols : (quarter + 1) * cols]


def pair_backward(half, pair, d_bias, bias, mean, rstd, pair_gain, pair_weight, partial):
    structs, _, quarters, half_rows, cols, chans = pair.shape
    heads = pair_weight.shape[1]
    lanes = quarters * cols
    step = 32
    gained = (pair_weight.astype(jnp.float32) * pair_gain[:, None]).T
    coef_sum = jnp.sum(gained, axis=1)[:, None, None]
    ones = jnp.ones((1, chans), jnp.bfloat16)
    zeros = jnp.zeros((1, chans), jnp.bfloat16)
    rows = gained.astype(jnp.bfloat16)
    left = jnp.concatenate([rows, rows, ones, zeros, ones, zeros], axis=0)
    right = jnp.concatenate(
        [jnp.zeros((2 * heads, chans), jnp.bfloat16), zeros, ones, zeros, ones], axis=0
    )
    coef = jnp.concatenate([left, right], axis=1)
    coef = jnp.concatenate([coef, jnp.zeros((12, 2 * chans), jnp.bfloat16)], axis=0)
    grad, inner, offset = pl.pallas_call(
        pair_backward_kernel,
        grid=(structs, half_rows // step),
        in_specs=[
            pl.BlockSpec((1, 1, quarters, step, cols, chans), lambda c, r: (c, half, 0, r, 0, 0)),
            pl.BlockSpec((heads, 1, step, lanes), lambda c, r: (0, c, r, 0)),
            pl.BlockSpec((heads, 1, 1, step, lanes), lambda c, r: (0, half, c, r, 0)),
            pl.BlockSpec((1, 1, step, lanes), lambda c, r: (half, c, r, 0)),
            pl.BlockSpec((1, 1, step, lanes), lambda c, r: (half, c, r, 0)),
            pl.BlockSpec(coef.shape, lambda c, r: (0, 0)),
            pl.BlockSpec(coef_sum.shape, lambda c, r: (0, 0, 0)),
        ]
        + [pl.BlockSpec(memory_space=pl.ANY)] * len(partial),
        out_specs=[
            pl.BlockSpec((1, 1, quarters, step, cols, chans), lambda c, r: (c, half, 0, r, 0, 0)),
            pl.BlockSpec((2 * heads, chans), lambda c, r: (0, 0)),
            pl.BlockSpec((heads, lanes), lambda c, r: (0, 0)),
        ],
        input_output_aliases={7: 0} if partial else {},
        out_shape=[
            jax.ShapeDtypeStruct(pair.shape, jnp.float32),
            jax.ShapeDtypeStruct((2 * heads, chans), jnp.float32),
            jax.ShapeDtypeStruct((heads, lanes), jnp.float32),
        ],
        compiler_params=pltpu.CompilerParams(vmem_limit_bytes=VMEM_BYTES),
        cost_estimate=spends(13),
        name="pair_backward",
    )(pair, d_bias, bias, mean, rstd, coef, coef_sum, *partial)
    moment = inner[:heads] + inner[heads:] - jnp.sum(offset, axis=1, keepdims=True)
    return grad, moment


def attention_forward_kernel(
    ids_ref, limits_ref, blk_ref,
    query_ref, key_own_ref, key_far_ref, value_own_ref, value_far_ref, bias_ref,
    sent_ref, attn_ref, inverse_ref, weights_ref,
    table_ref,
):
    sources, _, structs, _, lanes = bias_ref.shape
    tile = query_ref.shape[2]
    cols = lanes // 2
    sample = pl.program_id(0)
    near = sources // 2

    @pl.when(sample == 0)
    def _():
        for struct in range(structs):
            limit = limits_ref[struct]
            for source in range(sources):
                part = bias_ref[source, 0, struct].astype(jnp.float32).T
                part = jnp.concatenate([part[:cols], part[cols:]], axis=1)
                position = (
                    lax.rem(source // near + blk_ref[0], 2) * (near * cols) + (source % near) * cols
                )
                position = pl.multiple_of(position, cols)
                keys = source * cols + lax.broadcasted_iota(jnp.int32, part.shape, 0)
                table_ref[struct, pl.ds(position, cols)] = jnp.where(
                    keys < limit, part, -1e30
                ).astype(jnp.bfloat16)

    head_dim = query_ref.shape[1]
    for member in range(query_ref.shape[0]):
        struct = ids_ref[sample * query_ref.shape[0] + member]
        keys_t = jnp.concatenate([key_own_ref[member], key_far_ref[member]], axis=1)
        keys = keys_t.astype(jnp.float32).T.astype(jnp.bfloat16)
        values_t = jnp.concatenate([value_own_ref[member], value_far_ref[member]], axis=1)
        values_t = jnp.concatenate(
            [values_t, jnp.ones((16, values_t.shape[1]), jnp.bfloat16)], axis=0
        )
        query = query_ref[member]
        scores = []
        peak = None
        for start in range(0, keys.shape[0], KEY_CHUNK):
            part = nn_dot(keys[start : start + KEY_CHUNK], query)
            part = part + table_ref[struct, start : start + KEY_CHUNK].astype(jnp.float32)
            part_peak = jnp.max(part.reshape(-1, 8, tile), axis=0)
            peak = part_peak if peak is None else jnp.maximum(peak, part_peak)
            scores.append(part)
        peak = jnp.max(peak, axis=0, keepdims=True)
        summed = 0.0
        for index, part in enumerate(scores):
            span = slice(index * KEY_CHUNK, (index + 1) * KEY_CHUNK)
            weights = jnp.exp2(part - peak).astype(jnp.bfloat16)
            weights_ref[member, span] = weights
            summed = summed + nn_dot(values_t[:, span], weights)
        inverse = 1.0 / summed[head_dim : head_dim + 1]
        attn = summed[:head_dim] * inverse
        attn_ref[member] = attn
        sent_ref[member] = attn.astype(jnp.bfloat16)
        inverse_ref[member] = inverse


def attention_forward(half, ids, limits, blk, qkv, kv_far, bias):
    samples, triple, tokens = qkv.shape
    head_dim = triple // 3
    structs = bias.shape[2]
    tile = tokens // 2
    keys = 2 * tokens
    group = FORWARD_GROUP
    part = (group, head_dim, tokens)
    tile_part = (group, head_dim, tile)
    grid_spec = pltpu.PrefetchScalarGridSpec(
        num_scalar_prefetch=3,
        grid=(samples // group,),
        in_specs=[
            pl.BlockSpec(tile_part, lambda n, *_: (n, 0, half)),
            pl.BlockSpec(part, lambda n, *_: (n, 1, 0)),
            pl.BlockSpec(part, lambda n, *_: (n, 0, 0)),
            pl.BlockSpec(part, lambda n, *_: (n, 2, 0)),
            pl.BlockSpec(part, lambda n, *_: (n, 1, 0)),
            pl.BlockSpec(
                (bias.shape[0], 1) + bias.shape[2:], lambda n, *_: (0, half, 0, 0, 0)
            ),
        ],
        out_specs=[
            pl.BlockSpec(tile_part, lambda n, *_: (n, 0, 0)),
            pl.BlockSpec(tile_part, lambda n, *_: (n, 0, 0)),
            pl.BlockSpec((group, 1, tile), lambda n, *_: (n, 0, 0)),
            pl.BlockSpec((group, keys, tile), lambda n, *_: (n, 0, 0)),
        ],
        scratch_shapes=[pltpu.VMEM((structs, keys, tile), jnp.bfloat16)],
    )
    return pl.pallas_call(
        attention_forward_kernel,
        grid_spec=grid_spec,
        out_shape=[
            jax.ShapeDtypeStruct((samples, head_dim, tile), jnp.bfloat16),
            jax.ShapeDtypeStruct((samples, head_dim, tile), jnp.float32),
            jax.ShapeDtypeStruct((samples, 1, tile), jnp.float32),
            jax.ShapeDtypeStruct((samples, keys, tile), jnp.bfloat16),
        ],
        compiler_params=pltpu.CompilerParams(vmem_limit_bytes=VMEM_BYTES),
        cost_estimate=spends(14),
        name="attention_forward",
    )(ids, limits, blk, qkv, qkv, kv_far, qkv, kv_far, bias)


def attention_backward_kernel(
    ids_ref, blk_ref,
    query_ref, key_own_ref, key_far_ref, value_own_ref, value_far_ref,
    d_attn_ref, attn_ref, inverse_ref, weights_ref, *refs, score_scale,
):
    d_query_ref, d_own_ref, d_far_ref, d_bias_ref, total_ref = refs[-5:]
    sources, structs, _, lanes = d_bias_ref.shape
    cols = lanes // 2
    sample = pl.program_id(0)
    near = sources // 2
    group, head_dim, tile = query_ref.shape
    tokens = key_own_ref.shape[2]

    @pl.when(sample == 0)
    def _():
        total_ref[...] = jnp.zeros_like(total_ref)

    tail = jnp.zeros((14, tile), jnp.bfloat16)
    for index in range(group):
        struct = ids_ref[sample * group + index]
        keys_t = jnp.concatenate([key_own_ref[index], key_far_ref[index]], axis=1)
        values_t = jnp.concatenate([value_own_ref[index], value_far_ref[index]], axis=1)
        values_t = jnp.concatenate(
            [values_t, jnp.ones((16, values_t.shape[1]), jnp.bfloat16)], axis=0
        )
        values = turned(values_t)
        inverse = inverse_ref[index]
        d_attn = d_attn_ref[index].astype(jnp.float32)
        delta = jnp.sum(d_attn * attn_ref[index], axis=0, keepdims=True)
        d_attn = (d_attn * inverse).astype(jnp.bfloat16)
        delta_high, delta_low = split_two(-delta * inverse)
        d_probs = nn_dot(values, jnp.concatenate([d_attn, delta_high, delta_low, tail], axis=0))
        weights = weights_ref[index]
        d_scores = weights.astype(jnp.float32) * d_probs
        total_ref[struct] += d_scores
        d_scores = d_scores.astype(jnp.bfloat16)
        d_values = nn_dot(weights, turned(d_attn)).T
        d_keys = nn_dot(d_scores, turned(query_ref[index])).T * LN2
        d_query_ref[index] = (nn_dot(keys_t, d_scores) * score_scale).astype(jnp.bfloat16)
        for place, value in ((slice(0, head_dim), d_keys), (slice(head_dim, None), d_values)):
            own, far = value[:, :tokens], value[:, tokens:]
            if len(refs) > 5:
                own = own + refs[0][index, place].astype(jnp.float32)
                far = far + refs[1][index, place].astype(jnp.float32)
            d_own_ref[index, place] = own.astype(jnp.bfloat16)
            d_far_ref[index, place] = far.astype(jnp.bfloat16)

    @pl.when(sample == pl.num_programs(0) - 1)
    def _():
        for member in range(structs):
            for source in range(sources):
                position = (
                    lax.rem(source // near + blk_ref[0], 2) * (near * cols) + (source % near) * cols
                )
                position = pl.multiple_of(position, cols)
                part = total_ref[member, pl.ds(position, cols)]
                part = jnp.concatenate([part[:, : tile // 2], part[:, tile // 2 :]], axis=0)
                d_bias_ref[source, member] = part.T.astype(jnp.bfloat16)


def attention_backward(half, ids, blk, qkv, kv_far, d_attn, attn, inverse, weights, bias, partial):
    samples, triple, tokens = qkv.shape
    head_dim = triple // 3
    keys, tile = weights.shape[1:]
    bias_shape = bias.shape[:1] + bias.shape[2:]
    structs = bias.shape[2]
    group = BACKWARD_GROUP
    part = (group, head_dim, tokens)
    tile_part = pl.BlockSpec((group, head_dim, tile), lambda n, *_: (n, 0, 0))
    pair_part = pl.BlockSpec((group, 2 * head_dim, tokens), lambda n, *_: (n, 0, 0))
    grid_spec = pltpu.PrefetchScalarGridSpec(
        num_scalar_prefetch=2,
        grid=(samples // group,),
        in_specs=[
            pl.BlockSpec((group, head_dim, tile), lambda n, *_: (n, 0, half)),
            pl.BlockSpec(part, lambda n, *_: (n, 1, 0)),
            pl.BlockSpec(part, lambda n, *_: (n, 0, 0)),
            pl.BlockSpec(part, lambda n, *_: (n, 2, 0)),
            pl.BlockSpec(part, lambda n, *_: (n, 1, 0)),
            tile_part,
            tile_part,
            pl.BlockSpec((group, 1, tile), lambda n, *_: (n, 0, 0)),
            pl.BlockSpec((group, keys, tile), lambda n, *_: (n, 0, 0)),
        ]
        + [pair_part] * len(partial),
        out_specs=[
            tile_part, pair_part, pair_part, pl.BlockSpec(bias_shape, lambda n, *_: (0, 0, 0, 0))
        ],
        scratch_shapes=[pltpu.VMEM((structs, keys, tile), jnp.float32)],
    )
    pair_shape = jax.ShapeDtypeStruct((samples, 2 * head_dim, tokens), jnp.bfloat16)
    return pl.pallas_call(
        functools.partial(attention_backward_kernel, score_scale=1.0 / math.sqrt(head_dim)),
        grid_spec=grid_spec,
        out_shape=[
            jax.ShapeDtypeStruct((samples, head_dim, tile), jnp.bfloat16),
            pair_shape,
            pair_shape,
            jax.ShapeDtypeStruct(bias_shape, jnp.bfloat16),
        ],
        compiler_params=pltpu.CompilerParams(vmem_limit_bytes=VMEM_BYTES),
        cost_estimate=spends(13),
        name="attention_backward",
    )(ids, blk, qkv, qkv, kv_far, qkv, kv_far, d_attn, attn, inverse, weights, *partial)


def turned(value):
    return value.astype(jnp.float32).T.astype(jnp.bfloat16)


def store_tiles(out_refs, core, grad, start):
    groups = out_refs[0].shape[0]
    rows = grad.reshape(groups, 2, -1, grad.shape[1]).astype(jnp.bfloat16)
    span = slice(start, start + rows.shape[2])
    for mine in range(2):

        @pl.when(core == mine)
        def _():
            out_refs[0][:, span] = rows[:, mine]
            out_refs[1][:, span] = rows[:, 1 - mine]


def cond_tiles(out_refs, core, cond_t, d_cond_ref, place, stride):
    tiles = 2 * out_refs[0].shape[0]
    rows = cond_t.shape[0] // tiles
    per_blk = d_cond_ref.shape[1] // (2 * TILE_COLS)
    blank = jnp.zeros((tiles, -(per_blk * rows) % 16, TILE_COLS), jnp.float32)
    for blk in range(2):
        parts = []
        for chunk in range(per_blk):
            start = (blk * per_blk + chunk) * TILE_COLS
            grad = nn_dot(cond_t, d_cond_ref[:, start : start + TILE_COLS])
            parts.append(grad.reshape(tiles, rows, TILE_COLS))
        grad = jnp.concatenate(parts + [blank], axis=1).reshape(-1, TILE_COLS)
        store_tiles(out_refs, core, grad, blk * stride + place)


def early_grads_kernel(place_ref, *refs):
    core = place_ref[0]
    out_refs = refs[-2:]
    pairs = [refs[2 * index : 2 * index + 2] for index in range(7)]
    x_refs, d_up_refs, hidden_refs, d_trans_refs, mixed_refs, d_att_refs, d_cond_refs = pairs
    cond_ref = refs[14]
    place = 0
    tiles = 2 * out_refs[0].shape[0]
    stride = out_refs[0].shape[1] // 2
    for left, right_refs in (
        (turned(rows_of(x_refs)), d_up_refs),
        (turned(rows_of(hidden_refs)), d_trans_refs),
        (jnp.concatenate([mixed_refs[0][...], mixed_refs[1][...]], axis=1), d_att_refs),
    ):
        rows = left.shape[0] // tiles
        per_blk = right_refs[0].shape[1] // (2 * TILE_COLS)
        for chunk in range(2 * per_blk):
            span = slice(chunk * TILE_COLS, (chunk + 1) * TILE_COLS)
            right = jnp.concatenate([right_refs[0][:, span], right_refs[1][:, span]], axis=0)
            start = chunk // per_blk * stride + place + chunk % per_blk * rows
            store_tiles(out_refs, core, nn_dot(left, right), start)
        place += per_blk * rows
    cond_tiles(out_refs, core, turned(cond_ref[...]), rows_of(d_cond_refs), place, stride)


def rows_of(refs):
    return jnp.concatenate([refs[0][...], refs[1][...]], axis=0)


def early_grads(samp, place, operands, cond_in):
    x_trans, d_up, hidden, d_trans, mixed, d_att, d_cond = (pair[0] for pair in operands)
    sizes = [
        x_trans.shape[1] * d_up.shape[1],
        hidden.shape[1] * d_trans.shape[1],
        mixed.shape[0] * d_att.shape[1],
        cond_in.shape[1] * d_cond.shape[1],
    ]
    rows = 16 * math.ceil(sum(sizes) / (samp * 2 * TILE_COLS * 16))
    vmem = pl.BlockSpec(memory_space=pltpu.VMEM)
    shape = jax.ShapeDtypeStruct((samp // 2, 2 * rows, TILE_COLS), jnp.bfloat16)
    return pl.pallas_call(
        early_grads_kernel,
        in_specs=[pl.BlockSpec(memory_space=pltpu.SMEM)] + [vmem] * (2 * len(operands) + 1),
        out_specs=[vmem, vmem],
        out_shape=[shape, shape],
        compiler_params=pltpu.CompilerParams(vmem_limit_bytes=VMEM_BYTES),
        cost_estimate=spends(15),
        name="early_grads",
    )(place, *[value for pair in operands for value in pair], cond_in)


def norm_parts(value):
    center = value - jnp.mean(value, axis=1, keepdims=True)
    rstd = lax.rsqrt(jnp.mean(center * center, axis=1, keepdims=True) + EPS)
    return center * rstd, rstd


def norm_grad(grad, hat, rstd):
    inner = jnp.mean(grad * hat, axis=1, keepdims=True)
    return rstd * (grad - jnp.mean(grad, axis=1, keepdims=True) - hat * inner)


def sigmoid(value):
    return 1.0 / (1.0 + jnp.exp(-value))


def first_kernel(
    place_ref, single_ref, act_ref, cond_weight_ref, cond_bias_ref, gain_ref, weight_ref,
    query_bias_ref, qkv_ref, gate_t_ref, x_ref, scale_ref, gate_ref, *, score_scale,
):
    heads = qkv_ref.shape[0]
    head_dim = qkv_ref.shape[1] // 3
    tokens, width = act_ref.shape
    single_hat, _ = norm_parts(single_ref[place_ref[1]].astype(jnp.float32))
    cond_in = (single_hat * gain_ref[0:1]).astype(jnp.bfloat16)
    bias = cond_bias_ref[0:1]
    scale = sigmoid(nn_dot(cond_in, cond_weight_ref[0, :, :width]) + bias[:, :width])
    scale_ref[...] = scale
    shift = nn_dot(cond_in, cond_weight_ref[0, :, width : 2 * width])
    gate_ref[...] = sigmoid(nn_dot(cond_in, cond_weight_ref[0, :, 2 * width :]) + bias[:, width:])
    act_hat, _ = norm_parts(act_ref[...].astype(jnp.float32))
    x_attn = (scale * act_hat + shift).astype(jnp.bfloat16)
    x_ref[...] = x_attn
    for part in range(4):
        value = nn_dot(x_attn, weight_ref[:, part * width : (part + 1) * width])
        if part == 0:
            value = (value + query_bias_ref[...][None]) * (score_scale * LOG2E)
        value = value.T
        if part == 3:
            gate_t_ref[...] = sigmoid(value)
        else:
            value = value.reshape(heads, head_dim, tokens).astype(jnp.bfloat16)
            qkv_ref[:, part * head_dim : (part + 1) * head_dim] = value


def first_call(heads, place, single_cond, act, cond_weight, cond_bias, gain, weight, query_bias):
    tokens, width = act.shape
    head_dim = width // heads
    vmem = pl.BlockSpec(memory_space=pltpu.VMEM)
    wide = jax.ShapeDtypeStruct((tokens, width), jnp.float32)
    return pl.pallas_call(
        functools.partial(first_kernel, score_scale=1.0 / math.sqrt(head_dim)),
        grid=(1,),
        in_specs=[
            pl.BlockSpec(memory_space=pltpu.SMEM),
            vmem,
            vmem,
            pl.BlockSpec((1,) + cond_weight.shape[1:], lambda _: (0, 0, 0)),
            vmem,
            vmem,
            vmem,
            vmem,
        ],
        out_specs=[vmem] * 5,
        out_shape=[
            jax.ShapeDtypeStruct((heads, 3 * head_dim, tokens), jnp.bfloat16),
            jax.ShapeDtypeStruct((width, tokens), jnp.float32),
            jax.ShapeDtypeStruct((tokens, width), jnp.bfloat16),
            wide,
            wide,
        ],
        compiler_params=pltpu.CompilerParams(vmem_limit_bytes=VMEM_BYTES),
        cost_estimate=spends(12),
        name="first",
    )(place, single_cond, act, cond_weight, cond_bias, gain, weight, query_bias)


def middle_kernel(
    attn_ref, gate_t_ref, act_ref, gate_attn_ref, cond_ref, cotangent_ref,
    out_weight_ref, in_weight_ref, down_weight_ref,
    block_ref, x_ref, d_up_ref, hid_ref, d_trans_ref, mixed_ref, d_att_ref, d_cond_ref,
    d_hidden_ref, d_cond_gate_ref, d_gate_ref, d_attn_ref,
):
    tokens, width = act_ref.shape
    units = hid_ref.shape[1]
    attn = attn_ref[...].reshape(width, tokens).astype(jnp.float32)
    gate = gate_t_ref[...]
    mixed = gate * attn
    mixed_ref[...] = mixed.astype(jnp.bfloat16)
    att_out = nn_dot(mixed.T.astype(jnp.bfloat16), out_weight_ref[...])
    gate_attn = gate_attn_ref[...]
    hidden = act_ref[...].astype(jnp.float32) + gate_attn * att_out
    hat, rstd = norm_parts(hidden)
    scale = sigmoid(cond_ref[:, :width])
    x_trans = (scale * hat + cond_ref[:, width : 2 * width]).astype(jnp.bfloat16)
    x_ref[...] = x_trans
    up_gate = nn_dot(x_trans, in_weight_ref[:, :units])
    up_lin = nn_dot(x_trans, in_weight_ref[:, units:])
    sig = sigmoid(up_gate)
    silu = up_gate * sig
    hid = (silu * up_lin).astype(jnp.bfloat16)
    hid_ref[...] = hid
    gate_trans = sigmoid(cond_ref[:, 2 * width :])
    cotangent = cotangent_ref[...].astype(jnp.float32)
    gated = gate_trans * cotangent
    d_trans = gated.astype(jnp.bfloat16)
    d_trans_ref[...] = d_trans
    d_hid = nt_dot(d_trans, down_weight_ref[...])
    slope = sig * (1.0 + up_gate * (1.0 - sig))
    d_up_ref[:, :units] = (d_hid * up_lin * slope).astype(jnp.bfloat16)
    d_up_ref[:, units:] = (d_hid * silu).astype(jnp.bfloat16)
    d_xt = nt_dot(d_up_ref[...], in_weight_ref[...])
    scaled = d_xt * scale
    d_hidden = cotangent + norm_grad(scaled, hat, rstd)
    d_hidden_ref[...] = d_hidden
    d_att = (gate_attn * d_hidden).astype(jnp.bfloat16)
    d_att_ref[...] = d_att
    d_mixed = nt_dot(out_weight_ref[...], d_att)
    d_attn_ref[...] = (gate * d_mixed).astype(jnp.bfloat16).reshape(d_attn_ref.shape)
    d_gate_ref[...] = (d_mixed * mixed * (1.0 - gate)).astype(jnp.bfloat16)
    d_cond_gate_ref[...] = (d_hidden * att_out * gate_attn * (1.0 - gate_attn)).astype(jnp.bfloat16)
    trans = nn_dot(hid, down_weight_ref[...])
    block_ref[...] = (hidden + gate_trans * trans).astype(jnp.bfloat16)
    d_cond_ref[:, :width] = (scaled * hat * (1.0 - scale)).astype(jnp.bfloat16)
    d_cond_ref[:, width : 2 * width] = d_xt.astype(jnp.bfloat16)
    d_cond_ref[:, 2 * width :] = (gated * trans * (1.0 - gate_trans)).astype(jnp.bfloat16)


def middle_call(half, attn, gate_t, act, gate_attn, cond, cotangent, *weights):
    tile = attn.shape[2]
    width = act.shape[1]
    units = weights[2].shape[0]
    once = pl.Buffered(1)

    def whole(value):
        zeros = (0,) * value.ndim
        return pl.BlockSpec(value.shape, lambda _: zeros, pipeline_mode=once)

    def rows(value):
        return pl.BlockSpec((tile, value.shape[1]), lambda _: (half, 0), pipeline_mode=once)

    shapes = [
        jax.ShapeDtypeStruct((tile, width), jnp.bfloat16),
        jax.ShapeDtypeStruct((tile, width), jnp.bfloat16),
        jax.ShapeDtypeStruct((tile, 2 * units), jnp.bfloat16),
        jax.ShapeDtypeStruct((tile, units), jnp.bfloat16),
        jax.ShapeDtypeStruct((tile, width), jnp.bfloat16),
        jax.ShapeDtypeStruct((width, tile), jnp.bfloat16),
        jax.ShapeDtypeStruct((tile, width), jnp.bfloat16),
        jax.ShapeDtypeStruct((tile, 3 * width), jnp.bfloat16),
        jax.ShapeDtypeStruct((tile, width), jnp.float32),
        jax.ShapeDtypeStruct((tile, width), jnp.bfloat16),
        jax.ShapeDtypeStruct((width, tile), jnp.bfloat16),
        jax.ShapeDtypeStruct(attn.shape, jnp.bfloat16),
    ]
    return pl.pallas_call(
        middle_kernel,
        grid=(1,),
        in_specs=[
            whole(attn),
            pl.BlockSpec((width, tile), lambda _: (0, half), pipeline_mode=once),
            rows(act), rows(gate_attn), rows(cond), rows(cotangent),
        ]
        + [whole(weight) for weight in weights],
        out_specs=[whole(shape) for shape in shapes],
        out_shape=shapes,
        compiler_params=pltpu.CompilerParams(vmem_limit_bytes=VMEM_BYTES),
        cost_estimate=spends(10),
        name="middle",
    )(attn, gate_t, act, gate_attn, cond, cotangent, *weights)


def final_kernel(
    place_ref, x_ref, d_query_ref, d_kv_ref, d_gate_one_ref, d_gate_two_ref,
    weight_ref, act_ref, scale_ref,
    d_hidden_one_ref, d_hidden_two_ref, d_cond_gate_one_ref, d_cond_gate_two_ref, single_ref, d_hat_ref, cond_weight_ref, gain_ref,
    cond_sums_ref, gain_sums_ref,
    act_grad_ref, keep_one_ref, give_one_ref, keep_two_ref, give_two_ref, sums_ref,
    d_cond_ref,
):
    core = place_ref[0]
    struct = place_ref[1]
    ones = jnp.ones((8, x_ref.shape[0]), jnp.bfloat16)
    left = turned(x_ref[...])
    width, tokens = left.shape
    groups = keep_one_ref.shape[0]
    rows = width // (2 * groups)
    head_dim = d_query_ref.shape[1] // 2
    one = (keep_one_ref, give_one_ref)
    two = (keep_two_ref, give_two_ref)
    stride_one = keep_one_ref.shape[1] // 2
    share = tokens // (2 * groups)
    stride_two = (keep_two_ref.shape[1] - 2 * share) // 2
    first_slots = stride_one // rows
    sums = []
    d_xa = 0.0
    for part in range(4):
        if part == 0:
            right = jnp.concatenate(
                [d_query_ref[:, :head_dim], d_query_ref[:, head_dim:]], axis=2
            )
            right = right.reshape(width, tokens)
            sums.append(nt_dot(ones, right)[0:1])
        elif part == 3:
            right = jnp.concatenate([d_gate_one_ref[...], d_gate_two_ref[...]], axis=1)
        else:
            right = d_kv_ref[:, (part - 1) * head_dim : part * head_dim].reshape(width, tokens)
        d_xa = d_xa + nn_dot(weight_ref[:, part * width : (part + 1) * width], right)
        for chunk in range(2):
            grad = nt_dot(left, right[chunk * TILE_COLS : (chunk + 1) * TILE_COLS])
            slot = 2 * (part % 2) + chunk
            if slot < first_slots:
                store_tiles(one, core, grad, part // 2 * stride_one + slot * rows)
            else:
                start = part // 2 * stride_two + (slot - first_slots) * rows
                store_tiles(two, core, grad, start)
    d_xa = d_xa.T
    act_hat, act_rstd = norm_parts(act_ref[...].astype(jnp.float32))
    scale = scale_ref[...].astype(jnp.float32)
    grad = d_xa * scale
    d_hidden = rows_of((d_hidden_one_ref, d_hidden_two_ref))
    act_grad_ref[...] = d_hidden + norm_grad(grad, act_hat, act_rstd)
    d_cond_ref[:, :width] = (grad * act_hat * (1.0 - scale)).astype(jnp.bfloat16)
    d_cond_ref[:, width : 2 * width] = d_xa.astype(jnp.bfloat16)
    d_cond_ref[:, 2 * width :] = rows_of((d_cond_gate_one_ref, d_cond_gate_two_ref))
    single_hat, single_rstd = norm_parts(single_ref[...].astype(jnp.float32))
    gain = gain_ref[...]
    cond_t = turned((single_hat * gain).astype(jnp.bfloat16))
    cond_tiles(two, core, cond_t, d_cond_ref, (4 - first_slots) * rows, stride_two)
    d_cond = d_cond_ref[...]
    d_in = nt_dot(d_cond, cond_weight_ref[...])
    for cond_sums in (nn_dot(ones, d_cond)[0:1], cond_sums_ref[...]):
        sums.extend([cond_sums[:, :width], cond_sums[:, 2 * width :]])
    sums.extend([jnp.sum(d_in * single_hat, axis=0, keepdims=True), gain_sums_ref[...]])
    sums_ref[...] = jnp.zeros_like(sums_ref)
    row = 0
    for value in sums:
        for start in range(0, value.shape[1], 128):
            sums_ref[row : row + 1] = value[:, start : start + 128]
            row += 1
    single_grad = norm_grad(d_in * gain + d_hat_ref[...], single_hat, single_rstd)
    single_grad = single_grad.reshape(2 * groups, share, single_grad.shape[1])
    chosen = [jnp.where(struct == member, single_grad, 0.0) for member in range(2)]
    chosen = jnp.concatenate(chosen, axis=1).reshape(-1, single_grad.shape[2])
    store_tiles(two, core, chosen, 2 * stride_two)


def final_call(samp, place, x_attn, d_query, d_kv, d_gate, weight, act, scale, d_hidden,
               d_cond_gate, single, d_hat, cond_weight, gain, cond_sums, gain_sums):
    groups = samp // 2
    tokens, width = act.shape
    chans = single.shape[1]
    rows = width // samp
    one_rows = 3 * rows
    cond_rows = cond_weight.size // (samp * 2 * TILE_COLS)
    two_rows = rows + 16 * math.ceil(cond_rows / 16)
    vmem = pl.BlockSpec(memory_space=pltpu.VMEM)
    share = tokens // samp
    one = jax.ShapeDtypeStruct((groups, 2 * one_rows, TILE_COLS), jnp.bfloat16)
    two = jax.ShapeDtypeStruct((groups, 2 * (two_rows + share), TILE_COLS), jnp.bfloat16)
    return pl.pallas_call(
        final_kernel,
        in_specs=[pl.BlockSpec(memory_space=pltpu.SMEM)] + [vmem] * 18,
        out_specs=[vmem] * 6,
        out_shape=[
            jax.ShapeDtypeStruct((tokens, width), jnp.float32),
            one, one, two, two,
            jax.ShapeDtypeStruct((8 * math.ceil((5 * width + 2 * chans) / 1024), 128), jnp.float32),
        ],
        scratch_shapes=[pltpu.VMEM((tokens, 3 * width), jnp.bfloat16)],
        compiler_params=pltpu.CompilerParams(vmem_limit_bytes=VMEM_BYTES),
        cost_estimate=spends(20),
        name="final",
    )(place, x_attn, d_query, d_kv, *d_gate, weight, act, scale, *d_hidden,
      *d_cond_gate, single, d_hat, cond_weight, gain, cond_sums, gain_sums)


def tie(*values):
    return lax.optimization_barrier(values)


def flip(value, axis, distance):
    size = lax.axis_size(axis)
    return lax.ppermute(value, axis, [(i, i ^ distance) for i in range(size)])


def halve(value, axis, distance, dim):
    bit = (lax.axis_index(axis) // distance) % 2
    keep = lax.dynamic_index_in_dim(value, bit, dim, keepdims=False)
    give = lax.dynamic_index_in_dim(value, 1 - bit, dim, keepdims=False)
    return add_low(keep, flip(give, axis, distance))


def spread(value, distance, dim):
    other = flip(value, "samp", distance)
    first = (lax.axis_index("samp") // distance) % 2 == 0
    return jnp.stack([jnp.where(first, value, other), jnp.where(first, other, value)], axis=dim)


def add_low(left, right):
    return (left.astype(jnp.float32) + right.astype(jnp.float32)).astype(jnp.bfloat16)


def grad_from_tiles(tiles, rows):
    blocks = tiles.reshape(-1, rows, TILE_COLS)
    return blocks.transpose(1, 0, 2).reshape(rows, -1)


def exchange(value):
    return lax.all_to_all(value, "samp", 0, 0, tiled=True)


def fast_local(
    activations,
    single_cond,
    pair_repr,
    struct_id,
    seq_lengths,
    qkvg_weight,
    query_bias,
    out_weight,
    in_weight,
    down_weight,
    cond_weight,
    cond_bias,
    single_gain,
    pair_gain,
    pair_weight,
    cotangent,
):
    samp = lax.axis_size("samp")
    blks = lax.axis_size("blk")
    tokens, width = activations.shape[1:]
    heads = pair_weight.shape[1]
    head_dim = width // heads
    hidden_units = down_weight.shape[0]
    structs, _, cols, chans = pair_repr.shape
    blk_arg = lax.axis_index("blk").astype(jnp.int32)[None]
    index = lax.axis_index("samp").astype(jnp.int32)
    place = jnp.stack([index % 2, struct_id[0]])
    act = activations[0]

    qkv, gate_val, x_attn, scale_attn, gate_attn = first_call(
        heads, place, single_cond, act, cond_weight, cond_bias, single_gain,
        qkvg_weight, query_bias,
    )
    own_id = jnp.where(
        lax.broadcasted_iota(jnp.int32, (8, 128), 1) == index, struct_id[0], 0
    ).astype(jnp.float32)
    qkv, pair_in, own_id = tie(qkv, pair_repr, own_id)
    pair = pair_in.reshape(structs, 2, 2, tokens // 4, cols, chans)
    bias_part, pair_mean, pair_rstd = pair_forward(pair, pair_gain, pair_weight)
    own_id, bias_sent = tie(own_id, bias_part)
    for distance in (1, 2, 4):
        own_id = own_id + flip(own_id, "samp", distance)
    qkv, own_id, bias_sent = tie(exchange(qkv), own_id, bias_sent)
    single = jnp.where(struct_id[0] == 1, single_cond[1], single_cond[0])
    single_hat = norm_rows(single.astype(jnp.float32))
    cond_in = (single_hat * single_gain[1]).astype(jnp.bfloat16)
    bias_row = jnp.concatenate(
        [cond_bias[1, :width], jnp.zeros((width,), jnp.float32), cond_bias[1, width:]]
    )
    cond_trans = nn_dot(cond_in, cond_weight[1]) + bias_row
    own_id = own_id + flip(own_id, "samp", 8)
    bias, kv_far, cond_trans, own_id = tie(
        exchange(bias_sent), flip(qkv[:, head_dim:], "blk", 1), cond_trans, own_id
    )
    ids = own_id[0, :samp].astype(jnp.int32)
    forward_args = (ids, seq_lengths, blk_arg, qkv, kv_far)
    sent_one, *saved_one = attention_forward(0, *forward_args, bias)
    sent_one, bias = tie(sent_one, bias)
    sent_two, *saved_two = attention_forward(1, *forward_args, bias)
    attn_one, sent_two = tie(exchange(sent_one), sent_two)
    middle_args = (
        gate_val, act, gate_attn, cond_trans, cotangent[0], out_weight, in_weight, down_weight
    )
    *middle_one, d_attn_one = middle_call(0, attn_one, *middle_args)
    attn_two, d_attn_one = tie(exchange(sent_two), d_attn_one)
    *middle_two, d_attn_two = middle_call(1, attn_two, *middle_args)
    d_attn_one, d_attn_two, *middle_two = tie(exchange(d_attn_one), d_attn_two, *middle_two)
    both = list(zip(middle_one, middle_two))
    block_out = jnp.concatenate(both[0], axis=0)
    d_hidden, d_cond_gate, d_gate_pre = both[8:]

    backward_args = (ids, blk_arg, qkv, kv_far)
    d_query_one, d_own, d_far, d_bias_one = attention_backward(
        0, *backward_args, d_attn_one, *saved_one, bias, ()
    )
    d_attn_two, d_query_one, d_own, d_far, d_bias_one = tie(
        exchange(d_attn_two), d_query_one, d_own, d_far, d_bias_one
    )
    d_bias_one = exchange(d_bias_one)
    d_query_two, d_own, d_far, d_bias_two = attention_backward(
        1, *backward_args, d_attn_two, *saved_two, bias, (d_own, d_far)
    )
    d_query = jnp.concatenate([d_query_one, d_query_two], axis=1)
    d_far, d_bias_two, *operands = tie(
        d_far, d_bias_two, *[value for pair in both[1:8] for value in pair]
    )
    operands = list(zip(operands[::2], operands[1::2]))
    keep_early, give_early = early_grads(samp, place, operands, cond_in)
    d_cond_trans = jnp.concatenate(operands[6], axis=0)
    d_in = nt_dot(d_cond_trans, cond_weight[1])
    gain_sums_trans = jnp.sum(d_in * single_hat, axis=0, keepdims=True)
    cond_sums_trans = jnp.sum(d_cond_trans.astype(jnp.float32), axis=0, keepdims=True)
    d_hat = d_in * single_gain[1]
    d_kv = add_low(d_own, flip(d_far, "blk", 1))
    d_query, d_bias_one = tie(d_query, d_bias_one)
    (
        d_kv, d_query, d_hat, gain_sums_trans, cond_sums_trans, keep_early, give_early,
        d_bias_one, d_bias_two,
    ) = tie(
        d_kv, exchange(d_query), d_hat, gain_sums_trans, cond_sums_trans, keep_early, give_early,
        d_bias_one, d_bias_two,
    )
    cube = (samp // 8, 2, 2)
    early = add_low(keep_early, flip(give_early, "samp", 1))
    pair_grad, moment_one = pair_backward(
        0, pair, d_bias_one, bias_part, pair_mean, pair_rstd, pair_gain, pair_weight, ()
    )
    d_kv, d_bias_two, pair_grad = tie(exchange(d_kv), d_bias_two, pair_grad)
    early = halve(early.reshape(cube + (2, -1, TILE_COLS)), "blk", 1, 3)
    d_bias_two = exchange(d_bias_two)

    act_grad, keep_one, give_one, keep_two, give_two, sums = final_call(
        samp, place, x_attn, d_query, d_kv, d_gate_pre, qkvg_weight, act, scale_attn,
        d_hidden, d_cond_gate, single, d_hat, cond_weight[0], single_gain[0][None],
        cond_sums_trans, gain_sums_trans,
    )
    d_bias_two, act_grad, keep_one, give_one, keep_two, give_two, early = tie(
        d_bias_two, act_grad, keep_one, give_one, keep_two, give_two, early
    )
    early = halve(early, "samp", 4, 1)
    one = add_low(keep_one, flip(give_one, "samp", 1)).reshape(cube + (2, -1, TILE_COLS))
    two = add_low(keep_two, flip(give_two, "samp", 1)).reshape(cube + (-1, TILE_COLS))
    one, two, d_bias_two = tie(one, two, d_bias_two)
    one = halve(one, "blk", 1, 3)
    two = halve(two, "samp", 2, 2)
    pair_grad, moment_two = pair_backward(
        1, pair, d_bias_two, bias_part, pair_mean, pair_rstd, pair_gain, pair_weight, (pair_grad,)
    )
    one, two, pair_grad, summed = tie(
        one, two, pair_grad, jnp.concatenate([sums, moment_one + moment_two], axis=0)
    )
    shared = 2 * tokens // samp
    alone = two[:, :, -shared:]
    two = two[:, :, :-shared].reshape(two.shape[:2] + (2, -1, TILE_COLS))
    one = halve(one, "samp", 2, 2)
    two = halve(two, "blk", 1, 2)
    alone = add_low(alone, flip(alone, "samp", 4))
    summed = summed + flip(summed, "samp", 4)
    summed = summed + flip(summed, "samp", 8)
    one, two, early, alone, summed = tie(one, two, early, alone, summed)
    early = halve(early, "samp", 2, 1)
    late = halve(jnp.concatenate([one, two], axis=2), "samp", 4, 1)
    alone = add_low(alone, flip(alone, "samp", 8))
    summed = summed + flip(summed, "blk", 1)
    summed = summed + flip(summed, "samp", 1)
    late, early, alone, summed = tie(late, early, alone, summed)
    late = halve(late, "samp", 8, 0).astype(jnp.float32)
    early = halve(early, "samp", 8, 0)
    alone = spread(alone, 2, 2)
    summed = summed + flip(summed, "samp", 2)
    alone = spread(alone, 1, 3)
    single_grad = alone.reshape(samp, structs, tokens // samp, -1).transpose(1, 0, 2, 3)
    single_grad = single_grad.reshape(structs, tokens, -1).astype(jnp.float32)
    early = early.astype(jnp.float32)
    small_grads = []
    start = 0
    for like in (query_bias, cond_bias, single_gain):
        stop = start + like.size // 128
        small_grads.append(summed[start:stop].reshape(like.shape))
        start = stop
    query_bias_grad, cond_bias_grad, single_gain_grad = small_grads
    moment = summed[-heads:].T
    pair_weight_grad = moment * pair_gain[:, None]
    pair_gain_grad = jnp.sum(moment * pair_weight.astype(jnp.float32), axis=1)

    def take(tiles, start, rows, width_out):
        count = rows * width_out // TILE_COLS
        return grad_from_tiles(tiles[start : start + count], rows), start + count

    start = 0
    in_grad, start = take(early, start, width // samp, in_weight.shape[1] // blks)
    down_grad, start = take(early, start, hidden_units // samp, width // blks)
    out_grad, start = take(early, start, width // samp, width // blks)
    cond_rows_dev = cond_weight.shape[1] // samp
    cond_cols_dev = cond_weight.shape[2] // blks
    cond_trans_grad, start = take(early, start, cond_rows_dev, cond_cols_dev)
    qkvg_grad, start = take(late, 0, width // samp, qkvg_weight.shape[1] // blks)
    cond_attn_grad, start = take(late, start, cond_rows_dev, cond_cols_dev)
    return (
        block_out[None],
        act_grad[None],
        single_grad,
        pair_grad.reshape(pair_repr.shape),
        qkvg_grad,
        query_bias_grad,
        out_grad,
        in_grad,
        down_grad,
        jnp.stack([cond_attn_grad, cond_trans_grad]),
        cond_bias_grad,
        single_gain_grad,
        pair_gain_grad,
        pair_weight_grad,
    )


def solution(mesh):
    sizes = dict(mesh.shape)
    program = fast_local if (sizes["samp"], sizes["blk"]) == (16, 2) else local
    return jax.shard_map(
        program,
        mesh=mesh,
        in_specs=(
            P("samp", "blk", None),
            P(None, "blk", None),
            P(None, "blk", "samp", None),
            P("samp"),
            P(),
            P(),
            P(),
            P(),
            P(),
            P(),
            P(),
            P(),
            P(),
            P(),
            P(),
            P("samp", "blk", None),
        ),
        out_specs=(
            P("samp", "blk", None),
            P("samp", "blk", None),
            P(None, "blk", None),
            P(None, "blk", "samp", None),
            P("samp", "blk"),
            P(),
            P("samp", "blk"),
            P("samp", "blk"),
            P("samp", "blk"),
            P(None, "samp", "blk"),
            P(),
            P(),
            P(),
            P(),
        ),
        check_vma=False,
    )
```

```python
import functools
import math

import jax
import jax.numpy as jnp
from jax import lax
from jax.experimental import pallas as pl
from jax.experimental.pallas import tpu as pltpu
from jax.sharding import PartitionSpec as P

EPS = 1e-05
MASKED = -1000000000.0
LOG2E = 1.4426950408889634
LN2 = 0.6931471805599453
VMEM_BYTES = 56 * 1024 * 1024
TILE_COLS = 384


def norm_rows(value):
    center = value - jnp.mean(value, axis=-1, keepdims=True)
    return center * lax.rsqrt(jnp.mean(center * center, axis=-1, keepdims=True) + EPS)


def pick_struct(table, ids):
    expand = (ids.shape[0],) + (1,) * (table.ndim - 1)
    chosen = jnp.broadcast_to(table[0][None], (ids.shape[0],) + table.shape[1:])
    chosen = jnp.where(ids.reshape(expand) == 1, table[1][None], chosen)
    return chosen


def struct_sum(values, ids, structs):
    expand = (ids.shape[0],) + (1,) * (values.ndim - 1)
    return jnp.stack(
        [
            jnp.sum(jnp.where(ids.reshape(expand) == member, values, 0.0), axis=0)
            for member in range(structs)
        ]
    )


def block_length(piece_len):
    return math.gcd(piece_len, 512)


def local(
    activations,
    single_cond,
    pair_repr,
    struct_id,
    seq_lengths,
    qkvg_weight,
    query_bias,
    out_weight,
    in_weight,
    down_weight,
    cond_weight,
    cond_bias,
    single_gain,
    pair_gain,
    pair_weight,
    cotangent,
):
    samples_dev, tok_rows, width = activations.shape
    heads = pair_weight.shape[1]
    head_dim = width // heads
    hidden_units = down_weight.shape[0]
    structs = single_cond.shape[0]
    seq_total = tok_rows * lax.axis_size("blk")
    score_scale = 1.0 / math.sqrt(head_dim)
    zero_index = jnp.zeros((), jnp.int32)
    key_limit = pick_struct(seq_lengths, struct_id)
    single_hat = norm_rows(single_cond.astype(jnp.float32))
    cond_inputs = []
    cond_rows = []
    for sublayer in range(2):
        cond_in = (single_hat * single_gain[sublayer]).astype(jnp.bfloat16)
        bias_row = jnp.concatenate(
            [
                cond_bias[sublayer, :width],
                jnp.zeros((width,), jnp.float32),
                cond_bias[sublayer, width:],
            ]
        )
        cond_pre = (
            jnp.einsum(
                "cti,ij->ctj", cond_in, cond_weight[sublayer], preferred_element_type=jnp.float32
            )
            + bias_row
        )
        cond_inputs.append(cond_in)
        cond_rows.append(pick_struct(cond_pre, struct_id))
    pair_hat, pair_norm_back = jax.vjp(norm_rows, pair_repr.astype(jnp.float32))
    pair_in = (pair_hat * pair_gain).astype(jnp.bfloat16)
    bias_local = jnp.einsum(
        "crkz,zh->crhk", pair_in, pair_weight, preferred_element_type=jnp.float32
    ).astype(jnp.bfloat16)
    bias_all = lax.all_gather(bias_local, "samp", axis=3, tiled=True)
    act_float = activations.astype(jnp.float32)
    act_hat, act_norm_back = jax.vjp(norm_rows, act_float)
    cond_attn = cond_rows[0]
    scale_attn = jax.nn.sigmoid(cond_attn[..., :width])
    gate_attn = jax.nn.sigmoid(cond_attn[..., 2 * width :])
    x_attn = (scale_attn * act_hat + cond_attn[..., width : 2 * width]).astype(jnp.bfloat16)
    proj_bias = jnp.concatenate([query_bias, jnp.zeros((3 * width,), jnp.float32)])
    projected = (
        jnp.einsum("sti,ij->stj", x_attn, qkvg_weight, preferred_element_type=jnp.float32)
        + proj_bias
    )
    query = (
        projected[..., :width].astype(jnp.bfloat16).reshape(samples_dev, tok_rows, heads, head_dim)
    )
    keys_values = projected[..., width : 3 * width].astype(jnp.bfloat16)
    gate_pre = projected[..., 3 * width :]

    def block_scores(sub_kv, offset):
        block_len = sub_kv.shape[1]
        keys_block = sub_kv[..., :width].reshape(samples_dev, block_len, heads, head_dim)
        scores = (
            jnp.einsum("sqhd,skhd->sqhk", query, keys_block, preferred_element_type=jnp.float32)
            * score_scale
        )
        bias_block = lax.dynamic_slice_in_dim(bias_all, offset, block_len, 3)
        scores = scores + pick_struct(bias_block, struct_id).astype(jnp.float32)
        positions = offset + jnp.arange(block_len, dtype=jnp.int32)
        valid = positions[None, :] < key_limit[:, None]
        return jnp.where(valid[:, None, None, :], scores, MASKED)

    def forward_fold(state, block_kv):
        block_len = block_length(block_kv.shape[1])
        count = block_kv.shape[1] // block_len

        def forward_step(carry, index):
            row_peak, row_total, row_acc = carry
            sub_offset = index * block_len
            sub_kv = lax.dynamic_slice_in_dim(block_kv, index * block_len, block_len, 1)
            scores = block_scores(sub_kv, sub_offset)
            values_block = sub_kv[..., width:].reshape(samples_dev, block_len, heads, head_dim)
            new_peak = jnp.maximum(row_peak, jnp.max(scores, axis=-1))
            rescale = jnp.exp(row_peak - new_peak)
            weights = jnp.exp(scores - new_peak[..., None])
            row_total = row_total * rescale + jnp.sum(weights, axis=-1)
            row_acc = row_acc * rescale[..., None] + jnp.einsum(
                "sqhk,skhd->sqhd",
                weights.astype(jnp.bfloat16),
                values_block,
                preferred_element_type=jnp.float32,
            )
            return ((new_peak, row_total, row_acc), None)

        result, ignored = lax.scan(
            jax.checkpoint(forward_step), state, jnp.arange(count, dtype=jnp.int32)
        )
        return result

    stats_shape = (samples_dev, tok_rows, heads)
    forward_init = (
        jnp.full(stats_shape, -1e30, jnp.float32),
        jnp.zeros(stats_shape, jnp.float32),
        jnp.zeros((samples_dev, tok_rows, heads, head_dim), jnp.float32),
    )
    row_peak, row_total, row_acc = forward_fold(
        forward_init, lax.all_gather(keys_values, "blk", axis=1, tiled=True)
    )
    attn4 = row_acc / row_total[..., None]
    log_sum = row_peak + jnp.log(row_total)
    attn = attn4.reshape(samples_dev, tok_rows, width)
    gate_val = jax.nn.sigmoid(gate_pre)
    mixed = (gate_val * attn).astype(jnp.bfloat16)
    att_out = jnp.einsum("sti,ij->stj", mixed, out_weight, preferred_element_type=jnp.float32)
    hidden_state = act_float + gate_attn * att_out
    cond_trans = cond_rows[1]
    scale_trans = jax.nn.sigmoid(cond_trans[..., :width])
    gate_trans = jax.nn.sigmoid(cond_trans[..., 2 * width :])
    hidden_hat, hidden_norm_back = jax.vjp(norm_rows, hidden_state)
    x_trans = (scale_trans * hidden_hat + cond_trans[..., width : 2 * width]).astype(jnp.bfloat16)
    up_proj = jnp.einsum("sti,ij->stj", x_trans, in_weight, preferred_element_type=jnp.float32)
    up_gate = up_proj[..., :hidden_units]
    up_lin = up_proj[..., hidden_units:]
    sig_gate = jax.nn.sigmoid(up_gate)
    silu_gate = up_gate * sig_gate
    hidden_act = (silu_gate * up_lin).astype(jnp.bfloat16)
    trans = jnp.einsum("stf,fd->std", hidden_act, down_weight, preferred_element_type=jnp.float32)
    block_out = (hidden_state + gate_trans * trans).astype(jnp.bfloat16)
    d_out = cotangent.astype(jnp.float32)
    d_trans = (gate_trans * d_out).astype(jnp.bfloat16)
    grad_down = jnp.einsum("stf,std->fd", hidden_act, d_trans, preferred_element_type=jnp.float32)
    d_hid = jnp.einsum("std,fd->stf", d_trans, down_weight, preferred_element_type=jnp.float32)
    silu_slope = sig_gate * (1.0 + up_gate * (1.0 - sig_gate))
    d_up = jnp.concatenate([d_hid * up_lin * silu_slope, d_hid * silu_gate], axis=-1).astype(
        jnp.bfloat16
    )
    grad_in = jnp.einsum("sti,stj->ij", x_trans, d_up, preferred_element_type=jnp.float32)
    d_xt = jnp.einsum("stj,ij->sti", d_up, in_weight, preferred_element_type=jnp.float32)
    d_hidden = d_out + hidden_norm_back(d_xt * scale_trans)[0]
    d_cond_trans = jnp.concatenate(
        [
            d_xt * hidden_hat * scale_trans * (1.0 - scale_trans),
            d_xt,
            d_out * trans * gate_trans * (1.0 - gate_trans),
        ],
        axis=-1,
    )
    d_att = (gate_attn * d_hidden).astype(jnp.bfloat16)
    grad_out = jnp.einsum("sti,stj->ij", mixed, d_att, preferred_element_type=jnp.float32)
    d_mixed = jnp.einsum("stj,ij->sti", d_att, out_weight, preferred_element_type=jnp.float32)
    d_attn = (gate_val * d_mixed).astype(jnp.bfloat16)
    d_gate_pre = d_mixed * attn * gate_val * (1.0 - gate_val)
    d_attn4 = d_attn.reshape(samples_dev, tok_rows, heads, head_dim)
    row_delta = jnp.sum(d_attn4.astype(jnp.float32) * attn4, axis=-1)

    def backward_fold(state, block_kv):
        block_len = block_length(block_kv.shape[1])
        count = block_kv.shape[1] // block_len

        def backward_step(carry, index):
            d_query, d_kv, d_bias = carry
            sub_offset = index * block_len
            sub_kv = lax.dynamic_slice_in_dim(block_kv, index * block_len, block_len, 1)
            keys_block = sub_kv[..., :width].reshape(samples_dev, block_len, heads, head_dim)
            values_block = sub_kv[..., width:].reshape(samples_dev, block_len, heads, head_dim)
            scores = block_scores(sub_kv, sub_offset)
            attn_probs = jnp.exp(scores - log_sum[..., None])
            d_probs = jnp.einsum(
                "sqhd,skhd->sqhk", d_attn4, values_block, preferred_element_type=jnp.float32
            )
            d_scores = (attn_probs * (d_probs - row_delta[..., None])).astype(jnp.bfloat16)
            d_query = (
                d_query
                + jnp.einsum(
                    "sqhk,skhd->sqhd", d_scores, keys_block, preferred_element_type=jnp.float32
                )
                * score_scale
            )
            d_keys = (
                jnp.einsum("sqhk,sqhd->skhd", d_scores, query, preferred_element_type=jnp.float32)
                * score_scale
            )
            d_values = jnp.einsum(
                "sqhk,sqhd->skhd",
                attn_probs.astype(jnp.bfloat16),
                d_attn4,
                preferred_element_type=jnp.float32,
            )
            d_new = jnp.concatenate(
                [
                    d_keys.reshape(samples_dev, block_len, width),
                    d_values.reshape(samples_dev, block_len, width),
                ],
                axis=-1,
            )
            d_kv = lax.dynamic_update_slice(d_kv, d_new, (zero_index, sub_offset, zero_index))
            bias_part = struct_sum(d_scores.astype(jnp.float32), struct_id, structs)
            d_bias = lax.dynamic_update_slice(
                d_bias, bias_part, (zero_index, zero_index, zero_index, sub_offset)
            )
            return ((d_query, d_kv, d_bias), None)

        result, ignored = lax.scan(
            jax.checkpoint(backward_step), state, jnp.arange(count, dtype=jnp.int32)
        )
        return result

    backward_init = (
        jnp.zeros((samples_dev, tok_rows, heads, head_dim), jnp.float32),
        jnp.zeros((samples_dev, seq_total, 2 * width), jnp.float32),
        jnp.zeros((structs, tok_rows, heads, seq_total), jnp.float32),
    )
    d_query, d_kv, d_bias = backward_fold(
        backward_init, lax.all_gather(keys_values, "blk", axis=1, tiled=True)
    )
    d_kv_own = lax.psum_scatter(
        d_kv.astype(jnp.bfloat16), "blk", scatter_dimension=1, tiled=True
    ).astype(jnp.float32)
    d_proj = jnp.concatenate(
        [d_query.reshape(samples_dev, tok_rows, width), d_kv_own, d_gate_pre], axis=-1
    ).astype(jnp.bfloat16)
    grad_qkvg = jnp.einsum("sti,stj->ij", x_attn, d_proj, preferred_element_type=jnp.float32)
    grad_query_bias = jnp.sum(d_proj[..., :width].astype(jnp.float32), axis=(0, 1))
    d_xa = jnp.einsum("stj,ij->sti", d_proj, qkvg_weight, preferred_element_type=jnp.float32)
    act_grad = d_hidden + act_norm_back(d_xa * scale_attn)[0]
    d_cond_attn = jnp.concatenate(
        [
            d_xa * act_hat * scale_attn * (1.0 - scale_attn),
            d_xa,
            d_hidden * att_out * gate_attn * (1.0 - gate_attn),
        ],
        axis=-1,
    )
    d_cond_all = jnp.concatenate(
        [struct_sum(d_cond_attn, struct_id, structs), struct_sum(d_cond_trans, struct_id, structs)],
        axis=-1,
    )
    bias_sum, cond_sum = (
        lax.psum_scatter(
            d_bias.astype(jnp.bfloat16), "samp", scatter_dimension=3, tiled=True
        ).astype(jnp.float32),
        lax.psum_scatter(
            d_cond_all.astype(jnp.bfloat16), "samp", scatter_dimension=1, tiled=True
        ).astype(jnp.float32),
    )
    bias_round = bias_sum.astype(jnp.bfloat16)
    grad_pair_weight = jnp.einsum(
        "crkz,crhk->zh", pair_in, bias_round, preferred_element_type=jnp.float32
    )
    d_pair_in = jnp.einsum(
        "crhk,zh->crkz", bias_round, pair_weight, preferred_element_type=jnp.float32
    )
    grad_pair_gain = jnp.sum(d_pair_in * pair_hat, axis=(0, 1, 2))
    pair_grad = pair_norm_back(d_pair_in * pair_gain)[0]
    slice_len = cond_sum.shape[1]
    slice_start = lax.axis_index("samp") * slice_len
    single_part = lax.dynamic_slice_in_dim(single_cond, slice_start, slice_len, 1).astype(
        jnp.float32
    )
    part_hat, part_norm_back = jax.vjp(norm_rows, single_part)
    cond_round = cond_sum.astype(jnp.bfloat16)
    d_part_hat = jnp.zeros_like(part_hat)
    cond_grads = []
    cond_bias_grads = []
    gain_grads = []
    for sublayer in range(2):
        d_layer = cond_round[..., sublayer * 3 * width : (sublayer + 1) * 3 * width]
        part_in = lax.dynamic_slice_in_dim(cond_inputs[sublayer], slice_start, slice_len, 1)
        cond_grads.append(
            jnp.einsum("cti,ctj->ij", part_in, d_layer, preferred_element_type=jnp.float32)
        )
        layer_sums = jnp.sum(d_layer.astype(jnp.float32), axis=(0, 1))
        cond_bias_grads.append(jnp.concatenate([layer_sums[:width], layer_sums[2 * width :]]))
        d_in = jnp.einsum(
            "ctj,ij->cti", d_layer, cond_weight[sublayer], preferred_element_type=jnp.float32
        )
        gain_grads.append(jnp.sum(d_in * part_hat, axis=(0, 1)))
        d_part_hat = d_part_hat + d_in * single_gain[sublayer]
    single_part_grad = part_norm_back(d_part_hat)[0]
    single_grad = lax.all_gather(single_part_grad, "samp", axis=1, tiled=True)
    grad_cond = jnp.stack(cond_grads)
    part_qkvg, part_out, part_in_w, part_down, part_cond = (
        lax.psum_scatter(
            grad_qkvg.astype(jnp.bfloat16), "blk", scatter_dimension=1, tiled=True
        ).astype(jnp.float32),
        lax.psum_scatter(
            grad_out.astype(jnp.bfloat16), "blk", scatter_dimension=1, tiled=True
        ).astype(jnp.float32),
        lax.psum_scatter(
            grad_in.astype(jnp.bfloat16), "blk", scatter_dimension=1, tiled=True
        ).astype(jnp.float32),
        lax.psum_scatter(
            grad_down.astype(jnp.bfloat16), "blk", scatter_dimension=1, tiled=True
        ).astype(jnp.float32),
        lax.psum_scatter(
            grad_cond.astype(jnp.bfloat16), "blk", scatter_dimension=2, tiled=True
        ).astype(jnp.float32),
    )
    qkvg_grad, out_grad, in_grad, down_grad, cond_grad = (
        lax.psum_scatter(
            part_qkvg.astype(jnp.bfloat16), "samp", scatter_dimension=0, tiled=True
        ).astype(jnp.float32),
        lax.psum_scatter(
            part_out.astype(jnp.bfloat16), "samp", scatter_dimension=0, tiled=True
        ).astype(jnp.float32),
        lax.psum_scatter(
            part_in_w.astype(jnp.bfloat16), "samp", scatter_dimension=0, tiled=True
        ).astype(jnp.float32),
        lax.psum_scatter(
            part_down.astype(jnp.bfloat16), "samp", scatter_dimension=0, tiled=True
        ).astype(jnp.float32),
        lax.psum_scatter(
            part_cond.astype(jnp.bfloat16), "samp", scatter_dimension=1, tiled=True
        ).astype(jnp.float32),
    )
    query_bias_grad, cond_bias_grad, single_gain_grad, pair_gain_grad, pair_weight_grad = lax.psum(
        (
            grad_query_bias,
            jnp.stack(cond_bias_grads),
            jnp.stack(gain_grads),
            grad_pair_gain,
            grad_pair_weight,
        ),
        ("samp", "blk"),
    )
    return (
        block_out,
        act_grad,
        single_grad,
        pair_grad,
        qkvg_grad,
        query_bias_grad,
        out_grad,
        in_grad,
        down_grad,
        cond_grad,
        cond_bias_grad,
        single_gain_grad,
        pair_gain_grad,
        pair_weight_grad,
    )


FORWARD_GROUP = 4
BACKWARD_GROUP = 4
KEY_CHUNK = 128


def nt_dot(left, right):
    return lax.dot_general(
        left, right, (((1,), (1,)), ((), ())), preferred_element_type=jnp.float32
    )


def nn_dot(left, right):
    return lax.dot_general(
        left, right, (((1,), (0,)), ((), ())), preferred_element_type=jnp.float32
    )


def tn_dot(left, right):
    return lax.dot_general(
        left, right, (((0,), (0,)), ((), ())), preferred_element_type=jnp.float32
    )


def split_two(value):
    high = value.astype(jnp.bfloat16)
    return high, (value - high.astype(jnp.float32)).astype(jnp.bfloat16)


def spends(micros):
    return pl.CostEstimate(
        flops=int(micros * 1e9), bytes_accessed=int(micros * 3e6), transcendentals=0
    )


def pair_rows(pair_ref):
    quarters, rows, cols, chans = pair_ref.shape[2:]
    both = jnp.concatenate([pair_ref[0, 0, quarter] for quarter in range(quarters)], axis=1)
    return both.reshape(rows * quarters * cols, chans)


def pair_forward_kernel(pair_ref, coef_ref, coef_sum_ref, bias_ref, mean_ref, rstd_ref):
    heads = bias_ref.shape[0]
    rows, lanes = mean_ref.shape[2:]
    chans = pair_ref.shape[5]
    cells = pair_rows(pair_ref)
    wide = cells.astype(jnp.float32)
    square_high, square_low = split_two(wide * wide)
    sums = nt_dot(coef_ref[...], jnp.concatenate([cells, square_high], axis=1))
    low_sums = nt_dot(jnp.ones((16, chans), jnp.bfloat16), square_low)
    raw = sums[:heads] + sums[heads : 2 * heads]
    total = sums[2 * heads : 2 * heads + 1]
    squares = sums[2 * heads + 8 : 2 * heads + 9] + low_sums[0:1]
    total_high = total.astype(jnp.bfloat16).astype(jnp.float32)
    total_low = total - total_high
    spread = squares * chans - total_high * total_high
    spread = spread - 2.0 * total_high * total_low - total_low * total_low
    rstd = lax.rsqrt(jnp.maximum(spread, 0.0) * (1.0 / (chans * chans)) + EPS)
    mean = total * (1.0 / chans)
    bias = (raw - coef_sum_ref[...] * mean) * (rstd * LOG2E)
    bias_ref[:, 0, 0] = bias.reshape(heads, rows, lanes).astype(jnp.bfloat16)
    mean_ref[0, 0] = mean.reshape(rows, lanes)
    rstd_ref[0, 0] = rstd.reshape(rows, lanes)


def pair_forward(pair, pair_gain, pair_weight):
    structs, halves, quarters, rows, cols, chans = pair.shape
    heads = pair_weight.shape[1]
    lanes = quarters * cols
    step = 32
    gained = pair_weight.astype(jnp.float32) * pair_gain[:, None]
    high, low = split_two(gained.T)
    ones_row = jnp.zeros((8, chans), jnp.bfloat16).at[0].set(1.0)
    blank = jnp.zeros((8, chans), jnp.bfloat16)
    coef = jnp.concatenate(
        [
            jnp.concatenate([high, low, ones_row, blank], axis=0),
            jnp.concatenate([jnp.zeros((2 * heads, chans), jnp.bfloat16), blank, ones_row], axis=0),
        ],
        axis=1,
    )
    coef_sum = jnp.sum(gained, axis=0)[:, None]
    return pl.pallas_call(
        pair_forward_kernel,
        grid=(halves, structs, rows // step),
        in_specs=[
            pl.BlockSpec((1, 1, quarters, step, cols, chans), lambda h, c, r: (c, h, 0, r, 0, 0)),
            pl.BlockSpec(coef.shape, lambda h, c, r: (0, 0)),
            pl.BlockSpec(coef_sum.shape, lambda h, c, r: (0, 0)),
        ],
        out_specs=[
            pl.BlockSpec((heads, 1, 1, step, lanes), lambda h, c, r: (0, h, c, r, 0)),
            pl.BlockSpec((1, 1, step, lanes), lambda h, c, r: (h, c, r, 0)),
            pl.BlockSpec((1, 1, step, lanes), lambda h, c, r: (h, c, r, 0)),
        ],
        out_shape=[
            jax.ShapeDtypeStruct((heads, halves, structs, rows, lanes), jnp.bfloat16),
            jax.ShapeDtypeStruct((halves, structs, rows, lanes), jnp.float32),
            jax.ShapeDtypeStruct((halves, structs, rows, lanes), jnp.float32),
        ],
        compiler_params=pltpu.CompilerParams(vmem_limit_bytes=VMEM_BYTES),
        cost_estimate=spends(20),
        name="pair_forward",
    )(pair, coef, coef_sum)


def pair_backward_kernel(
    pair_ref, d_bias_ref, bias_ref, mean_ref, rstd_ref, coef_ref, coef_sum_ref, *refs
):
    grad_ref, inner_ref, offset_ref = refs[-3:]
    heads = d_bias_ref.shape[0]
    rows, lanes = mean_ref.shape[2:]
    quarters, _, cols, chans = pair_ref.shape[2:]
    count = rows * lanes
    cells = pair_rows(pair_ref)
    d_bias = d_bias_ref[:, 0].astype(jnp.float32)
    bias = bias_ref[:, 0, 0].astype(jnp.float32)
    mean = mean_ref[0]
    rstd = rstd_ref[0]
    g_mean = jnp.sum(d_bias * coef_sum_ref[...], axis=0, keepdims=True) * (1.0 / chans)
    gy_mean = jnp.sum(d_bias * bias, axis=0, keepdims=True) * (LN2 / chans)
    slope = rstd * rstd * gy_mean
    shift = mean * slope - rstd * g_mean
    scaled = d_bias * rstd

    @pl.when((pl.program_id(0) == 0) & (pl.program_id(1) == 0))
    def _():
        inner_ref[...] = jnp.zeros_like(inner_ref)
        offset_ref[...] = jnp.zeros_like(offset_ref)

    offset_ref[...] += jnp.sum(scaled * mean, axis=1)
    scaled_high, scaled_low = split_two(scaled.reshape(heads, count))
    ends = jnp.concatenate([shift, slope], axis=0).reshape(2, count)
    ends_high, ends_low = split_two(ends)
    blank = jnp.zeros((12, count), jnp.bfloat16)
    inner_ref[...] += nn_dot(jnp.concatenate([scaled_high, scaled_low], axis=0), cells)
    factors = jnp.concatenate([scaled_high, scaled_low, ends_high, ends_low, blank], axis=0)
    spread = tn_dot(factors, coef_ref[...])
    grad = spread[:, :chans] - cells.astype(jnp.float32) * spread[:, chans:]
    grad = grad.reshape(rows, lanes, chans)
    for quarter in range(quarters):
        grad_ref[0, 0, quarter] = grad[:, quarter * cols : (quarter + 1) * cols]


def pair_backward(half, pair, d_bias, bias, mean, rstd, pair_gain, pair_weight, partial):
    structs, _, quarters, half_rows, cols, chans = pair.shape
    heads = pair_weight.shape[1]
    lanes = quarters * cols
    step = 32
    gained = (pair_weight.astype(jnp.float32) * pair_gain[:, None]).T
    coef_sum = jnp.sum(gained, axis=1)[:, None, None]
    ones = jnp.ones((1, chans), jnp.bfloat16)
    zeros = jnp.zeros((1, chans), jnp.bfloat16)
    rows = gained.astype(jnp.bfloat16)
    left = jnp.concatenate([rows, rows, ones, zeros, ones, zeros], axis=0)
    right = jnp.concatenate(
        [jnp.zeros((2 * heads, chans), jnp.bfloat16), zeros, ones, zeros, ones], axis=0
    )
    coef = jnp.concatenate([left, right], axis=1)
    coef = jnp.concatenate([coef, jnp.zeros((12, 2 * chans), jnp.bfloat16)], axis=0)
    grad, inner, offset = pl.pallas_call(
        pair_backward_kernel,
        grid=(structs, half_rows // step),
        in_specs=[
            pl.BlockSpec((1, 1, quarters, step, cols, chans), lambda c, r: (c, half, 0, r, 0, 0)),
            pl.BlockSpec((heads, 1, step, lanes), lambda c, r: (0, c, r, 0)),
            pl.BlockSpec((heads, 1, 1, step, lanes), lambda c, r: (0, half, c, r, 0)),
            pl.BlockSpec((1, 1, step, lanes), lambda c, r: (half, c, r, 0)),
            pl.BlockSpec((1, 1, step, lanes), lambda c, r: (half, c, r, 0)),
            pl.BlockSpec(coef.shape, lambda c, r: (0, 0)),
            pl.BlockSpec(coef_sum.shape, lambda c, r: (0, 0, 0)),
        ]
        + [pl.BlockSpec(memory_space=pl.ANY)] * len(partial),
        out_specs=[
            pl.BlockSpec((1, 1, quarters, step, cols, chans), lambda c, r: (c, half, 0, r, 0, 0)),
            pl.BlockSpec((2 * heads, chans), lambda c, r: (0, 0)),
            pl.BlockSpec((heads, lanes), lambda c, r: (0, 0)),
        ],
        input_output_aliases={7: 0} if partial else {},
        out_shape=[
            jax.ShapeDtypeStruct(pair.shape, jnp.float32),
            jax.ShapeDtypeStruct((2 * heads, chans), jnp.float32),
            jax.ShapeDtypeStruct((heads, lanes), jnp.float32),
        ],
        compiler_params=pltpu.CompilerParams(vmem_limit_bytes=VMEM_BYTES),
        cost_estimate=spends(13),
        name="pair_backward",
    )(pair, d_bias, bias, mean, rstd, coef, coef_sum, *partial)
    moment = inner[:heads] + inner[heads:] - jnp.sum(offset, axis=1, keepdims=True)
    return grad, moment


def attention_forward_kernel(
    ids_ref, limits_ref, blk_ref,
    query_ref, key_own_ref, key_far_ref, value_own_ref, value_far_ref, bias_ref,
    sent_ref, attn_ref, inverse_ref, weights_ref,
    table_ref,
):
    sources, _, structs, _, lanes = bias_ref.shape
    tile = query_ref.shape[2]
    cols = lanes // 2
    sample = pl.program_id(0)
    near = sources // 2

    @pl.when(sample == 0)
    def _():
        for struct in range(structs):
            limit = limits_ref[struct]
            for source in range(sources):
                part = bias_ref[source, 0, struct].astype(jnp.float32).T
                part = jnp.concatenate([part[:cols], part[cols:]], axis=1)
                position = (
                    lax.rem(source // near + blk_ref[0], 2) * (near * cols) + (source % near) * cols
                )
                position = pl.multiple_of(position, cols)
                keys = source * cols + lax.broadcasted_iota(jnp.int32, part.shape, 0)
                table_ref[struct, pl.ds(position, cols)] = jnp.where(
                    keys < limit, part, -1e30
                ).astype(jnp.bfloat16)

    head_dim = query_ref.shape[1]
    for member in range(query_ref.shape[0]):
        struct = ids_ref[sample * query_ref.shape[0] + member]
        keys_t = jnp.concatenate([key_own_ref[member], key_far_ref[member]], axis=1)
        keys = keys_t.astype(jnp.float32).T.astype(jnp.bfloat16)
        values_t = jnp.concatenate([value_own_ref[member], value_far_ref[member]], axis=1)
        values_t = jnp.concatenate(
            [values_t, jnp.ones((16, values_t.shape[1]), jnp.bfloat16)], axis=0
        )
        query = query_ref[member]
        scores = []
        peak = None
        for start in range(0, keys.shape[0], KEY_CHUNK):
            part = nn_dot(keys[start : start + KEY_CHUNK], query)
            part = part + table_ref[struct, start : start + KEY_CHUNK].astype(jnp.float32)
            part_peak = jnp.max(part.reshape(-1, 8, tile), axis=0)
            peak = part_peak if peak is None else jnp.maximum(peak, part_peak)
            scores.append(part)
        peak = jnp.max(peak, axis=0, keepdims=True)
        summed = 0.0
        for index, part in enumerate(scores):
            span = slice(index * KEY_CHUNK, (index + 1) * KEY_CHUNK)
            weights = jnp.exp2(part - peak).astype(jnp.bfloat16)
            weights_ref[member, span] = weights
            summed = summed + nn_dot(values_t[:, span], weights)
        inverse = 1.0 / summed[head_dim : head_dim + 1]
        attn = summed[:head_dim] * inverse
        attn_ref[member] = attn
        sent_ref[member] = attn.astype(jnp.bfloat16)
        inverse_ref[member] = inverse


def attention_forward(half, ids, limits, blk, qkv, kv_far, bias):
    samples, triple, tokens = qkv.shape
    head_dim = triple // 3
    structs = bias.shape[2]
    tile = tokens // 2
    keys = 2 * tokens
    group = FORWARD_GROUP
    part = (group, head_dim, tokens)
    tile_part = (group, head_dim, tile)
    grid_spec = pltpu.PrefetchScalarGridSpec(
        num_scalar_prefetch=3,
        grid=(samples // group,),
        in_specs=[
            pl.BlockSpec(tile_part, lambda n, *_: (n, 0, half)),
            pl.BlockSpec(part, lambda n, *_: (n, 1, 0)),
            pl.BlockSpec(part, lambda n, *_: (n, 0, 0)),
            pl.BlockSpec(part, lambda n, *_: (n, 2, 0)),
            pl.BlockSpec(part, lambda n, *_: (n, 1, 0)),
            pl.BlockSpec(
                (bias.shape[0], 1) + bias.shape[2:], lambda n, *_: (0, half, 0, 0, 0)
            ),
        ],
        out_specs=[
            pl.BlockSpec(tile_part, lambda n, *_: (n, 0, 0)),
            pl.BlockSpec(tile_part, lambda n, *_: (n, 0, 0)),
            pl.BlockSpec((group, 1, tile), lambda n, *_: (n, 0, 0)),
            pl.BlockSpec((group, keys, tile), lambda n, *_: (n, 0, 0)),
        ],
        scratch_shapes=[pltpu.VMEM((structs, keys, tile), jnp.bfloat16)],
    )
    return pl.pallas_call(
        attention_forward_kernel,
        grid_spec=grid_spec,
        out_shape=[
            jax.ShapeDtypeStruct((samples, head_dim, tile), jnp.bfloat16),
            jax.ShapeDtypeStruct((samples, head_dim, tile), jnp.float32),
            jax.ShapeDtypeStruct((samples, 1, tile), jnp.float32),
            jax.ShapeDtypeStruct((samples, keys, tile), jnp.bfloat16),
        ],
        compiler_params=pltpu.CompilerParams(vmem_limit_bytes=VMEM_BYTES),
        cost_estimate=spends(14),
        name="attention_forward",
    )(ids, limits, blk, qkv, qkv, kv_far, qkv, kv_far, bias)


def attention_backward_kernel(
    ids_ref, blk_ref,
    query_ref, key_own_ref, key_far_ref, value_own_ref, value_far_ref,
    d_attn_ref, attn_ref, inverse_ref, weights_ref, *refs, score_scale,
):
    d_query_ref, d_own_ref, d_far_ref, d_bias_ref, total_ref = refs[-5:]
    sources, structs, _, lanes = d_bias_ref.shape
    cols = lanes // 2
    sample = pl.program_id(0)
    near = sources // 2
    group, head_dim, tile = query_ref.shape
    tokens = key_own_ref.shape[2]

    @pl.when(sample == 0)
    def _():
        total_ref[...] = jnp.zeros_like(total_ref)

    tail = jnp.zeros((14, tile), jnp.bfloat16)
    for index in range(group):
        struct = ids_ref[sample * group + index]
        keys_t = jnp.concatenate([key_own_ref[index], key_far_ref[index]], axis=1)
        values_t = jnp.concatenate([value_own_ref[index], value_far_ref[index]], axis=1)
        values_t = jnp.concatenate(
            [values_t, jnp.ones((16, values_t.shape[1]), jnp.bfloat16)], axis=0
        )
        values = turned(values_t)
        inverse = inverse_ref[index]
        d_attn = d_attn_ref[index].astype(jnp.float32)
        delta = jnp.sum(d_attn * attn_ref[index], axis=0, keepdims=True)
        d_attn = (d_attn * inverse).astype(jnp.bfloat16)
        delta_high, delta_low = split_two(-delta * inverse)
        d_probs = nn_dot(values, jnp.concatenate([d_attn, delta_high, delta_low, tail], axis=0))
        weights = weights_ref[index]
        d_scores = weights.astype(jnp.float32) * d_probs
        total_ref[struct] += d_scores
        d_scores = d_scores.astype(jnp.bfloat16)
        d_values = nn_dot(weights, turned(d_attn)).T
        d_keys = nn_dot(d_scores, turned(query_ref[index])).T * LN2
        d_query_ref[index] = (nn_dot(keys_t, d_scores) * score_scale).astype(jnp.bfloat16)
        for place, value in ((slice(0, head_dim), d_keys), (slice(head_dim, None), d_values)):
            own, far = value[:, :tokens], value[:, tokens:]
            if len(refs) > 5:
                own = own + refs[0][index, place].astype(jnp.float32)
                far = far + refs[1][index, place].astype(jnp.float32)
            d_own_ref[index, place] = own.astype(jnp.bfloat16)
            d_far_ref[index, place] = far.astype(jnp.bfloat16)

    @pl.when(sample == pl.num_programs(0) - 1)
    def _():
        for member in range(structs):
            for source in range(sources):
                position = (
                    lax.rem(source // near + blk_ref[0], 2) * (near * cols) + (source % near) * cols
                )
                position = pl.multiple_of(position, cols)
                part = total_ref[member, pl.ds(position, cols)]
                part = jnp.concatenate([part[:, : tile // 2], part[:, tile // 2 :]], axis=0)
                d_bias_ref[source, member] = part.T.astype(jnp.bfloat16)


def attention_backward(half, ids, blk, qkv, kv_far, d_attn, attn, inverse, weights, bias, partial):
    samples, triple, tokens = qkv.shape
    head_dim = triple // 3
    keys, tile = weights.shape[1:]
    bias_shape = bias.shape[:1] + bias.shape[2:]
    structs = bias.shape[2]
    group = BACKWARD_GROUP
    part = (group, head_dim, tokens)
    tile_part = pl.BlockSpec((group, head_dim, tile), lambda n, *_: (n, 0, 0))
    pair_part = pl.BlockSpec((group, 2 * head_dim, tokens), lambda n, *_: (n, 0, 0))
    grid_spec = pltpu.PrefetchScalarGridSpec(
        num_scalar_prefetch=2,
        grid=(samples // group,),
        in_specs=[
            pl.BlockSpec((group, head_dim, tile), lambda n, *_: (n, 0, half)),
            pl.BlockSpec(part, lambda n, *_: (n, 1, 0)),
            pl.BlockSpec(part, lambda n, *_: (n, 0, 0)),
            pl.BlockSpec(part, lambda n, *_: (n, 2, 0)),
            pl.BlockSpec(part, lambda n, *_: (n, 1, 0)),
            tile_part,
            tile_part,
            pl.BlockSpec((group, 1, tile), lambda n, *_: (n, 0, 0)),
            pl.BlockSpec((group, keys, tile), lambda n, *_: (n, 0, 0)),
        ]
        + [pair_part] * len(partial),
        out_specs=[
            tile_part, pair_part, pair_part, pl.BlockSpec(bias_shape, lambda n, *_: (0, 0, 0, 0))
        ],
        scratch_shapes=[pltpu.VMEM((structs, keys, tile), jnp.float32)],
    )
    pair_shape = jax.ShapeDtypeStruct((samples, 2 * head_dim, tokens), jnp.bfloat16)
    return pl.pallas_call(
        functools.partial(attention_backward_kernel, score_scale=1.0 / math.sqrt(head_dim)),
        grid_spec=grid_spec,
        out_shape=[
            jax.ShapeDtypeStruct((samples, head_dim, tile), jnp.bfloat16),
            pair_shape,
            pair_shape,
            jax.ShapeDtypeStruct(bias_shape, jnp.bfloat16),
        ],
        compiler_params=pltpu.CompilerParams(vmem_limit_bytes=VMEM_BYTES),
        cost_estimate=spends(13),
        name="attention_backward",
    )(ids, blk, qkv, qkv, kv_far, qkv, kv_far, d_attn, attn, inverse, weights, *partial)


def bring(sources, targets, sems):
    copies = [
        pltpu.make_async_copy(source, target, sems.at[index])
        for index, (source, target) in enumerate(zip(sources, targets))
    ]
    for copy in copies:
        copy.start()
    return copies


def turned(value):
    return value.astype(jnp.float32).T.astype(jnp.bfloat16)


def store_tiles(out_refs, core, grad, start):
    groups = out_refs[0].shape[0]
    rows = grad.reshape(groups, 2, -1, grad.shape[1]).astype(jnp.bfloat16)
    span = slice(start, start + rows.shape[2])
    for mine in range(2):

        @pl.when(core == mine)
        def _():
            out_refs[0][:, span] = rows[:, mine]
            out_refs[1][:, span] = rows[:, 1 - mine]


def cond_tiles(out_refs, core, cond_t, d_cond_ref, place, stride):
    tiles = 2 * out_refs[0].shape[0]
    rows = cond_t.shape[0] // tiles
    per_blk = d_cond_ref.shape[1] // (2 * TILE_COLS)
    blank = jnp.zeros((tiles, -(per_blk * rows) % 16, TILE_COLS), jnp.float32)
    for blk in range(2):
        parts = []
        for chunk in range(per_blk):
            start = (blk * per_blk + chunk) * TILE_COLS
            grad = nn_dot(cond_t, d_cond_ref[:, start : start + TILE_COLS])
            parts.append(grad.reshape(tiles, rows, TILE_COLS))
        grad = jnp.concatenate(parts + [blank], axis=1).reshape(-1, TILE_COLS)
        store_tiles(out_refs, core, grad, blk * stride + place)


def early_grads_kernel(place_ref, *refs):
    core = place_ref[0]
    out_refs = refs[-2:]
    pairs = [refs[2 * index : 2 * index + 2] for index in range(7)]
    x_refs, d_up_refs, hidden_refs, d_trans_refs, mixed_refs, d_att_refs, d_cond_refs = pairs
    cond_ref = refs[14]
    place = 0
    tiles = 2 * out_refs[0].shape[0]
    stride = out_refs[0].shape[1] // 2
    for left, right_refs in (
        (turned(rows_of(x_refs)), d_up_refs),
        (turned(rows_of(hidden_refs)), d_trans_refs),
        (jnp.concatenate([mixed_refs[0][...], mixed_refs[1][...]], axis=1), d_att_refs),
    ):
        rows = left.shape[0] // tiles
        per_blk = right_refs[0].shape[1] // (2 * TILE_COLS)
        for chunk in range(2 * per_blk):
            span = slice(chunk * TILE_COLS, (chunk + 1) * TILE_COLS)
            right = jnp.concatenate([right_refs[0][:, span], right_refs[1][:, span]], axis=0)
            start = chunk // per_blk * stride + place + chunk % per_blk * rows
            store_tiles(out_refs, core, nn_dot(left, right), start)
        place += per_blk * rows
    cond_tiles(out_refs, core, turned(cond_ref[...]), rows_of(d_cond_refs), place, stride)


def rows_of(refs):
    return jnp.concatenate([refs[0][...], refs[1][...]], axis=0)


def early_grads(samp, place, operands, cond_in):
    x_trans, d_up, hidden, d_trans, mixed, d_att, d_cond = (pair[0] for pair in operands)
    sizes = [
        x_trans.shape[1] * d_up.shape[1],
        hidden.shape[1] * d_trans.shape[1],
        mixed.shape[0] * d_att.shape[1],
        cond_in.shape[1] * d_cond.shape[1],
    ]
    rows = 16 * math.ceil(sum(sizes) / (samp * 2 * TILE_COLS * 16))
    vmem = pl.BlockSpec(memory_space=pltpu.VMEM)
    shape = jax.ShapeDtypeStruct((samp // 2, 2 * rows, TILE_COLS), jnp.bfloat16)
    return pl.pallas_call(
        early_grads_kernel,
        in_specs=[pl.BlockSpec(memory_space=pltpu.SMEM)] + [vmem] * (2 * len(operands) + 1),
        out_specs=[vmem, vmem],
        out_shape=[shape, shape],
        compiler_params=pltpu.CompilerParams(vmem_limit_bytes=VMEM_BYTES),
        cost_estimate=spends(15),
        name="early_grads",
    )(place, *[value for pair in operands for value in pair], cond_in)


def norm_parts(value):
    center = value - jnp.mean(value, axis=1, keepdims=True)
    rstd = lax.rsqrt(jnp.mean(center * center, axis=1, keepdims=True) + EPS)
    return center * rstd, rstd


def norm_grad(grad, hat, rstd):
    inner = jnp.mean(grad * hat, axis=1, keepdims=True)
    return rstd * (grad - jnp.mean(grad, axis=1, keepdims=True) - hat * inner)


def sigmoid(value):
    return 1.0 / (1.0 + jnp.exp(-value))


def first_kernel(
    place_ref, single_ref, act_ref, cond_weight_ref, cond_bias_ref, gain_ref, weight_far,
    query_bias_ref, qkv_ref, gate_t_ref, x_ref, scale_ref, gate_ref, weight_ref, sems,
    *, score_scale,
):
    copies = bring((weight_far,), (weight_ref,), sems)
    heads = qkv_ref.shape[0]
    head_dim = qkv_ref.shape[1] // 3
    tokens, width = act_ref.shape
    single_hat, _ = norm_parts(single_ref[place_ref[1]].astype(jnp.float32))
    cond_in = (single_hat * gain_ref[0:1]).astype(jnp.bfloat16)
    bias = cond_bias_ref[0:1]
    scale = sigmoid(nn_dot(cond_in, cond_weight_ref[0, :, :width]) + bias[:, :width])
    scale_ref[...] = scale
    shift = nn_dot(cond_in, cond_weight_ref[0, :, width : 2 * width])
    gate_ref[...] = sigmoid(nn_dot(cond_in, cond_weight_ref[0, :, 2 * width :]) + bias[:, width:])
    act_hat, _ = norm_parts(act_ref[...].astype(jnp.float32))
    x_attn = (scale * act_hat + shift).astype(jnp.bfloat16)
    x_ref[...] = x_attn
    copies[0].wait()
    for part in range(4):
        value = nn_dot(x_attn, weight_ref[:, part * width : (part + 1) * width])
        if part == 0:
            value = (value + query_bias_ref[...][None]) * (score_scale * LOG2E)
        value = value.T
        if part == 3:
            gate_t_ref[...] = sigmoid(value)
        else:
            value = value.reshape(heads, head_dim, tokens).astype(jnp.bfloat16)
            qkv_ref[:, part * head_dim : (part + 1) * head_dim] = value


def first_call(heads, place, single_cond, act, cond_weight, cond_bias, gain, weight, query_bias):
    tokens, width = act.shape
    head_dim = width // heads
    vmem = pl.BlockSpec(memory_space=pltpu.VMEM)
    wide = jax.ShapeDtypeStruct((tokens, width), jnp.float32)
    return pl.pallas_call(
        functools.partial(first_kernel, score_scale=1.0 / math.sqrt(head_dim)),
        grid=(1,),
        in_specs=[
            pl.BlockSpec(memory_space=pltpu.SMEM),
            vmem,
            vmem,
            pl.BlockSpec((1,) + cond_weight.shape[1:], lambda _: (0, 0, 0)),
            vmem,
            vmem,
            pl.BlockSpec(memory_space=pl.ANY),
            vmem,
        ],
        out_specs=[vmem] * 5,
        out_shape=[
            jax.ShapeDtypeStruct((heads, 3 * head_dim, tokens), jnp.bfloat16),
            jax.ShapeDtypeStruct((width, tokens), jnp.float32),
            jax.ShapeDtypeStruct((tokens, width), jnp.bfloat16),
            wide,
            wide,
        ],
        scratch_shapes=[
            pltpu.VMEM(weight.shape, weight.dtype), pltpu.SemaphoreType.DMA((1,))
        ],
        compiler_params=pltpu.CompilerParams(vmem_limit_bytes=VMEM_BYTES),
        cost_estimate=spends(12),
        name="first",
    )(place, single_cond, act, cond_weight, cond_bias, gain, weight, query_bias)


def middle_kernel(
    attn_ref, gate_t_ref, act_ref, gate_attn_ref, cond_ref, cotangent_ref,
    out_far_ref, in_far_ref, down_far_ref,
    block_ref, x_ref, d_up_ref, hid_ref, d_trans_ref, mixed_ref, d_att_ref, d_cond_ref,
    d_hidden_ref, d_cond_gate_ref, d_gate_ref, d_attn_ref,
    out_weight_ref, in_weight_ref, down_weight_ref, sems,
):
    copies = bring(
        (out_far_ref, in_far_ref, down_far_ref),
        (out_weight_ref, in_weight_ref, down_weight_ref),
        sems,
    )
    tokens, width = act_ref.shape
    units = hid_ref.shape[1]
    attn = attn_ref[...].reshape(width, tokens).astype(jnp.float32)
    gate = gate_t_ref[...]
    mixed = gate * attn
    mixed_ref[...] = mixed.astype(jnp.bfloat16)
    mixed_rows = mixed.T.astype(jnp.bfloat16)
    copies[0].wait()
    att_out = nn_dot(mixed_rows, out_weight_ref[...])
    gate_attn = gate_attn_ref[...]
    hidden = act_ref[...].astype(jnp.float32) + gate_attn * att_out
    hat, rstd = norm_parts(hidden)
    scale = sigmoid(cond_ref[:, :width])
    x_trans = (scale * hat + cond_ref[:, width : 2 * width]).astype(jnp.bfloat16)
    x_ref[...] = x_trans
    copies[1].wait()
    up_gate = nn_dot(x_trans, in_weight_ref[:, :units])
    up_lin = nn_dot(x_trans, in_weight_ref[:, units:])
    sig = sigmoid(up_gate)
    silu = up_gate * sig
    hid = (silu * up_lin).astype(jnp.bfloat16)
    hid_ref[...] = hid
    gate_trans = sigmoid(cond_ref[:, 2 * width :])
    cotangent = cotangent_ref[...].astype(jnp.float32)
    gated = gate_trans * cotangent
    d_trans = gated.astype(jnp.bfloat16)
    d_trans_ref[...] = d_trans
    copies[2].wait()
    d_hid = nt_dot(d_trans, down_weight_ref[...])
    slope = sig * (1.0 + up_gate * (1.0 - sig))
    d_up_ref[:, :units] = (d_hid * up_lin * slope).astype(jnp.bfloat16)
    d_up_ref[:, units:] = (d_hid * silu).astype(jnp.bfloat16)
    d_xt = nt_dot(d_up_ref[...], in_weight_ref[...])
    scaled = d_xt * scale
    d_hidden = cotangent + norm_grad(scaled, hat, rstd)
    d_hidden_ref[...] = d_hidden
    d_att = (gate_attn * d_hidden).astype(jnp.bfloat16)
    d_att_ref[...] = d_att
    d_mixed = nt_dot(out_weight_ref[...], d_att)
    d_attn_ref[...] = (gate * d_mixed).astype(jnp.bfloat16).reshape(d_attn_ref.shape)
    d_gate_ref[...] = (d_mixed * mixed * (1.0 - gate)).astype(jnp.bfloat16)
    d_cond_gate_ref[...] = (d_hidden * att_out * gate_attn * (1.0 - gate_attn)).astype(jnp.bfloat16)
    trans = nn_dot(hid, down_weight_ref[...])
    block_ref[...] = (hidden + gate_trans * trans).astype(jnp.bfloat16)
    d_cond_ref[:, :width] = (scaled * hat * (1.0 - scale)).astype(jnp.bfloat16)
    d_cond_ref[:, width : 2 * width] = d_xt.astype(jnp.bfloat16)
    d_cond_ref[:, 2 * width :] = (gated * trans * (1.0 - gate_trans)).astype(jnp.bfloat16)


def middle_call(half, attn, gate_t, act, gate_attn, cond, cotangent, *weights):
    tile = attn.shape[2]
    width = act.shape[1]
    units = weights[2].shape[0]
    once = pl.Buffered(1)

    def whole(value):
        zeros = (0,) * value.ndim
        return pl.BlockSpec(value.shape, lambda _: zeros, pipeline_mode=once)

    def rows(value):
        return pl.BlockSpec((tile, value.shape[1]), lambda _: (half, 0), pipeline_mode=once)

    shapes = [
        jax.ShapeDtypeStruct((tile, width), jnp.bfloat16),
        jax.ShapeDtypeStruct((tile, width), jnp.bfloat16),
        jax.ShapeDtypeStruct((tile, 2 * units), jnp.bfloat16),
        jax.ShapeDtypeStruct((tile, units), jnp.bfloat16),
        jax.ShapeDtypeStruct((tile, width), jnp.bfloat16),
        jax.ShapeDtypeStruct((width, tile), jnp.bfloat16),
        jax.ShapeDtypeStruct((tile, width), jnp.bfloat16),
        jax.ShapeDtypeStruct((tile, 3 * width), jnp.bfloat16),
        jax.ShapeDtypeStruct((tile, width), jnp.float32),
        jax.ShapeDtypeStruct((tile, width), jnp.bfloat16),
        jax.ShapeDtypeStruct((width, tile), jnp.bfloat16),
        jax.ShapeDtypeStruct(attn.shape, jnp.bfloat16),
    ]
    return pl.pallas_call(
        middle_kernel,
        grid=(1,),
        in_specs=[
            whole(attn),
            pl.BlockSpec((width, tile), lambda _: (0, half), pipeline_mode=once),
            rows(act), rows(gate_attn), rows(cond), rows(cotangent),
        ]
        + [pl.BlockSpec(memory_space=pl.ANY)] * len(weights),
        out_specs=[whole(shape) for shape in shapes],
        out_shape=shapes,
        scratch_shapes=[pltpu.VMEM(weight.shape, weight.dtype) for weight in weights]
        + [pltpu.SemaphoreType.DMA((len(weights),))],
        compiler_params=pltpu.CompilerParams(vmem_limit_bytes=VMEM_BYTES),
        cost_estimate=spends(10),
        name="middle",
    )(attn, gate_t, act, gate_attn, cond, cotangent, *weights)


def final_kernel(
    place_ref, x_ref, d_query_ref, d_kv_ref, d_gate_one_ref, d_gate_two_ref, cond_sums_ref,
    gain_sums_ref, gain_ref,
    weight_far, act_far, scale_far, d_hidden_one_far, d_hidden_two_far,
    d_cond_gate_one_far, d_cond_gate_two_far, single_far, d_hat_far, cond_weight_far,
    act_grad_ref, keep_one_ref, give_one_ref, keep_two_ref, give_two_ref, sums_ref,
    d_cond_ref,
    weight_ref, act_ref, scale_ref, d_hidden_one_ref, d_hidden_two_ref,
    d_cond_gate_one_ref, d_cond_gate_two_ref, single_ref, d_hat_ref, cond_weight_ref, sems,
):
    copies = bring(
        (weight_far, act_far, scale_far, d_hidden_one_far, d_hidden_two_far,
         d_cond_gate_one_far, d_cond_gate_two_far, single_far, d_hat_far, cond_weight_far.at[0]),
        (weight_ref, act_ref, scale_ref, d_hidden_one_ref, d_hidden_two_ref,
         d_cond_gate_one_ref, d_cond_gate_two_ref, single_ref, d_hat_ref, cond_weight_ref),
        sems,
    )
    core = place_ref[0]
    struct = place_ref[1]
    ones = jnp.ones((8, x_ref.shape[0]), jnp.bfloat16)
    left = turned(x_ref[...])
    width, tokens = left.shape
    groups = keep_one_ref.shape[0]
    rows = width // (2 * groups)
    head_dim = d_query_ref.shape[1] // 2
    one = (keep_one_ref, give_one_ref)
    two = (keep_two_ref, give_two_ref)
    stride_one = keep_one_ref.shape[1] // 2
    share = tokens // (2 * groups)
    stride_two = (keep_two_ref.shape[1] - 2 * share) // 2
    first_slots = stride_one // rows
    sums = []
    rights = []
    for part in range(4):
        if part == 0:
            right = jnp.concatenate(
                [d_query_ref[:, :head_dim], d_query_ref[:, head_dim:]], axis=2
            )
            right = right.reshape(width, tokens)
            sums.append(nt_dot(ones, right)[0:1])
        elif part == 3:
            right = jnp.concatenate([d_gate_one_ref[...], d_gate_two_ref[...]], axis=1)
        else:
            right = d_kv_ref[:, (part - 1) * head_dim : part * head_dim].reshape(width, tokens)
        rights.append(right)
        for chunk in range(2):
            grad = nt_dot(left, right[chunk * TILE_COLS : (chunk + 1) * TILE_COLS])
            slot = 2 * (part % 2) + chunk
            if slot < first_slots:
                store_tiles(one, core, grad, part // 2 * stride_one + slot * rows)
            else:
                start = part // 2 * stride_two + (slot - first_slots) * rows
                store_tiles(two, core, grad, start)
    for copy in copies:
        copy.wait()
    d_xa = 0.0
    for part, right in enumerate(rights):
        d_xa = d_xa + nn_dot(weight_ref[:, part * width : (part + 1) * width], right)
    d_xa = d_xa.T
    act_hat, act_rstd = norm_parts(act_ref[...].astype(jnp.float32))
    scale = scale_ref[...].astype(jnp.float32)
    grad = d_xa * scale
    d_hidden = rows_of((d_hidden_one_ref, d_hidden_two_ref))
    act_grad_ref[...] = d_hidden + norm_grad(grad, act_hat, act_rstd)
    d_cond_ref[:, :width] = (grad * act_hat * (1.0 - scale)).astype(jnp.bfloat16)
    d_cond_ref[:, width : 2 * width] = d_xa.astype(jnp.bfloat16)
    d_cond_ref[:, 2 * width :] = rows_of((d_cond_gate_one_ref, d_cond_gate_two_ref))
    single_hat, single_rstd = norm_parts(single_ref[...].astype(jnp.float32))
    gain = gain_ref[...]
    cond_t = turned((single_hat * gain).astype(jnp.bfloat16))
    cond_tiles(two, core, cond_t, d_cond_ref, (4 - first_slots) * rows, stride_two)
    d_cond = d_cond_ref[...]
    d_in = nt_dot(d_cond, cond_weight_ref[...])
    for cond_sums in (nn_dot(ones, d_cond)[0:1], cond_sums_ref[...]):
        sums.extend([cond_sums[:, :width], cond_sums[:, 2 * width :]])
    sums.extend([jnp.sum(d_in * single_hat, axis=0, keepdims=True), gain_sums_ref[...]])
    sums_ref[...] = jnp.zeros_like(sums_ref)
    row = 0
    for value in sums:
        for start in range(0, value.shape[1], 128):
            sums_ref[row : row + 1] = value[:, start : start + 128]
            row += 1
    single_grad = norm_grad(d_in * gain + d_hat_ref[...], single_hat, single_rstd)
    single_grad = single_grad.reshape(2 * groups, share, single_grad.shape[1])
    chosen = [jnp.where(struct == member, single_grad, 0.0) for member in range(2)]
    chosen = jnp.concatenate(chosen, axis=1).reshape(-1, single_grad.shape[2])
    store_tiles(two, core, chosen, 2 * stride_two)


def final_call(samp, place, x_attn, d_query, d_kv, d_gate, weight, act, scale, d_hidden,
               d_cond_gate, single, d_hat, cond_weight, gain, cond_sums, gain_sums):
    groups = samp // 2
    tokens, width = act.shape
    chans = single.shape[1]
    rows = width // samp
    one_rows = 3 * rows
    cond_rows = cond_weight[0].size // (samp * 2 * TILE_COLS)
    two_rows = rows + 16 * math.ceil(cond_rows / 16)
    vmem = pl.BlockSpec(memory_space=pltpu.VMEM)
    share = tokens // samp
    one = jax.ShapeDtypeStruct((groups, 2 * one_rows, TILE_COLS), jnp.bfloat16)
    two = jax.ShapeDtypeStruct((groups, 2 * (two_rows + share), TILE_COLS), jnp.bfloat16)
    near = (x_attn, d_query, d_kv, *d_gate, cond_sums, gain_sums, gain)
    far = (weight, act, scale, *d_hidden, *d_cond_gate, single, d_hat, cond_weight)
    return pl.pallas_call(
        final_kernel,
        in_specs=[pl.BlockSpec(memory_space=pltpu.SMEM)]
        + [vmem] * len(near)
        + [pl.BlockSpec(memory_space=pl.ANY)] * len(far),
        out_specs=[vmem] * 6,
        out_shape=[
            jax.ShapeDtypeStruct((tokens, width), jnp.float32),
            one, one, two, two,
            jax.ShapeDtypeStruct((8 * math.ceil((5 * width + 2 * chans) / 1024), 128), jnp.float32),
        ],
        scratch_shapes=[pltpu.VMEM((tokens, 3 * width), jnp.bfloat16)]
        + [pltpu.VMEM(value.shape, value.dtype) for value in far[:-1]]
        + [pltpu.VMEM(cond_weight.shape[1:], cond_weight.dtype)]
        + [pltpu.SemaphoreType.DMA((len(far),))],
        compiler_params=pltpu.CompilerParams(vmem_limit_bytes=VMEM_BYTES),
        cost_estimate=spends(20),
        name="final",
    )(place, *near, *far)


def tie(*values):
    return lax.optimization_barrier(values)


def flip(value, axis, distance):
    size = lax.axis_size(axis)
    return lax.ppermute(value, axis, [(i, i ^ distance) for i in range(size)])


def halve(value, axis, distance, dim):
    bit = (lax.axis_index(axis) // distance) % 2
    keep = lax.dynamic_index_in_dim(value, bit, dim, keepdims=False)
    give = lax.dynamic_index_in_dim(value, 1 - bit, dim, keepdims=False)
    return add_low(keep, flip(give, axis, distance))


def spread(value, distance, dim):
    other = flip(value, "samp", distance)
    first = (lax.axis_index("samp") // distance) % 2 == 0
    return jnp.stack([jnp.where(first, value, other), jnp.where(first, other, value)], axis=dim)


def add_low(left, right):
    return (left.astype(jnp.float32) + right.astype(jnp.float32)).astype(jnp.bfloat16)


def grad_from_tiles(tiles, rows):
    blocks = tiles.reshape(-1, rows, TILE_COLS)
    return blocks.transpose(1, 0, 2).reshape(rows, -1)


def exchange(value):
    return lax.all_to_all(value, "samp", 0, 0, tiled=True)


def fast_local(
    activations,
    single_cond,
    pair_repr,
    struct_id,
    seq_lengths,
    qkvg_weight,
    query_bias,
    out_weight,
    in_weight,
    down_weight,
    cond_weight,
    cond_bias,
    single_gain,
    pair_gain,
    pair_weight,
    cotangent,
):
    samp = lax.axis_size("samp")
    blks = lax.axis_size("blk")
    tokens, width = activations.shape[1:]
    heads = pair_weight.shape[1]
    head_dim = width // heads
    hidden_units = down_weight.shape[0]
    structs, _, cols, chans = pair_repr.shape
    blk_arg = lax.axis_index("blk").astype(jnp.int32)[None]
    index = lax.axis_index("samp").astype(jnp.int32)
    place = jnp.stack([index % 2, struct_id[0]])
    act = activations[0]

    qkv, gate_val, x_attn, scale_attn, gate_attn = first_call(
        heads, place, single_cond, act, cond_weight, cond_bias, single_gain,
        qkvg_weight, query_bias,
    )
    own_id = jnp.where(
        lax.broadcasted_iota(jnp.int32, (8, 128), 1) == index, struct_id[0], 0
    ).astype(jnp.float32)
    qkv, pair_in, own_id = tie(qkv, pair_repr, own_id)
    pair = pair_in.reshape(structs, 2, 2, tokens // 4, cols, chans)
    bias_part, pair_mean, pair_rstd = pair_forward(pair, pair_gain, pair_weight)
    own_id, bias_sent = tie(own_id, bias_part)
    for distance in (1, 2, 4):
        own_id = own_id + flip(own_id, "samp", distance)
    qkv, own_id, bias_sent = tie(exchange(qkv), own_id, bias_sent)
    single = jnp.where(struct_id[0] == 1, single_cond[1], single_cond[0])
    single_hat = norm_rows(single.astype(jnp.float32))
    cond_in = (single_hat * single_gain[1]).astype(jnp.bfloat16)
    bias_row = jnp.concatenate(
        [cond_bias[1, :width], jnp.zeros((width,), jnp.float32), cond_bias[1, width:]]
    )
    cond_trans = nn_dot(cond_in, cond_weight[1]) + bias_row
    own_id = own_id + flip(own_id, "samp", 8)
    bias, kv_far, cond_trans, own_id = tie(
        exchange(bias_sent), flip(qkv[:, head_dim:], "blk", 1), cond_trans, own_id
    )
    ids = own_id[0, :samp].astype(jnp.int32)
    forward_args = (ids, seq_lengths, blk_arg, qkv, kv_far)
    sent_one, *saved_one = attention_forward(0, *forward_args, bias)
    sent_one, bias = tie(sent_one, bias)
    sent_two, *saved_two = attention_forward(1, *forward_args, bias)
    attn_one, sent_two = tie(exchange(sent_one), sent_two)
    middle_args = (
        gate_val, act, gate_attn, cond_trans, cotangent[0], out_weight, in_weight, down_weight
    )
    *middle_one, d_attn_one = middle_call(0, attn_one, *middle_args)
    attn_two, d_attn_one = tie(exchange(sent_two), d_attn_one)
    *middle_two, d_attn_two = middle_call(1, attn_two, *middle_args)
    d_attn_one, d_attn_two, *middle_two = tie(exchange(d_attn_one), d_attn_two, *middle_two)
    both = list(zip(middle_one, middle_two))
    block_out = jnp.concatenate(both[0], axis=0)
    d_hidden, d_cond_gate, d_gate_pre = both[8:]

    backward_args = (ids, blk_arg, qkv, kv_far)
    d_query_one, d_own, d_far, d_bias_one = attention_backward(
        0, *backward_args, d_attn_one, *saved_one, bias, ()
    )
    d_attn_two, d_query_one, d_own, d_far, d_bias_one = tie(
        exchange(d_attn_two), d_query_one, d_own, d_far, d_bias_one
    )
    d_bias_one = exchange(d_bias_one)
    d_query_two, d_own, d_far, d_bias_two = attention_backward(
        1, *backward_args, d_attn_two, *saved_two, bias, (d_own, d_far)
    )
    d_query = jnp.concatenate([d_query_one, d_query_two], axis=1)
    d_far, d_bias_two, *operands = tie(
        d_far, d_bias_two, *[value for pair in both[1:8] for value in pair]
    )
    operands = list(zip(operands[::2], operands[1::2]))
    keep_early, give_early = early_grads(samp, place, operands, cond_in)
    d_cond_trans = jnp.concatenate(operands[6], axis=0)
    d_in = nt_dot(d_cond_trans, cond_weight[1])
    gain_sums_trans = jnp.sum(d_in * single_hat, axis=0, keepdims=True)
    cond_sums_trans = jnp.sum(d_cond_trans.astype(jnp.float32), axis=0, keepdims=True)
    d_hat = d_in * single_gain[1]
    d_kv = add_low(d_own, flip(d_far, "blk", 1))
    d_query, d_bias_one = tie(d_query, d_bias_one)
    (
        d_kv, d_query, d_hat, gain_sums_trans, cond_sums_trans, keep_early, give_early,
        d_bias_one, d_bias_two,
    ) = tie(
        d_kv, exchange(d_query), d_hat, gain_sums_trans, cond_sums_trans, keep_early, give_early,
        d_bias_one, d_bias_two,
    )
    cube = (samp // 8, 2, 2)
    early = add_low(keep_early, flip(give_early, "samp", 1))
    pair_grad, moment_one = pair_backward(
        0, pair, d_bias_one, bias_part, pair_mean, pair_rstd, pair_gain, pair_weight, ()
    )
    d_kv, d_bias_two, pair_grad = tie(exchange(d_kv), d_bias_two, pair_grad)
    early = halve(early.reshape(cube + (2, -1, TILE_COLS)), "blk", 1, 3)
    d_bias_two = exchange(d_bias_two)

    act_grad, keep_one, give_one, keep_two, give_two, sums = final_call(
        samp, place, x_attn, d_query, d_kv, d_gate_pre, qkvg_weight, act, scale_attn,
        d_hidden, d_cond_gate, single, d_hat, cond_weight, single_gain[0][None],
        cond_sums_trans, gain_sums_trans,
    )
    d_bias_two, act_grad, keep_one, give_one, keep_two, give_two, early = tie(
        d_bias_two, act_grad, keep_one, give_one, keep_two, give_two, early
    )
    early = halve(early, "samp", 4, 1)
    one = add_low(keep_one, flip(give_one, "samp", 1)).reshape(cube + (2, -1, TILE_COLS))
    two = add_low(keep_two, flip(give_two, "samp", 1)).reshape(cube + (-1, TILE_COLS))
    one, two, d_bias_two = tie(one, two, d_bias_two)
    one = halve(one, "blk", 1, 3)
    two = halve(two, "samp", 2, 2)
    pair_grad, moment_two = pair_backward(
        1, pair, d_bias_two, bias_part, pair_mean, pair_rstd, pair_gain, pair_weight, (pair_grad,)
    )
    one, two, pair_grad, summed = tie(
        one, two, pair_grad, jnp.concatenate([sums, moment_one + moment_two], axis=0)
    )
    shared = 2 * tokens // samp
    alone = two[:, :, -shared:]
    two = two[:, :, :-shared].reshape(two.shape[:2] + (2, -1, TILE_COLS))
    one = halve(one, "samp", 2, 2)
    two = halve(two, "blk", 1, 2)
    alone = add_low(alone, flip(alone, "samp", 4))
    summed = summed + flip(summed, "samp", 4)
    one, two, early, alone, summed = tie(one, two, early, alone, summed)
    early = halve(early, "samp", 2, 1)
    late = halve(jnp.concatenate([one, two], axis=2), "samp", 4, 1)
    alone = add_low(alone, flip(alone, "samp", 8))
    summed = summed + flip(summed, "samp", 8)
    summed = summed + flip(summed, "blk", 1)
    summed = summed + flip(summed, "samp", 1)
    late, early, alone, summed = tie(late, early, alone, summed)
    late = halve(late, "samp", 8, 0).astype(jnp.float32)
    early = halve(early, "samp", 8, 0)
    alone = spread(alone, 2, 2)
    summed = summed + flip(summed, "samp", 2)
    alone = spread(alone, 1, 3)
    single_grad = alone.reshape(samp, structs, tokens // samp, -1).transpose(1, 0, 2, 3)
    single_grad = single_grad.reshape(structs, tokens, -1).astype(jnp.float32)
    early = early.astype(jnp.float32)
    small_grads = []
    start = 0
    for like in (query_bias, cond_bias, single_gain):
        stop = start + like.size // 128
        small_grads.append(summed[start:stop].reshape(like.shape))
        start = stop
    query_bias_grad, cond_bias_grad, single_gain_grad = small_grads
    moment = summed[-heads:].T
    pair_weight_grad = moment * pair_gain[:, None]
    pair_gain_grad = jnp.sum(moment * pair_weight.astype(jnp.float32), axis=1)

    def take(tiles, start, rows, width_out):
        count = rows * width_out // TILE_COLS
        return grad_from_tiles(tiles[start : start + count], rows), start + count

    start = 0
    in_grad, start = take(early, start, width // samp, in_weight.shape[1] // blks)
    down_grad, start = take(early, start, hidden_units // samp, width // blks)
    out_grad, start = take(early, start, width // samp, width // blks)
    cond_rows_dev = cond_weight.shape[1] // samp
    cond_cols_dev = cond_weight.shape[2] // blks
    cond_trans_grad, start = take(early, start, cond_rows_dev, cond_cols_dev)
    qkvg_grad, start = take(late, 0, width // samp, qkvg_weight.shape[1] // blks)
    cond_attn_grad, start = take(late, start, cond_rows_dev, cond_cols_dev)
    return (
        block_out[None],
        act_grad[None],
        single_grad,
        pair_grad.reshape(pair_repr.shape),
        qkvg_grad,
        query_bias_grad,
        out_grad,
        in_grad,
        down_grad,
        jnp.stack([cond_attn_grad, cond_trans_grad]),
        cond_bias_grad,
        single_gain_grad,
        pair_gain_grad,
        pair_weight_grad,
    )


def solution(mesh):
    sizes = dict(mesh.shape)
    program = fast_local if (sizes["samp"], sizes["blk"]) == (16, 2) else local
    return jax.shard_map(
        program,
        mesh=mesh,
        in_specs=(
            P("samp", "blk", None),
            P(None, "blk", None),
            P(None, "blk", "samp", None),
            P("samp"),
            P(),
            P(),
            P(),
            P(),
            P(),
            P(),
            P(),
            P(),
            P(),
            P(),
            P(),
            P("samp", "blk", None),
        ),
        out_specs=(
            P("samp", "blk", None),
            P("samp", "blk", None),
            P(None, "blk", None),
            P(None, "blk", "samp", None),
            P("samp", "blk"),
            P(),
            P("samp", "blk"),
            P("samp", "blk"),
            P("samp", "blk"),
            P(None, "samp", "blk"),
            P(),
            P(),
            P(),
            P(),
        ),
        check_vma=False,
    )
```

```python
import functools
import math

import jax
import jax.numpy as jnp
from jax import lax
from jax.experimental import pallas as pl
from jax.experimental.pallas import tpu as pltpu
from jax.sharding import PartitionSpec as P

EPS = 1e-05
MASKED = -1000000000.0
LOG2E = 1.4426950408889634
LN2 = 0.6931471805599453
VMEM_BYTES = 56 * 1024 * 1024
TILE_COLS = 384


def norm_rows(value):
    center = value - jnp.mean(value, axis=-1, keepdims=True)
    return center * lax.rsqrt(jnp.mean(center * center, axis=-1, keepdims=True) + EPS)


def pick_struct(table, ids):
    expand = (ids.shape[0],) + (1,) * (table.ndim - 1)
    chosen = jnp.broadcast_to(table[0][None], (ids.shape[0],) + table.shape[1:])
    chosen = jnp.where(ids.reshape(expand) == 1, table[1][None], chosen)
    return chosen


def struct_sum(values, ids, structs):
    expand = (ids.shape[0],) + (1,) * (values.ndim - 1)
    return jnp.stack(
        [
            jnp.sum(jnp.where(ids.reshape(expand) == member, values, 0.0), axis=0)
            for member in range(structs)
        ]
    )


def block_length(piece_len):
    return math.gcd(piece_len, 512)


def local(
    activations,
    single_cond,
    pair_repr,
    struct_id,
    seq_lengths,
    qkvg_weight,
    query_bias,
    out_weight,
    in_weight,
    down_weight,
    cond_weight,
    cond_bias,
    single_gain,
    pair_gain,
    pair_weight,
    cotangent,
):
    samples_dev, tok_rows, width = activations.shape
    heads = pair_weight.shape[1]
    head_dim = width // heads
    hidden_units = down_weight.shape[0]
    structs = single_cond.shape[0]
    seq_total = tok_rows * lax.axis_size("blk")
    score_scale = 1.0 / math.sqrt(head_dim)
    zero_index = jnp.zeros((), jnp.int32)
    key_limit = pick_struct(seq_lengths, struct_id)
    single_hat = norm_rows(single_cond.astype(jnp.float32))
    cond_inputs = []
    cond_rows = []
    for sublayer in range(2):
        cond_in = (single_hat * single_gain[sublayer]).astype(jnp.bfloat16)
        bias_row = jnp.concatenate(
            [
                cond_bias[sublayer, :width],
                jnp.zeros((width,), jnp.float32),
                cond_bias[sublayer, width:],
            ]
        )
        cond_pre = (
            jnp.einsum(
                "cti,ij->ctj", cond_in, cond_weight[sublayer], preferred_element_type=jnp.float32
            )
            + bias_row
        )
        cond_inputs.append(cond_in)
        cond_rows.append(pick_struct(cond_pre, struct_id))
    pair_hat, pair_norm_back = jax.vjp(norm_rows, pair_repr.astype(jnp.float32))
    pair_in = (pair_hat * pair_gain).astype(jnp.bfloat16)
    bias_local = jnp.einsum(
        "crkz,zh->crhk", pair_in, pair_weight, preferred_element_type=jnp.float32
    ).astype(jnp.bfloat16)
    bias_all = lax.all_gather(bias_local, "samp", axis=3, tiled=True)
    act_float = activations.astype(jnp.float32)
    act_hat, act_norm_back = jax.vjp(norm_rows, act_float)
    cond_attn = cond_rows[0]
    scale_attn = jax.nn.sigmoid(cond_attn[..., :width])
    gate_attn = jax.nn.sigmoid(cond_attn[..., 2 * width :])
    x_attn = (scale_attn * act_hat + cond_attn[..., width : 2 * width]).astype(jnp.bfloat16)
    proj_bias = jnp.concatenate([query_bias, jnp.zeros((3 * width,), jnp.float32)])
    projected = (
        jnp.einsum("sti,ij->stj", x_attn, qkvg_weight, preferred_element_type=jnp.float32)
        + proj_bias
    )
    query = (
        projected[..., :width].astype(jnp.bfloat16).reshape(samples_dev, tok_rows, heads, head_dim)
    )
    keys_values = projected[..., width : 3 * width].astype(jnp.bfloat16)
    gate_pre = projected[..., 3 * width :]

    def block_scores(sub_kv, offset):
        block_len = sub_kv.shape[1]
        keys_block = sub_kv[..., :width].reshape(samples_dev, block_len, heads, head_dim)
        scores = (
            jnp.einsum("sqhd,skhd->sqhk", query, keys_block, preferred_element_type=jnp.float32)
            * score_scale
        )
        bias_block = lax.dynamic_slice_in_dim(bias_all, offset, block_len, 3)
        scores = scores + pick_struct(bias_block, struct_id).astype(jnp.float32)
        positions = offset + jnp.arange(block_len, dtype=jnp.int32)
        valid = positions[None, :] < key_limit[:, None]
        return jnp.where(valid[:, None, None, :], scores, MASKED)

    def forward_fold(state, block_kv):
        block_len = block_length(block_kv.shape[1])
        count = block_kv.shape[1] // block_len

        def forward_step(carry, index):
            row_peak, row_total, row_acc = carry
            sub_offset = index * block_len
            sub_kv = lax.dynamic_slice_in_dim(block_kv, index * block_len, block_len, 1)
            scores = block_scores(sub_kv, sub_offset)
            values_block = sub_kv[..., width:].reshape(samples_dev, block_len, heads, head_dim)
            new_peak = jnp.maximum(row_peak, jnp.max(scores, axis=-1))
            rescale = jnp.exp(row_peak - new_peak)
            weights = jnp.exp(scores - new_peak[..., None])
            row_total = row_total * rescale + jnp.sum(weights, axis=-1)
            row_acc = row_acc * rescale[..., None] + jnp.einsum(
                "sqhk,skhd->sqhd",
                weights.astype(jnp.bfloat16),
                values_block,
                preferred_element_type=jnp.float32,
            )
            return ((new_peak, row_total, row_acc), None)

        result, ignored = lax.scan(
            jax.checkpoint(forward_step), state, jnp.arange(count, dtype=jnp.int32)
        )
        return result

    stats_shape = (samples_dev, tok_rows, heads)
    forward_init = (
        jnp.full(stats_shape, -1e30, jnp.float32),
        jnp.zeros(stats_shape, jnp.float32),
        jnp.zeros((samples_dev, tok_rows, heads, head_dim), jnp.float32),
    )
    row_peak, row_total, row_acc = forward_fold(
        forward_init, lax.all_gather(keys_values, "blk", axis=1, tiled=True)
    )
    attn4 = row_acc / row_total[..., None]
    log_sum = row_peak + jnp.log(row_total)
    attn = attn4.reshape(samples_dev, tok_rows, width)
    gate_val = jax.nn.sigmoid(gate_pre)
    mixed = (gate_val * attn).astype(jnp.bfloat16)
    att_out = jnp.einsum("sti,ij->stj", mixed, out_weight, preferred_element_type=jnp.float32)
    hidden_state = act_float + gate_attn * att_out
    cond_trans = cond_rows[1]
    scale_trans = jax.nn.sigmoid(cond_trans[..., :width])
    gate_trans = jax.nn.sigmoid(cond_trans[..., 2 * width :])
    hidden_hat, hidden_norm_back = jax.vjp(norm_rows, hidden_state)
    x_trans = (scale_trans * hidden_hat + cond_trans[..., width : 2 * width]).astype(jnp.bfloat16)
    up_proj = jnp.einsum("sti,ij->stj", x_trans, in_weight, preferred_element_type=jnp.float32)
    up_gate = up_proj[..., :hidden_units]
    up_lin = up_proj[..., hidden_units:]
    sig_gate = jax.nn.sigmoid(up_gate)
    silu_gate = up_gate * sig_gate
    hidden_act = (silu_gate * up_lin).astype(jnp.bfloat16)
    trans = jnp.einsum("stf,fd->std", hidden_act, down_weight, preferred_element_type=jnp.float32)
    block_out = (hidden_state + gate_trans * trans).astype(jnp.bfloat16)
    d_out = cotangent.astype(jnp.float32)
    d_trans = (gate_trans * d_out).astype(jnp.bfloat16)
    grad_down = jnp.einsum("stf,std->fd", hidden_act, d_trans, preferred_element_type=jnp.float32)
    d_hid = jnp.einsum("std,fd->stf", d_trans, down_weight, preferred_element_type=jnp.float32)
    silu_slope = sig_gate * (1.0 + up_gate * (1.0 - sig_gate))
    d_up = jnp.concatenate([d_hid * up_lin * silu_slope, d_hid * silu_gate], axis=-1).astype(
        jnp.bfloat16
    )
    grad_in = jnp.einsum("sti,stj->ij", x_trans, d_up, preferred_element_type=jnp.float32)
    d_xt = jnp.einsum("stj,ij->sti", d_up, in_weight, preferred_element_type=jnp.float32)
    d_hidden = d_out + hidden_norm_back(d_xt * scale_trans)[0]
    d_cond_trans = jnp.concatenate(
        [
            d_xt * hidden_hat * scale_trans * (1.0 - scale_trans),
            d_xt,
            d_out * trans * gate_trans * (1.0 - gate_trans),
        ],
        axis=-1,
    )
    d_att = (gate_attn * d_hidden).astype(jnp.bfloat16)
    grad_out = jnp.einsum("sti,stj->ij", mixed, d_att, preferred_element_type=jnp.float32)
    d_mixed = jnp.einsum("stj,ij->sti", d_att, out_weight, preferred_element_type=jnp.float32)
    d_attn = (gate_val * d_mixed).astype(jnp.bfloat16)
    d_gate_pre = d_mixed * attn * gate_val * (1.0 - gate_val)
    d_attn4 = d_attn.reshape(samples_dev, tok_rows, heads, head_dim)
    row_delta = jnp.sum(d_attn4.astype(jnp.float32) * attn4, axis=-1)

    def backward_fold(state, block_kv):
        block_len = block_length(block_kv.shape[1])
        count = block_kv.shape[1] // block_len

        def backward_step(carry, index):
            d_query, d_kv, d_bias = carry
            sub_offset = index * block_len
            sub_kv = lax.dynamic_slice_in_dim(block_kv, index * block_len, block_len, 1)
            keys_block = sub_kv[..., :width].reshape(samples_dev, block_len, heads, head_dim)
            values_block = sub_kv[..., width:].reshape(samples_dev, block_len, heads, head_dim)
            scores = block_scores(sub_kv, sub_offset)
            attn_probs = jnp.exp(scores - log_sum[..., None])
            d_probs = jnp.einsum(
                "sqhd,skhd->sqhk", d_attn4, values_block, preferred_element_type=jnp.float32
            )
            d_scores = (attn_probs * (d_probs - row_delta[..., None])).astype(jnp.bfloat16)
            d_query = (
                d_query
                + jnp.einsum(
                    "sqhk,skhd->sqhd", d_scores, keys_block, preferred_element_type=jnp.float32
                )
                * score_scale
            )
            d_keys = (
                jnp.einsum("sqhk,sqhd->skhd", d_scores, query, preferred_element_type=jnp.float32)
                * score_scale
            )
            d_values = jnp.einsum(
                "sqhk,sqhd->skhd",
                attn_probs.astype(jnp.bfloat16),
                d_attn4,
                preferred_element_type=jnp.float32,
            )
            d_new = jnp.concatenate(
                [
                    d_keys.reshape(samples_dev, block_len, width),
                    d_values.reshape(samples_dev, block_len, width),
                ],
                axis=-1,
            )
            d_kv = lax.dynamic_update_slice(d_kv, d_new, (zero_index, sub_offset, zero_index))
            bias_part = struct_sum(d_scores.astype(jnp.float32), struct_id, structs)
            d_bias = lax.dynamic_update_slice(
                d_bias, bias_part, (zero_index, zero_index, zero_index, sub_offset)
            )
            return ((d_query, d_kv, d_bias), None)

        result, ignored = lax.scan(
            jax.checkpoint(backward_step), state, jnp.arange(count, dtype=jnp.int32)
        )
        return result

    backward_init = (
        jnp.zeros((samples_dev, tok_rows, heads, head_dim), jnp.float32),
        jnp.zeros((samples_dev, seq_total, 2 * width), jnp.float32),
        jnp.zeros((structs, tok_rows, heads, seq_total), jnp.float32),
    )
    d_query, d_kv, d_bias = backward_fold(
        backward_init, lax.all_gather(keys_values, "blk", axis=1, tiled=True)
    )
    d_kv_own = lax.psum_scatter(
        d_kv.astype(jnp.bfloat16), "blk", scatter_dimension=1, tiled=True
    ).astype(jnp.float32)
    d_proj = jnp.concatenate(
        [d_query.reshape(samples_dev, tok_rows, width), d_kv_own, d_gate_pre], axis=-1
    ).astype(jnp.bfloat16)
    grad_qkvg = jnp.einsum("sti,stj->ij", x_attn, d_proj, preferred_element_type=jnp.float32)
    grad_query_bias = jnp.sum(d_proj[..., :width].astype(jnp.float32), axis=(0, 1))
    d_xa = jnp.einsum("stj,ij->sti", d_proj, qkvg_weight, preferred_element_type=jnp.float32)
    act_grad = d_hidden + act_norm_back(d_xa * scale_attn)[0]
    d_cond_attn = jnp.concatenate(
        [
            d_xa * act_hat * scale_attn * (1.0 - scale_attn),
            d_xa,
            d_hidden * att_out * gate_attn * (1.0 - gate_attn),
        ],
        axis=-1,
    )
    d_cond_all = jnp.concatenate(
        [struct_sum(d_cond_attn, struct_id, structs), struct_sum(d_cond_trans, struct_id, structs)],
        axis=-1,
    )
    bias_sum, cond_sum = (
        lax.psum_scatter(
            d_bias.astype(jnp.bfloat16), "samp", scatter_dimension=3, tiled=True
        ).astype(jnp.float32),
        lax.psum_scatter(
            d_cond_all.astype(jnp.bfloat16), "samp", scatter_dimension=1, tiled=True
        ).astype(jnp.float32),
    )
    bias_round = bias_sum.astype(jnp.bfloat16)
    grad_pair_weight = jnp.einsum(
        "crkz,crhk->zh", pair_in, bias_round, preferred_element_type=jnp.float32
    )
    d_pair_in = jnp.einsum(
        "crhk,zh->crkz", bias_round, pair_weight, preferred_element_type=jnp.float32
    )
    grad_pair_gain = jnp.sum(d_pair_in * pair_hat, axis=(0, 1, 2))
    pair_grad = pair_norm_back(d_pair_in * pair_gain)[0]
    slice_len = cond_sum.shape[1]
    slice_start = lax.axis_index("samp") * slice_len
    single_part = lax.dynamic_slice_in_dim(single_cond, slice_start, slice_len, 1).astype(
        jnp.float32
    )
    part_hat, part_norm_back = jax.vjp(norm_rows, single_part)
    cond_round = cond_sum.astype(jnp.bfloat16)
    d_part_hat = jnp.zeros_like(part_hat)
    cond_grads = []
    cond_bias_grads = []
    gain_grads = []
    for sublayer in range(2):
        d_layer = cond_round[..., sublayer * 3 * width : (sublayer + 1) * 3 * width]
        part_in = lax.dynamic_slice_in_dim(cond_inputs[sublayer], slice_start, slice_len, 1)
        cond_grads.append(
            jnp.einsum("cti,ctj->ij", part_in, d_layer, preferred_element_type=jnp.float32)
        )
        layer_sums = jnp.sum(d_layer.astype(jnp.float32), axis=(0, 1))
        cond_bias_grads.append(jnp.concatenate([layer_sums[:width], layer_sums[2 * width :]]))
        d_in = jnp.einsum(
            "ctj,ij->cti", d_layer, cond_weight[sublayer], preferred_element_type=jnp.float32
        )
        gain_grads.append(jnp.sum(d_in * part_hat, axis=(0, 1)))
        d_part_hat = d_part_hat + d_in * single_gain[sublayer]
    single_part_grad = part_norm_back(d_part_hat)[0]
    single_grad = lax.all_gather(single_part_grad, "samp", axis=1, tiled=True)
    grad_cond = jnp.stack(cond_grads)
    part_qkvg, part_out, part_in_w, part_down, part_cond = (
        lax.psum_scatter(
            grad_qkvg.astype(jnp.bfloat16), "blk", scatter_dimension=1, tiled=True
        ).astype(jnp.float32),
        lax.psum_scatter(
            grad_out.astype(jnp.bfloat16), "blk", scatter_dimension=1, tiled=True
        ).astype(jnp.float32),
        lax.psum_scatter(
            grad_in.astype(jnp.bfloat16), "blk", scatter_dimension=1, tiled=True
        ).astype(jnp.float32),
        lax.psum_scatter(
            grad_down.astype(jnp.bfloat16), "blk", scatter_dimension=1, tiled=True
        ).astype(jnp.float32),
        lax.psum_scatter(
            grad_cond.astype(jnp.bfloat16), "blk", scatter_dimension=2, tiled=True
        ).astype(jnp.float32),
    )
    qkvg_grad, out_grad, in_grad, down_grad, cond_grad = (
        lax.psum_scatter(
            part_qkvg.astype(jnp.bfloat16), "samp", scatter_dimension=0, tiled=True
        ).astype(jnp.float32),
        lax.psum_scatter(
            part_out.astype(jnp.bfloat16), "samp", scatter_dimension=0, tiled=True
        ).astype(jnp.float32),
        lax.psum_scatter(
            part_in_w.astype(jnp.bfloat16), "samp", scatter_dimension=0, tiled=True
        ).astype(jnp.float32),
        lax.psum_scatter(
            part_down.astype(jnp.bfloat16), "samp", scatter_dimension=0, tiled=True
        ).astype(jnp.float32),
        lax.psum_scatter(
            part_cond.astype(jnp.bfloat16), "samp", scatter_dimension=1, tiled=True
        ).astype(jnp.float32),
    )
    query_bias_grad, cond_bias_grad, single_gain_grad, pair_gain_grad, pair_weight_grad = lax.psum(
        (
            grad_query_bias,
            jnp.stack(cond_bias_grads),
            jnp.stack(gain_grads),
            grad_pair_gain,
            grad_pair_weight,
        ),
        ("samp", "blk"),
    )
    return (
        block_out,
        act_grad,
        single_grad,
        pair_grad,
        qkvg_grad,
        query_bias_grad,
        out_grad,
        in_grad,
        down_grad,
        cond_grad,
        cond_bias_grad,
        single_gain_grad,
        pair_gain_grad,
        pair_weight_grad,
    )


FORWARD_GROUP = 4
BACKWARD_GROUP = 4
KEY_CHUNK = 128


def nt_dot(left, right):
    return lax.dot_general(
        left, right, (((1,), (1,)), ((), ())), preferred_element_type=jnp.float32
    )


def nn_dot(left, right):
    return lax.dot_general(
        left, right, (((1,), (0,)), ((), ())), preferred_element_type=jnp.float32
    )


def tn_dot(left, right):
    return lax.dot_general(
        left, right, (((0,), (0,)), ((), ())), preferred_element_type=jnp.float32
    )


def split_two(value):
    high = value.astype(jnp.bfloat16)
    return high, (value - high.astype(jnp.float32)).astype(jnp.bfloat16)


def spends(micros):
    return pl.CostEstimate(
        flops=int(micros * 1e9), bytes_accessed=int(micros * 3e6), transcendentals=0
    )


def pair_rows(pair_ref):
    quarters, rows, cols, chans = pair_ref.shape[2:]
    both = jnp.concatenate([pair_ref[0, 0, quarter] for quarter in range(quarters)], axis=1)
    return both.reshape(rows * quarters * cols, chans)


def pair_forward_kernel(pair_ref, coef_ref, coef_sum_ref, bias_ref, mean_ref, rstd_ref):
    heads = bias_ref.shape[0]
    rows, lanes = mean_ref.shape[2:]
    chans = pair_ref.shape[5]
    cells = pair_rows(pair_ref)
    wide = cells.astype(jnp.float32)
    square_high, square_low = split_two(wide * wide)
    sums = nt_dot(coef_ref[...], jnp.concatenate([cells, square_high], axis=1))
    low_sums = nt_dot(jnp.ones((16, chans), jnp.bfloat16), square_low)
    raw = sums[:heads] + sums[heads : 2 * heads]
    total = sums[2 * heads : 2 * heads + 1]
    squares = sums[2 * heads + 8 : 2 * heads + 9] + low_sums[0:1]
    total_high = total.astype(jnp.bfloat16).astype(jnp.float32)
    total_low = total - total_high
    spread = squares * chans - total_high * total_high
    spread = spread - 2.0 * total_high * total_low - total_low * total_low
    rstd = lax.rsqrt(jnp.maximum(spread, 0.0) * (1.0 / (chans * chans)) + EPS)
    mean = total * (1.0 / chans)
    bias = (raw - coef_sum_ref[...] * mean) * (rstd * LOG2E)
    bias_ref[:, 0, 0] = bias.reshape(heads, rows, lanes).astype(jnp.bfloat16)
    mean_ref[0, 0] = mean.reshape(rows, lanes)
    rstd_ref[0, 0] = rstd.reshape(rows, lanes)


def pair_forward(pair, pair_gain, pair_weight):
    structs, halves, quarters, rows, cols, chans = pair.shape
    heads = pair_weight.shape[1]
    lanes = quarters * cols
    step = 32
    gained = pair_weight.astype(jnp.float32) * pair_gain[:, None]
    high, low = split_two(gained.T)
    ones_row = jnp.zeros((8, chans), jnp.bfloat16).at[0].set(1.0)
    blank = jnp.zeros((8, chans), jnp.bfloat16)
    coef = jnp.concatenate(
        [
            jnp.concatenate([high, low, ones_row, blank], axis=0),
            jnp.concatenate([jnp.zeros((2 * heads, chans), jnp.bfloat16), blank, ones_row], axis=0),
        ],
        axis=1,
    )
    coef_sum = jnp.sum(gained, axis=0)[:, None]
    return pl.pallas_call(
        pair_forward_kernel,
        grid=(halves, structs, rows // step),
        in_specs=[
            pl.BlockSpec((1, 1, quarters, step, cols, chans), lambda h, c, r: (c, h, 0, r, 0, 0)),
            pl.BlockSpec(coef.shape, lambda h, c, r: (0, 0)),
            pl.BlockSpec(coef_sum.shape, lambda h, c, r: (0, 0)),
        ],
        out_specs=[
            pl.BlockSpec((heads, 1, 1, step, lanes), lambda h, c, r: (0, h, c, r, 0)),
            pl.BlockSpec((1, 1, step, lanes), lambda h, c, r: (h, c, r, 0)),
            pl.BlockSpec((1, 1, step, lanes), lambda h, c, r: (h, c, r, 0)),
        ],
        out_shape=[
            jax.ShapeDtypeStruct((heads, halves, structs, rows, lanes), jnp.bfloat16),
            jax.ShapeDtypeStruct((halves, structs, rows, lanes), jnp.float32),
            jax.ShapeDtypeStruct((halves, structs, rows, lanes), jnp.float32),
        ],
        compiler_params=pltpu.CompilerParams(vmem_limit_bytes=VMEM_BYTES),
        cost_estimate=spends(20),
        name="pair_forward",
    )(pair, coef, coef_sum)


def pair_backward_kernel(
    pair_ref, d_bias_ref, bias_ref, mean_ref, rstd_ref, coef_ref, coef_sum_ref, *refs
):
    grad_ref, inner_ref, offset_ref = refs[-3:]
    heads = d_bias_ref.shape[0]
    rows, lanes = mean_ref.shape[2:]
    quarters, _, cols, chans = pair_ref.shape[2:]
    count = rows * lanes
    cells = pair_rows(pair_ref)
    d_bias = d_bias_ref[:, 0].astype(jnp.float32)
    bias = bias_ref[:, 0, 0].astype(jnp.float32)
    mean = mean_ref[0]
    rstd = rstd_ref[0]
    g_mean = jnp.sum(d_bias * coef_sum_ref[...], axis=0, keepdims=True) * (1.0 / chans)
    gy_mean = jnp.sum(d_bias * bias, axis=0, keepdims=True) * (LN2 / chans)
    slope = rstd * rstd * gy_mean
    shift = mean * slope - rstd * g_mean
    scaled = d_bias * rstd

    @pl.when((pl.program_id(0) == 0) & (pl.program_id(1) == 0))
    def _():
        inner_ref[...] = jnp.zeros_like(inner_ref)
        offset_ref[...] = jnp.zeros_like(offset_ref)

    offset_ref[...] += jnp.sum(scaled * mean, axis=1)
    scaled_high, scaled_low = split_two(scaled.reshape(heads, count))
    ends = jnp.concatenate([shift, slope], axis=0).reshape(2, count)
    ends_high, ends_low = split_two(ends)
    blank = jnp.zeros((12, count), jnp.bfloat16)
    inner_ref[...] += nn_dot(jnp.concatenate([scaled_high, scaled_low], axis=0), cells)
    factors = jnp.concatenate([scaled_high, scaled_low, ends_high, ends_low, blank], axis=0)
    spread = tn_dot(factors, coef_ref[...])
    grad = spread[:, :chans] - cells.astype(jnp.float32) * spread[:, chans:]
    grad = grad.reshape(rows, lanes, chans)
    for quarter in range(quarters):
        grad_ref[0, 0, quarter] = grad[:, quarter * cols : (quarter + 1) * cols]


def pair_backward(half, pair, d_bias, bias, mean, rstd, pair_gain, pair_weight, partial):
    structs, _, quarters, half_rows, cols, chans = pair.shape
    heads = pair_weight.shape[1]
    lanes = quarters * cols
    step = 32
    gained = (pair_weight.astype(jnp.float32) * pair_gain[:, None]).T
    coef_sum = jnp.sum(gained, axis=1)[:, None, None]
    ones = jnp.ones((1, chans), jnp.bfloat16)
    zeros = jnp.zeros((1, chans), jnp.bfloat16)
    rows = gained.astype(jnp.bfloat16)
    left = jnp.concatenate([rows, rows, ones, zeros, ones, zeros], axis=0)
    right = jnp.concatenate(
        [jnp.zeros((2 * heads, chans), jnp.bfloat16), zeros, ones, zeros, ones], axis=0
    )
    coef = jnp.concatenate([left, right], axis=1)
    coef = jnp.concatenate([coef, jnp.zeros((12, 2 * chans), jnp.bfloat16)], axis=0)
    grad, inner, offset = pl.pallas_call(
        pair_backward_kernel,
        grid=(structs, half_rows // step),
        in_specs=[
            pl.BlockSpec((1, 1, quarters, step, cols, chans), lambda c, r: (c, half, 0, r, 0, 0)),
            pl.BlockSpec((heads, 1, step, lanes), lambda c, r: (0, c, r, 0)),
            pl.BlockSpec((heads, 1, 1, step, lanes), lambda c, r: (0, half, c, r, 0)),
            pl.BlockSpec((1, 1, step, lanes), lambda c, r: (half, c, r, 0)),
            pl.BlockSpec((1, 1, step, lanes), lambda c, r: (half, c, r, 0)),
            pl.BlockSpec(coef.shape, lambda c, r: (0, 0)),
            pl.BlockSpec(coef_sum.shape, lambda c, r: (0, 0, 0)),
        ]
        + [pl.BlockSpec(memory_space=pl.ANY)] * len(partial),
        out_specs=[
            pl.BlockSpec((1, 1, quarters, step, cols, chans), lambda c, r: (c, half, 0, r, 0, 0)),
            pl.BlockSpec((2 * heads, chans), lambda c, r: (0, 0)),
            pl.BlockSpec((heads, lanes), lambda c, r: (0, 0)),
        ],
        input_output_aliases={7: 0} if partial else {},
        out_shape=[
            jax.ShapeDtypeStruct(pair.shape, jnp.float32),
            jax.ShapeDtypeStruct((2 * heads, chans), jnp.float32),
            jax.ShapeDtypeStruct((heads, lanes), jnp.float32),
        ],
        compiler_params=pltpu.CompilerParams(vmem_limit_bytes=VMEM_BYTES),
        cost_estimate=spends(13),
        name="pair_backward",
    )(pair, d_bias, bias, mean, rstd, coef, coef_sum, *partial)
    moment = inner[:heads] + inner[heads:] - jnp.sum(offset, axis=1, keepdims=True)
    return grad, moment


def attention_forward_kernel(
    ids_ref, limits_ref, blk_ref,
    query_ref, key_own_ref, key_far_ref, value_own_ref, value_far_ref, bias_ref,
    sent_ref, attn_ref, inverse_ref, weights_ref,
    table_ref,
):
    sources, _, structs, _, lanes = bias_ref.shape
    tile = query_ref.shape[2]
    cols = lanes // 2
    sample = pl.program_id(0)
    near = sources // 2

    @pl.when(sample == 0)
    def _():
        for struct in range(structs):
            limit = limits_ref[struct]
            for source in range(sources):
                part = bias_ref[source, 0, struct].astype(jnp.float32).T
                part = jnp.concatenate([part[:cols], part[cols:]], axis=1)
                position = (
                    lax.rem(source // near + blk_ref[0], 2) * (near * cols) + (source % near) * cols
                )
                position = pl.multiple_of(position, cols)
                keys = source * cols + lax.broadcasted_iota(jnp.int32, part.shape, 0)
                table_ref[struct, pl.ds(position, cols)] = jnp.where(
                    keys < limit, part, -1e30
                ).astype(jnp.bfloat16)

    head_dim = query_ref.shape[1]
    for member in range(query_ref.shape[0]):
        struct = ids_ref[sample * query_ref.shape[0] + member]
        keys_t = jnp.concatenate([key_own_ref[member], key_far_ref[member]], axis=1)
        keys = keys_t.astype(jnp.float32).T.astype(jnp.bfloat16)
        values_t = jnp.concatenate([value_own_ref[member], value_far_ref[member]], axis=1)
        values_t = jnp.concatenate(
            [values_t, jnp.ones((16, values_t.shape[1]), jnp.bfloat16)], axis=0
        )
        query = query_ref[member]
        scores = []
        peak = None
        for start in range(0, keys.shape[0], KEY_CHUNK):
            part = nn_dot(keys[start : start + KEY_CHUNK], query)
            part = part + table_ref[struct, start : start + KEY_CHUNK].astype(jnp.float32)
            part_peak = jnp.max(part.reshape(-1, 8, tile), axis=0)
            peak = part_peak if peak is None else jnp.maximum(peak, part_peak)
            scores.append(part)
        peak = jnp.max(peak, axis=0, keepdims=True)
        summed = 0.0
        for index, part in enumerate(scores):
            span = slice(index * KEY_CHUNK, (index + 1) * KEY_CHUNK)
            weights = jnp.exp2(part - peak).astype(jnp.bfloat16)
            weights_ref[member, span] = weights
            summed = summed + nn_dot(values_t[:, span], weights)
        inverse = 1.0 / summed[head_dim : head_dim + 1]
        attn = summed[:head_dim] * inverse
        attn_ref[member] = attn
        sent_ref[member] = attn.astype(jnp.bfloat16)
        inverse_ref[member] = inverse


def attention_forward(half, ids, limits, blk, qkv, kv_far, bias):
    samples, triple, tokens = qkv.shape
    head_dim = triple // 3
    structs = bias.shape[2]
    tile = tokens // 2
    keys = 2 * tokens
    group = FORWARD_GROUP
    part = (group, head_dim, tokens)
    tile_part = (group, head_dim, tile)
    grid_spec = pltpu.PrefetchScalarGridSpec(
        num_scalar_prefetch=3,
        grid=(samples // group,),
        in_specs=[
            pl.BlockSpec(tile_part, lambda n, *_: (n, 0, half)),
            pl.BlockSpec(part, lambda n, *_: (n, 1, 0)),
            pl.BlockSpec(part, lambda n, *_: (n, 0, 0)),
            pl.BlockSpec(part, lambda n, *_: (n, 2, 0)),
            pl.BlockSpec(part, lambda n, *_: (n, 1, 0)),
            pl.BlockSpec(
                (bias.shape[0], 1) + bias.shape[2:], lambda n, *_: (0, half, 0, 0, 0)
            ),
        ],
        out_specs=[
            pl.BlockSpec(tile_part, lambda n, *_: (n, 0, 0)),
            pl.BlockSpec(tile_part, lambda n, *_: (n, 0, 0)),
            pl.BlockSpec((group, 1, tile), lambda n, *_: (n, 0, 0)),
            pl.BlockSpec((group, keys, tile), lambda n, *_: (n, 0, 0)),
        ],
        scratch_shapes=[pltpu.VMEM((structs, keys, tile), jnp.bfloat16)],
    )
    return pl.pallas_call(
        attention_forward_kernel,
        grid_spec=grid_spec,
        out_shape=[
            jax.ShapeDtypeStruct((samples, head_dim, tile), jnp.bfloat16),
            jax.ShapeDtypeStruct((samples, head_dim, tile), jnp.float32),
            jax.ShapeDtypeStruct((samples, 1, tile), jnp.float32),
            jax.ShapeDtypeStruct((samples, keys, tile), jnp.bfloat16),
        ],
        compiler_params=pltpu.CompilerParams(vmem_limit_bytes=VMEM_BYTES),
        cost_estimate=spends(14),
        name="attention_forward",
    )(ids, limits, blk, qkv, qkv, kv_far, qkv, kv_far, bias)


def attention_backward_kernel(
    ids_ref, blk_ref,
    query_ref, key_own_ref, key_far_ref, value_own_ref, value_far_ref,
    d_attn_ref, attn_ref, inverse_ref, weights_ref, *refs, score_scale,
):
    d_query_ref, d_own_ref, d_far_ref, d_bias_ref, total_ref = refs[-5:]
    sources, structs, _, lanes = d_bias_ref.shape
    cols = lanes // 2
    sample = pl.program_id(0)
    near = sources // 2
    group, head_dim, tile = query_ref.shape
    tokens = key_own_ref.shape[2]

    @pl.when(sample == 0)
    def _():
        total_ref[...] = jnp.zeros_like(total_ref)

    tail = jnp.zeros((14, tile), jnp.bfloat16)
    for index in range(group):
        struct = ids_ref[sample * group + index]
        keys_t = jnp.concatenate([key_own_ref[index], key_far_ref[index]], axis=1)
        values_t = jnp.concatenate([value_own_ref[index], value_far_ref[index]], axis=1)
        values_t = jnp.concatenate(
            [values_t, jnp.ones((16, values_t.shape[1]), jnp.bfloat16)], axis=0
        )
        values = turned(values_t)
        inverse = inverse_ref[index]
        d_attn = d_attn_ref[index].astype(jnp.float32)
        delta = jnp.sum(d_attn * attn_ref[index], axis=0, keepdims=True)
        d_attn = (d_attn * inverse).astype(jnp.bfloat16)
        delta_high, delta_low = split_two(-delta * inverse)
        d_probs = nn_dot(values, jnp.concatenate([d_attn, delta_high, delta_low, tail], axis=0))
        weights = weights_ref[index]
        d_scores = weights.astype(jnp.float32) * d_probs
        total_ref[struct] += d_scores
        d_scores = d_scores.astype(jnp.bfloat16)
        d_values = nn_dot(weights, turned(d_attn)).T
        d_keys = nn_dot(d_scores, turned(query_ref[index])).T * LN2
        d_query_ref[index] = (nn_dot(keys_t, d_scores) * score_scale).astype(jnp.bfloat16)
        for place, value in ((slice(0, head_dim), d_keys), (slice(head_dim, None), d_values)):
            own, far = value[:, :tokens], value[:, tokens:]
            if len(refs) > 5:
                own = own + refs[0][index, place].astype(jnp.float32)
                far = far + refs[1][index, place].astype(jnp.float32)
            d_own_ref[index, place] = own.astype(jnp.bfloat16)
            d_far_ref[index, place] = far.astype(jnp.bfloat16)

    @pl.when(sample == pl.num_programs(0) - 1)
    def _():
        for member in range(structs):
            for source in range(sources):
                position = (
                    lax.rem(source // near + blk_ref[0], 2) * (near * cols) + (source % near) * cols
                )
                position = pl.multiple_of(position, cols)
                part = total_ref[member, pl.ds(position, cols)]
                part = jnp.concatenate([part[:, : tile // 2], part[:, tile // 2 :]], axis=0)
                d_bias_ref[source, member] = part.T.astype(jnp.bfloat16)


def attention_backward(half, ids, blk, qkv, kv_far, d_attn, attn, inverse, weights, bias, partial):
    samples, triple, tokens = qkv.shape
    head_dim = triple // 3
    keys, tile = weights.shape[1:]
    bias_shape = bias.shape[:1] + bias.shape[2:]
    structs = bias.shape[2]
    group = BACKWARD_GROUP
    part = (group, head_dim, tokens)
    tile_part = pl.BlockSpec((group, head_dim, tile), lambda n, *_: (n, 0, 0))
    pair_part = pl.BlockSpec((group, 2 * head_dim, tokens), lambda n, *_: (n, 0, 0))
    grid_spec = pltpu.PrefetchScalarGridSpec(
        num_scalar_prefetch=2,
        grid=(samples // group,),
        in_specs=[
            pl.BlockSpec((group, head_dim, tile), lambda n, *_: (n, 0, half)),
            pl.BlockSpec(part, lambda n, *_: (n, 1, 0)),
            pl.BlockSpec(part, lambda n, *_: (n, 0, 0)),
            pl.BlockSpec(part, lambda n, *_: (n, 2, 0)),
            pl.BlockSpec(part, lambda n, *_: (n, 1, 0)),
            tile_part,
            tile_part,
            pl.BlockSpec((group, 1, tile), lambda n, *_: (n, 0, 0)),
            pl.BlockSpec((group, keys, tile), lambda n, *_: (n, 0, 0)),
        ]
        + [pair_part] * len(partial),
        out_specs=[
            tile_part, pair_part, pair_part, pl.BlockSpec(bias_shape, lambda n, *_: (0, 0, 0, 0))
        ],
        scratch_shapes=[pltpu.VMEM((structs, keys, tile), jnp.float32)],
    )
    pair_shape = jax.ShapeDtypeStruct((samples, 2 * head_dim, tokens), jnp.bfloat16)
    return pl.pallas_call(
        functools.partial(attention_backward_kernel, score_scale=1.0 / math.sqrt(head_dim)),
        grid_spec=grid_spec,
        out_shape=[
            jax.ShapeDtypeStruct((samples, head_dim, tile), jnp.bfloat16),
            pair_shape,
            pair_shape,
            jax.ShapeDtypeStruct(bias_shape, jnp.bfloat16),
        ],
        compiler_params=pltpu.CompilerParams(vmem_limit_bytes=VMEM_BYTES),
        cost_estimate=spends(13),
        name="attention_backward",
    )(ids, blk, qkv, qkv, kv_far, qkv, kv_far, d_attn, attn, inverse, weights, *partial)


def bring(sources, targets, sems):
    copies = [
        pltpu.make_async_copy(source, target, sems.at[index])
        for index, (source, target) in enumerate(zip(sources, targets))
    ]
    for copy in copies:
        copy.start()
    return copies


def turned(value):
    return value.astype(jnp.float32).T.astype(jnp.bfloat16)


def store_tiles(out_refs, core, grad, start):
    groups = out_refs[0].shape[0]
    rows = grad.reshape(groups, 2, -1, grad.shape[1]).astype(jnp.bfloat16)
    span = slice(start, start + rows.shape[2])
    for mine in range(2):

        @pl.when(core == mine)
        def _():
            out_refs[0][:, span] = rows[:, mine]
            out_refs[1][:, span] = rows[:, 1 - mine]


def cond_tiles(out_refs, core, cond_t, d_cond_ref, place, stride):
    tiles = 2 * out_refs[0].shape[0]
    rows = cond_t.shape[0] // tiles
    per_blk = d_cond_ref.shape[1] // (2 * TILE_COLS)
    blank = jnp.zeros((tiles, -(per_blk * rows) % 16, TILE_COLS), jnp.float32)
    for blk in range(2):
        parts = []
        for chunk in range(per_blk):
            start = (blk * per_blk + chunk) * TILE_COLS
            grad = nn_dot(cond_t, d_cond_ref[:, start : start + TILE_COLS])
            parts.append(grad.reshape(tiles, rows, TILE_COLS))
        grad = jnp.concatenate(parts + [blank], axis=1).reshape(-1, TILE_COLS)
        store_tiles(out_refs, core, grad, blk * stride + place)


def early_grads_kernel(place_ref, *refs):
    core = place_ref[0]
    out_refs = refs[-2:]
    pairs = [refs[2 * index : 2 * index + 2] for index in range(7)]
    x_refs, d_up_refs, hidden_refs, d_trans_refs, mixed_refs, d_att_refs, d_cond_refs = pairs
    cond_ref = refs[14]
    place = 0
    tiles = 2 * out_refs[0].shape[0]
    stride = out_refs[0].shape[1] // 2
    for left, right_refs in (
        (turned(rows_of(x_refs)), d_up_refs),
        (turned(rows_of(hidden_refs)), d_trans_refs),
        (jnp.concatenate([mixed_refs[0][...], mixed_refs[1][...]], axis=1), d_att_refs),
    ):
        rows = left.shape[0] // tiles
        per_blk = right_refs[0].shape[1] // (2 * TILE_COLS)
        for chunk in range(2 * per_blk):
            span = slice(chunk * TILE_COLS, (chunk + 1) * TILE_COLS)
            right = jnp.concatenate([right_refs[0][:, span], right_refs[1][:, span]], axis=0)
            start = chunk // per_blk * stride + place + chunk % per_blk * rows
            store_tiles(out_refs, core, nn_dot(left, right), start)
        place += per_blk * rows
    cond_tiles(out_refs, core, turned(cond_ref[...]), rows_of(d_cond_refs), place, stride)


def rows_of(refs):
    return jnp.concatenate([refs[0][...], refs[1][...]], axis=0)


def early_grads(samp, place, operands, cond_in):
    x_trans, d_up, hidden, d_trans, mixed, d_att, d_cond = (pair[0] for pair in operands)
    sizes = [
        x_trans.shape[1] * d_up.shape[1],
        hidden.shape[1] * d_trans.shape[1],
        mixed.shape[0] * d_att.shape[1],
        cond_in.shape[1] * d_cond.shape[1],
    ]
    rows = 16 * math.ceil(sum(sizes) / (samp * 2 * TILE_COLS * 16))
    vmem = pl.BlockSpec(memory_space=pltpu.VMEM)
    shape = jax.ShapeDtypeStruct((samp // 2, 2 * rows, TILE_COLS), jnp.bfloat16)
    return pl.pallas_call(
        early_grads_kernel,
        in_specs=[pl.BlockSpec(memory_space=pltpu.SMEM)] + [vmem] * (2 * len(operands) + 1),
        out_specs=[vmem, vmem],
        out_shape=[shape, shape],
        compiler_params=pltpu.CompilerParams(vmem_limit_bytes=VMEM_BYTES),
        cost_estimate=spends(15),
        name="early_grads",
    )(place, *[value for pair in operands for value in pair], cond_in)


def norm_parts(value):
    center = value - jnp.mean(value, axis=1, keepdims=True)
    rstd = lax.rsqrt(jnp.mean(center * center, axis=1, keepdims=True) + EPS)
    return center * rstd, rstd


def norm_grad(grad, hat, rstd):
    inner = jnp.mean(grad * hat, axis=1, keepdims=True)
    return rstd * (grad - jnp.mean(grad, axis=1, keepdims=True) - hat * inner)


def sigmoid(value):
    return 1.0 / (1.0 + jnp.exp(-value))


def first_kernel(
    place_ref, single_ref, act_ref, cond_weight_ref, cond_bias_ref, gain_ref, weight_far,
    query_bias_ref, qkv_ref, gate_t_ref, x_ref, scale_ref, gate_ref, weight_ref, sems,
    *, score_scale,
):
    copies = bring((weight_far,), (weight_ref,), sems)
    heads = qkv_ref.shape[0]
    head_dim = qkv_ref.shape[1] // 3
    tokens, width = act_ref.shape
    single_hat, _ = norm_parts(single_ref[place_ref[1]].astype(jnp.float32))
    cond_in = (single_hat * gain_ref[0:1]).astype(jnp.bfloat16)
    bias = cond_bias_ref[0:1]
    scale = sigmoid(nn_dot(cond_in, cond_weight_ref[0, :, :width]) + bias[:, :width])
    scale_ref[...] = scale
    shift = nn_dot(cond_in, cond_weight_ref[0, :, width : 2 * width])
    gate_ref[...] = sigmoid(nn_dot(cond_in, cond_weight_ref[0, :, 2 * width :]) + bias[:, width:])
    act_hat, _ = norm_parts(act_ref[...].astype(jnp.float32))
    x_attn = (scale * act_hat + shift).astype(jnp.bfloat16)
    x_ref[...] = x_attn
    copies[0].wait()
    for part in range(4):
        value = nn_dot(x_attn, weight_ref[:, part * width : (part + 1) * width])
        if part == 0:
            value = (value + query_bias_ref[...][None]) * (score_scale * LOG2E)
        value = value.T
        if part == 3:
            gate_t_ref[...] = sigmoid(value)
        else:
            value = value.reshape(heads, head_dim, tokens).astype(jnp.bfloat16)
            qkv_ref[:, part * head_dim : (part + 1) * head_dim] = value


def first_call(heads, place, single_cond, act, cond_weight, cond_bias, gain, weight, query_bias):
    tokens, width = act.shape
    head_dim = width // heads
    vmem = pl.BlockSpec(memory_space=pltpu.VMEM)
    wide = jax.ShapeDtypeStruct((tokens, width), jnp.float32)
    return pl.pallas_call(
        functools.partial(first_kernel, score_scale=1.0 / math.sqrt(head_dim)),
        grid=(1,),
        in_specs=[
            pl.BlockSpec(memory_space=pltpu.SMEM),
            vmem,
            vmem,
            pl.BlockSpec((1,) + cond_weight.shape[1:], lambda _: (0, 0, 0)),
            vmem,
            vmem,
            pl.BlockSpec(memory_space=pl.ANY),
            vmem,
        ],
        out_specs=[vmem] * 5,
        out_shape=[
            jax.ShapeDtypeStruct((heads, 3 * head_dim, tokens), jnp.bfloat16),
            jax.ShapeDtypeStruct((width, tokens), jnp.float32),
            jax.ShapeDtypeStruct((tokens, width), jnp.bfloat16),
            wide,
            wide,
        ],
        scratch_shapes=[
            pltpu.VMEM(weight.shape, weight.dtype), pltpu.SemaphoreType.DMA((1,))
        ],
        compiler_params=pltpu.CompilerParams(vmem_limit_bytes=VMEM_BYTES),
        cost_estimate=spends(12),
        name="first",
    )(place, single_cond, act, cond_weight, cond_bias, gain, weight, query_bias)


def middle_kernel(
    attn_ref, gate_t_ref, act_ref, gate_attn_ref, cond_ref, cotangent_ref,
    out_far_ref, in_far_ref, down_far_ref,
    block_ref, x_ref, d_up_ref, hid_ref, d_trans_ref, mixed_ref, d_att_ref, d_cond_ref,
    d_hidden_ref, d_cond_gate_ref, d_gate_ref, d_attn_ref,
    out_weight_ref, in_weight_ref, down_weight_ref, sems,
):
    copies = bring(
        (out_far_ref, in_far_ref, down_far_ref),
        (out_weight_ref, in_weight_ref, down_weight_ref),
        sems,
    )
    tokens, width = act_ref.shape
    units = hid_ref.shape[1]
    attn = attn_ref[...].reshape(width, tokens).astype(jnp.float32)
    gate = gate_t_ref[...]
    mixed = gate * attn
    mixed_ref[...] = mixed.astype(jnp.bfloat16)
    mixed_rows = mixed.T.astype(jnp.bfloat16)
    copies[0].wait()
    att_out = nn_dot(mixed_rows, out_weight_ref[...])
    gate_attn = gate_attn_ref[...]
    hidden = act_ref[...].astype(jnp.float32) + gate_attn * att_out
    hat, rstd = norm_parts(hidden)
    scale = sigmoid(cond_ref[:, :width])
    x_trans = (scale * hat + cond_ref[:, width : 2 * width]).astype(jnp.bfloat16)
    x_ref[...] = x_trans
    copies[1].wait()
    up_gate = nn_dot(x_trans, in_weight_ref[:, :units])
    up_lin = nn_dot(x_trans, in_weight_ref[:, units:])
    sig = sigmoid(up_gate)
    silu = up_gate * sig
    hid = (silu * up_lin).astype(jnp.bfloat16)
    hid_ref[...] = hid
    gate_trans = sigmoid(cond_ref[:, 2 * width :])
    cotangent = cotangent_ref[...].astype(jnp.float32)
    gated = gate_trans * cotangent
    d_trans = gated.astype(jnp.bfloat16)
    d_trans_ref[...] = d_trans
    copies[2].wait()
    d_hid = nt_dot(d_trans, down_weight_ref[...])
    slope = sig * (1.0 + up_gate * (1.0 - sig))
    d_up_ref[:, :units] = (d_hid * up_lin * slope).astype(jnp.bfloat16)
    d_up_ref[:, units:] = (d_hid * silu).astype(jnp.bfloat16)
    d_xt = nt_dot(d_up_ref[...], in_weight_ref[...])
    scaled = d_xt * scale
    d_hidden = cotangent + norm_grad(scaled, hat, rstd)
    d_hidden_ref[...] = d_hidden
    d_att = (gate_attn * d_hidden).astype(jnp.bfloat16)
    d_att_ref[...] = d_att
    d_mixed = nt_dot(out_weight_ref[...], d_att)
    d_attn_ref[...] = (gate * d_mixed).astype(jnp.bfloat16).reshape(d_attn_ref.shape)
    d_gate_ref[...] = (d_mixed * mixed * (1.0 - gate)).astype(jnp.bfloat16)
    d_cond_gate_ref[...] = (d_hidden * att_out * gate_attn * (1.0 - gate_attn)).astype(jnp.bfloat16)
    trans = nn_dot(hid, down_weight_ref[...])
    block_ref[...] = (hidden + gate_trans * trans).astype(jnp.bfloat16)
    d_cond_ref[:, :width] = (scaled * hat * (1.0 - scale)).astype(jnp.bfloat16)
    d_cond_ref[:, width : 2 * width] = d_xt.astype(jnp.bfloat16)
    d_cond_ref[:, 2 * width :] = (gated * trans * (1.0 - gate_trans)).astype(jnp.bfloat16)


def middle_call(half, attn, gate_t, act, gate_attn, cond, cotangent, *weights):
    tile = attn.shape[2]
    width = act.shape[1]
    units = weights[2].shape[0]
    once = pl.Buffered(1)

    def whole(value):
        zeros = (0,) * value.ndim
        return pl.BlockSpec(value.shape, lambda _: zeros, pipeline_mode=once)

    def rows(value):
        return pl.BlockSpec((tile, value.shape[1]), lambda _: (half, 0), pipeline_mode=once)

    shapes = [
        jax.ShapeDtypeStruct((tile, width), jnp.bfloat16),
        jax.ShapeDtypeStruct((tile, width), jnp.bfloat16),
        jax.ShapeDtypeStruct((tile, 2 * units), jnp.bfloat16),
        jax.ShapeDtypeStruct((tile, units), jnp.bfloat16),
        jax.ShapeDtypeStruct((tile, width), jnp.bfloat16),
        jax.ShapeDtypeStruct((width, tile), jnp.bfloat16),
        jax.ShapeDtypeStruct((tile, width), jnp.bfloat16),
        jax.ShapeDtypeStruct((tile, 3 * width), jnp.bfloat16),
        jax.ShapeDtypeStruct((tile, width), jnp.float32),
        jax.ShapeDtypeStruct((tile, width), jnp.bfloat16),
        jax.ShapeDtypeStruct((width, tile), jnp.bfloat16),
        jax.ShapeDtypeStruct(attn.shape, jnp.bfloat16),
    ]
    return pl.pallas_call(
        middle_kernel,
        grid=(1,),
        in_specs=[
            whole(attn),
            pl.BlockSpec((width, tile), lambda _: (0, half), pipeline_mode=once),
            rows(act), rows(gate_attn), rows(cond), rows(cotangent),
        ]
        + [pl.BlockSpec(memory_space=pl.ANY)] * len(weights),
        out_specs=[whole(shape) for shape in shapes],
        out_shape=shapes,
        scratch_shapes=[pltpu.VMEM(weight.shape, weight.dtype) for weight in weights]
        + [pltpu.SemaphoreType.DMA((len(weights),))],
        compiler_params=pltpu.CompilerParams(vmem_limit_bytes=VMEM_BYTES),
        cost_estimate=spends(10),
        name="middle",
    )(attn, gate_t, act, gate_attn, cond, cotangent, *weights)


def final_kernel(
    place_ref, x_ref, d_query_ref, d_kv_ref, d_gate_one_ref, d_gate_two_ref, cond_sums_ref,
    gain_sums_ref, gain_ref,
    weight_far, act_far, scale_far, d_hidden_one_far, d_hidden_two_far,
    d_cond_gate_one_far, d_cond_gate_two_far, single_far, d_hat_far, cond_weight_far,
    act_grad_ref, keep_one_ref, give_one_ref, keep_two_ref, give_two_ref, sums_ref,
    d_cond_ref,
    weight_ref, act_ref, scale_ref, d_hidden_one_ref, d_hidden_two_ref,
    d_cond_gate_one_ref, d_cond_gate_two_ref, single_ref, d_hat_ref, cond_weight_ref, sems,
):
    copies = bring(
        (weight_far, act_far, scale_far, d_hidden_one_far, d_hidden_two_far,
         d_cond_gate_one_far, d_cond_gate_two_far, single_far, d_hat_far, cond_weight_far.at[0]),
        (weight_ref, act_ref, scale_ref, d_hidden_one_ref, d_hidden_two_ref,
         d_cond_gate_one_ref, d_cond_gate_two_ref, single_ref, d_hat_ref, cond_weight_ref),
        sems,
    )
    core = place_ref[0]
    struct = place_ref[1]
    ones = jnp.ones((8, x_ref.shape[0]), jnp.bfloat16)
    left = turned(x_ref[...])
    width, tokens = left.shape
    groups = keep_one_ref.shape[0]
    rows = width // (2 * groups)
    head_dim = d_query_ref.shape[1] // 2
    one = (keep_one_ref, give_one_ref)
    two = (keep_two_ref, give_two_ref)
    stride_one = keep_one_ref.shape[1] // 2
    share = tokens // (2 * groups)
    stride_two = (keep_two_ref.shape[1] - 2 * share) // 2
    first_slots = stride_one // rows
    sums = []
    rights = []
    for part in range(4):
        if part == 0:
            right = jnp.concatenate(
                [d_query_ref[:, :head_dim], d_query_ref[:, head_dim:]], axis=2
            )
            right = right.reshape(width, tokens)
            sums.append(nt_dot(ones, right)[0:1])
        elif part == 3:
            right = jnp.concatenate([d_gate_one_ref[...], d_gate_two_ref[...]], axis=1)
        else:
            right = d_kv_ref[:, (part - 1) * head_dim : part * head_dim].reshape(width, tokens)
        rights.append(right)
        for chunk in range(2):
            grad = nt_dot(left, right[chunk * TILE_COLS : (chunk + 1) * TILE_COLS])
            slot = 2 * (part % 2) + chunk
            if slot < first_slots:
                store_tiles(one, core, grad, part // 2 * stride_one + slot * rows)
            else:
                start = part // 2 * stride_two + (slot - first_slots) * rows
                store_tiles(two, core, grad, start)
    for copy in copies:
        copy.wait()
    d_xa = 0.0
    for part, right in enumerate(rights):
        d_xa = d_xa + nn_dot(weight_ref[:, part * width : (part + 1) * width], right)
    d_xa = d_xa.T
    act_hat, act_rstd = norm_parts(act_ref[...].astype(jnp.float32))
    scale = scale_ref[...].astype(jnp.float32)
    grad = d_xa * scale
    d_hidden = rows_of((d_hidden_one_ref, d_hidden_two_ref))
    act_grad_ref[...] = d_hidden + norm_grad(grad, act_hat, act_rstd)
    d_cond_ref[:, :width] = (grad * act_hat * (1.0 - scale)).astype(jnp.bfloat16)
    d_cond_ref[:, width : 2 * width] = d_xa.astype(jnp.bfloat16)
    d_cond_ref[:, 2 * width :] = rows_of((d_cond_gate_one_ref, d_cond_gate_two_ref))
    single_hat, single_rstd = norm_parts(single_ref[...].astype(jnp.float32))
    gain = gain_ref[...]
    cond_t = turned((single_hat * gain).astype(jnp.bfloat16))
    cond_tiles(two, core, cond_t, d_cond_ref, (4 - first_slots) * rows, stride_two)
    d_cond = d_cond_ref[...]
    d_in = nt_dot(d_cond, cond_weight_ref[...])
    for cond_sums in (nn_dot(ones, d_cond)[0:1], cond_sums_ref[...]):
        sums.extend([cond_sums[:, :width], cond_sums[:, 2 * width :]])
    sums.extend([jnp.sum(d_in * single_hat, axis=0, keepdims=True), gain_sums_ref[...]])
    sums_ref[...] = jnp.zeros_like(sums_ref)
    row = 0
    for value in sums:
        for start in range(0, value.shape[1], 128):
            sums_ref[row : row + 1] = value[:, start : start + 128]
            row += 1
    single_grad = norm_grad(d_in * gain + d_hat_ref[...], single_hat, single_rstd)
    single_grad = single_grad.reshape(2 * groups, share, single_grad.shape[1])
    chosen = [jnp.where(struct == member, single_grad, 0.0) for member in range(2)]
    chosen = jnp.concatenate(chosen, axis=1).reshape(-1, single_grad.shape[2])
    store_tiles(two, core, chosen, 2 * stride_two)


def final_call(samp, place, x_attn, d_query, d_kv, d_gate, weight, act, scale, d_hidden,
               d_cond_gate, single, d_hat, cond_weight, gain, cond_sums, gain_sums):
    groups = samp // 2
    tokens, width = act.shape
    chans = single.shape[1]
    rows = width // samp
    one_rows = 3 * rows
    cond_rows = cond_weight[0].size // (samp * 2 * TILE_COLS)
    two_rows = rows + 16 * math.ceil(cond_rows / 16)
    vmem = pl.BlockSpec(memory_space=pltpu.VMEM)
    share = tokens // samp
    one = jax.ShapeDtypeStruct((groups, 2 * one_rows, TILE_COLS), jnp.bfloat16)
    two = jax.ShapeDtypeStruct((groups, 2 * (two_rows + share), TILE_COLS), jnp.bfloat16)
    near = (x_attn, d_query, d_kv, *d_gate, cond_sums, gain_sums, gain)
    far = (weight, act, scale, *d_hidden, *d_cond_gate, single, d_hat, cond_weight)
    return pl.pallas_call(
        final_kernel,
        in_specs=[pl.BlockSpec(memory_space=pltpu.SMEM)]
        + [vmem] * len(near)
        + [pl.BlockSpec(memory_space=pl.ANY)] * len(far),
        out_specs=[vmem] * 6,
        out_shape=[
            jax.ShapeDtypeStruct((tokens, width), jnp.float32),
            one, one, two, two,
            jax.ShapeDtypeStruct((8 * math.ceil((5 * width + 2 * chans) / 1024), 128), jnp.float32),
        ],
        scratch_shapes=[pltpu.VMEM((tokens, 3 * width), jnp.bfloat16)]
        + [pltpu.VMEM(value.shape, value.dtype) for value in far[:-1]]
        + [pltpu.VMEM(cond_weight.shape[1:], cond_weight.dtype)]
        + [pltpu.SemaphoreType.DMA((len(far),))],
        compiler_params=pltpu.CompilerParams(vmem_limit_bytes=VMEM_BYTES),
        cost_estimate=spends(20),
        name="final",
    )(place, *near, *far)


def tie(*values):
    return lax.optimization_barrier(values)


def flip(value, axis, distance):
    size = lax.axis_size(axis)
    return lax.ppermute(value, axis, [(i, i ^ distance) for i in range(size)])


def halve(value, axis, distance, dim):
    bit = (lax.axis_index(axis) // distance) % 2
    keep = lax.dynamic_index_in_dim(value, bit, dim, keepdims=False)
    give = lax.dynamic_index_in_dim(value, 1 - bit, dim, keepdims=False)
    return add_low(keep, flip(give, axis, distance))


def spread(value, distance, dim):
    other = flip(value, "samp", distance)
    first = (lax.axis_index("samp") // distance) % 2 == 0
    return jnp.stack([jnp.where(first, value, other), jnp.where(first, other, value)], axis=dim)


def add_low(left, right):
    return (left.astype(jnp.float32) + right.astype(jnp.float32)).astype(jnp.bfloat16)


def grad_from_tiles(tiles, rows):
    blocks = tiles.reshape(-1, rows, TILE_COLS)
    return blocks.transpose(1, 0, 2).reshape(rows, -1)


def exchange(value):
    return lax.all_to_all(value, "samp", 0, 0, tiled=True)


def fast_local(
    activations,
    single_cond,
    pair_repr,
    struct_id,
    seq_lengths,
    qkvg_weight,
    query_bias,
    out_weight,
    in_weight,
    down_weight,
    cond_weight,
    cond_bias,
    single_gain,
    pair_gain,
    pair_weight,
    cotangent,
):
    samp = lax.axis_size("samp")
    blks = lax.axis_size("blk")
    tokens, width = activations.shape[1:]
    heads = pair_weight.shape[1]
    head_dim = width // heads
    hidden_units = down_weight.shape[0]
    structs, _, cols, chans = pair_repr.shape
    blk_arg = lax.axis_index("blk").astype(jnp.int32)[None]
    index = lax.axis_index("samp").astype(jnp.int32)
    place = jnp.stack([index % 2, struct_id[0]])
    act = activations[0]

    qkv, gate_val, x_attn, scale_attn, gate_attn = first_call(
        heads, place, single_cond, act, cond_weight, cond_bias, single_gain,
        qkvg_weight, query_bias,
    )
    own_id = jnp.where(
        lax.broadcasted_iota(jnp.int32, (8, 128), 1) == index, struct_id[0], 0
    ).astype(jnp.float32)
    qkv, pair_in, own_id = tie(qkv, pair_repr, own_id)
    pair = pair_in.reshape(structs, 2, 2, tokens // 4, cols, chans)
    bias_part, pair_mean, pair_rstd = pair_forward(pair, pair_gain, pair_weight)
    own_id, bias_sent = tie(own_id, bias_part)
    for distance in (1, 2, 4, 8):
        own_id = own_id + flip(own_id, "samp", distance)
    qkv, own_id, bias_sent = tie(exchange(qkv), own_id, bias_sent)
    single = jnp.where(struct_id[0] == 1, single_cond[1], single_cond[0])
    single_hat = norm_rows(single.astype(jnp.float32))
    cond_in = (single_hat * single_gain[1]).astype(jnp.bfloat16)
    bias_row = jnp.concatenate(
        [cond_bias[1, :width], jnp.zeros((width,), jnp.float32), cond_bias[1, width:]]
    )
    cond_trans = nn_dot(cond_in, cond_weight[1]) + bias_row
    bias, kv_far, cond_trans, own_id = tie(
        exchange(bias_sent), flip(qkv[:, head_dim:], "blk", 1), cond_trans, own_id
    )
    ids = own_id[0, :samp].astype(jnp.int32)
    forward_args = (ids, seq_lengths, blk_arg, qkv, kv_far)
    sent_one, *saved_one = attention_forward(0, *forward_args, bias)
    sent_one, bias = tie(sent_one, bias)
    sent_two, *saved_two = attention_forward(1, *forward_args, bias)
    attn_one, sent_two = tie(exchange(sent_one), sent_two)
    middle_args = (
        gate_val, act, gate_attn, cond_trans, cotangent[0], out_weight, in_weight, down_weight
    )
    *middle_one, d_attn_one = middle_call(0, attn_one, *middle_args)
    attn_two, d_attn_one = tie(exchange(sent_two), d_attn_one)
    *middle_two, d_attn_two = middle_call(1, attn_two, *middle_args)
    d_attn_one, d_attn_two, *middle_two = tie(exchange(d_attn_one), d_attn_two, *middle_two)
    both = list(zip(middle_one, middle_two))
    block_out = jnp.concatenate(both[0], axis=0)
    d_hidden, d_cond_gate, d_gate_pre = both[8:]

    backward_args = (ids, blk_arg, qkv, kv_far)
    d_query_one, d_own, d_far, d_bias_one = attention_backward(
        0, *backward_args, d_attn_one, *saved_one, bias, ()
    )
    d_attn_two, d_query_one, d_own, d_far, d_bias_one = tie(
        exchange(d_attn_two), d_query_one, d_own, d_far, d_bias_one
    )
    d_bias_one = exchange(d_bias_one)
    d_query_two, d_own, d_far, d_bias_two = attention_backward(
        1, *backward_args, d_attn_two, *saved_two, bias, (d_own, d_far)
    )
    d_query = jnp.concatenate([d_query_one, d_query_two], axis=1)
    d_far, d_bias_two, *operands = tie(
        d_far, d_bias_two, *[value for pair in both[1:8] for value in pair]
    )
    operands = list(zip(operands[::2], operands[1::2]))
    keep_early, give_early = early_grads(samp, place, operands, cond_in)
    d_cond_trans = jnp.concatenate(operands[6], axis=0)
    d_in = nt_dot(d_cond_trans, cond_weight[1])
    gain_sums_trans = jnp.sum(d_in * single_hat, axis=0, keepdims=True)
    cond_sums_trans = jnp.sum(d_cond_trans.astype(jnp.float32), axis=0, keepdims=True)
    d_hat = d_in * single_gain[1]
    d_kv = add_low(d_own, flip(d_far, "blk", 1))
    d_query, d_bias_one = tie(d_query, d_bias_one)
    (
        d_kv, d_query, d_hat, gain_sums_trans, cond_sums_trans, keep_early, give_early,
        d_bias_one, d_bias_two,
    ) = tie(
        d_kv, exchange(d_query), d_hat, gain_sums_trans, cond_sums_trans, keep_early, give_early,
        d_bias_one, d_bias_two,
    )
    cube = (samp // 8, 2, 2)
    early = add_low(keep_early, flip(give_early, "samp", 1))
    pair_grad, moment_one = pair_backward(
        0, pair, d_bias_one, bias_part, pair_mean, pair_rstd, pair_gain, pair_weight, ()
    )
    d_kv, d_bias_two, pair_grad = tie(exchange(d_kv), d_bias_two, pair_grad)
    early = halve(early.reshape(cube + (2, -1, TILE_COLS)), "blk", 1, 3)
    d_bias_two = exchange(d_bias_two)

    act_grad, keep_one, give_one, keep_two, give_two, sums = final_call(
        samp, place, x_attn, d_query, d_kv, d_gate_pre, qkvg_weight, act, scale_attn,
        d_hidden, d_cond_gate, single, d_hat, cond_weight, single_gain[0][None],
        cond_sums_trans, gain_sums_trans,
    )
    d_bias_two, act_grad, keep_one, give_one, keep_two, give_two, early = tie(
        d_bias_two, act_grad, keep_one, give_one, keep_two, give_two, early
    )
    early = halve(early, "samp", 4, 1)
    one = add_low(keep_one, flip(give_one, "samp", 1)).reshape(cube + (2, -1, TILE_COLS))
    two = add_low(keep_two, flip(give_two, "samp", 1)).reshape(cube + (-1, TILE_COLS))
    one, two, d_bias_two = tie(one, two, d_bias_two)
    one = halve(one, "blk", 1, 3)
    two = halve(two, "samp", 2, 2)
    pair_grad, moment_two = pair_backward(
        1, pair, d_bias_two, bias_part, pair_mean, pair_rstd, pair_gain, pair_weight, (pair_grad,)
    )
    one, two, pair_grad, summed = tie(
        one, two, pair_grad, jnp.concatenate([sums, moment_one + moment_two], axis=0)
    )
    shared = 2 * tokens // samp
    alone = two[:, :, -shared:]
    two = two[:, :, :-shared].reshape(two.shape[:2] + (2, -1, TILE_COLS))
    one = halve(one, "samp", 2, 2)
    two = halve(two, "blk", 1, 2)
    alone = add_low(alone, flip(alone, "samp", 4))
    summed = summed + flip(summed, "samp", 4)
    one, two, early, alone, summed = tie(one, two, early, alone, summed)
    early = halve(early, "samp", 2, 1)
    late = halve(jnp.concatenate([one, two], axis=2), "samp", 4, 1)
    alone = add_low(alone, flip(alone, "samp", 8))
    summed = summed + flip(summed, "samp", 8)
    summed = summed + flip(summed, "blk", 1)
    summed = summed + flip(summed, "samp", 1)
    late, early, alone, summed = tie(late, early, alone, summed)
    late = halve(late, "samp", 8, 0).astype(jnp.float32)
    early = halve(early, "samp", 8, 0)
    alone = spread(alone, 2, 2)
    summed = summed + flip(summed, "samp", 2)
    alone = spread(alone, 1, 3)
    single_grad = alone.reshape(samp, structs, tokens // samp, -1).transpose(1, 0, 2, 3)
    single_grad = single_grad.reshape(structs, tokens, -1).astype(jnp.float32)
    early = early.astype(jnp.float32)
    small_grads = []
    start = 0
    for like in (query_bias, cond_bias, single_gain):
        stop = start + like.size // 128
        small_grads.append(summed[start:stop].reshape(like.shape))
        start = stop
    query_bias_grad, cond_bias_grad, single_gain_grad = small_grads
    moment = summed[-heads:].T
    pair_weight_grad = moment * pair_gain[:, None]
    pair_gain_grad = jnp.sum(moment * pair_weight.astype(jnp.float32), axis=1)

    def take(tiles, start, rows, width_out):
        count = rows * width_out // TILE_COLS
        return grad_from_tiles(tiles[start : start + count], rows), start + count

    start = 0
    in_grad, start = take(early, start, width // samp, in_weight.shape[1] // blks)
    down_grad, start = take(early, start, hidden_units // samp, width // blks)
    out_grad, start = take(early, start, width // samp, width // blks)
    cond_rows_dev = cond_weight.shape[1] // samp
    cond_cols_dev = cond_weight.shape[2] // blks
    cond_trans_grad, start = take(early, start, cond_rows_dev, cond_cols_dev)
    qkvg_grad, start = take(late, 0, width // samp, qkvg_weight.shape[1] // blks)
    cond_attn_grad, start = take(late, start, cond_rows_dev, cond_cols_dev)
    return (
        block_out[None],
        act_grad[None],
        single_grad,
        pair_grad.reshape(pair_repr.shape),
        qkvg_grad,
        query_bias_grad,
        out_grad,
        in_grad,
        down_grad,
        jnp.stack([cond_attn_grad, cond_trans_grad]),
        cond_bias_grad,
        single_gain_grad,
        pair_gain_grad,
        pair_weight_grad,
    )


def solution(mesh):
    sizes = dict(mesh.shape)
    program = fast_local if (sizes["samp"], sizes["blk"]) == (16, 2) else local
    return jax.shard_map(
        program,
        mesh=mesh,
        in_specs=(
            P("samp", "blk", None),
            P(None, "blk", None),
            P(None, "blk", "samp", None),
            P("samp"),
            P(),
            P(),
            P(),
            P(),
            P(),
            P(),
            P(),
            P(),
            P(),
            P(),
            P(),
            P("samp", "blk", None),
        ),
        out_specs=(
            P("samp", "blk", None),
            P("samp", "blk", None),
            P(None, "blk", None),
            P(None, "blk", "samp", None),
            P("samp", "blk"),
            P(),
            P("samp", "blk"),
            P("samp", "blk"),
            P("samp", "blk"),
            P(None, "samp", "blk"),
            P(),
            P(),
            P(),
            P(),
        ),
        check_vma=False,
    )
```
